128 devices in a mesh: wave: 16 (over z, x), level: 8 (over y, core).
Axes of the slice: x: 4, y: 4, z: 4, core: 2. Of those that a mesh axis runs over, the one named last changes fastest.
Arguments:
- spec_in: float32 [640, 2, 16, 2, 1281], P('wave', None, 'level'), may hold values from -0.0034179688 to 0.0034179688
- legendre: float32 [640, 64, 1281], P('wave'), may hold values from -6 to 6
- gauss: float32 [64], replicated, may hold values from 0.3 to 3
- wave_map: int32 [640], replicated, may hold values from 0 to 639, each once
- band_map: int32 [128], replicated, may hold values from 0 to 127, each once
- row_len: int32 [64], replicated, may hold values from 20 to 5136, as said below
Outputs:
- grid_out: float32 [128, 2, 16, 5248], P(('wave', 'level'))
- spec_out: float32 [640, 5, 16, 2, 1281], P('wave', None, 'level')
The draws below stay inside these ranges and needn't reach their ends.
Inputs may be any that keep to these rules, and one draw needn't show every extreme that they name: `wave_map`: each pair index appears once. `band_map`: each row appears once. `row_len`: each length is 20 + 4 j for distinct j of 0 to 1279; the rows of 20 and of 5136 points are always among them.
All inputs are finite; a program needn't handle non-finite values.
Results may differ from the reference program's by a relative error of at most 0.0003.
Values sent between devices are 32-bit elements; how exact they have to be, the bound alone decides.
A program may use at most 192 MiB of HBM per device.

```python
import math
import jax
import jax.numpy as jnp
from jax import lax

WAVES = 1280
PAIRS = 640
PACK = 1281
ROWPAD = 5248
LEVELS = 16
ROWS = 128
LATP = 64


def draw_row_len(key, part):
    key = jax.random.fold_in(key, 7)
    first_key, second_key = jax.random.split(key)
    picks = jax.random.permutation(first_key, WAVES - 2)[:LATP - 2].astype(jnp.int32) + 1
    chosen = jnp.concatenate([picks, jnp.zeros((1,), jnp.int32), jnp.full((1,), WAVES - 1, jnp.int32)])
    chosen = jax.random.permutation(second_key, chosen)
    return (20 + 4 * chosen).astype(jnp.int32)


def shard_levels(stream_key, dims, cuts, least, top_value):
    factor_of, own = 1.0, jax.random.fold_in(stream_key, 6)
    for axis_at, shards_of in cuts:
        steps = jnp.exp(jax.random.uniform(jax.random.fold_in(own, axis_at), (shards_of,), jnp.float32, least / len(cuts), top_value / len(cuts)))
        factor_of = factor_of * jnp.repeat(steps, dims[axis_at] // shards_of).reshape([-1 if axis == axis_at else 1 for axis in range(len(dims))])
    return factor_of


def normal_values(own_key, extent, scale, reach, cuts=(), held_as=jnp.bfloat16):
    array = jax.random.normal(own_key, extent, jnp.float32) * scale
    if len(cuts) > 0:
        array = shard_levels(own_key, extent, cuts, -0.22, 0.18) * array
    return jnp.clip(array, min=-reach, max=reach).astype(held_as)


def setup_inputs(seed: int = 0) -> dict:
    key_of = jax.random.split(jax.random.key(seed), 7)
    return {
        "spec_in": normal_values(key_of[0], (PAIRS, 2, LEVELS, 2, PACK), (0.7071 / WAVES), 0.0034179688, ((0, 16), (2, 8)), jnp.float32),
        "legendre": normal_values(key_of[1], (PAIRS, LATP, PACK), 1.0, 6.0, ((0, 16),), jnp.float32),
        "gauss": jnp.clip(jnp.exp(jax.random.uniform(key_of[2], (LATP,), jnp.float32, math.log(0.3), math.log(3.0))), 0.3, 3.0),
        "wave_map": jax.random.permutation(key_of[3], PAIRS).astype(jnp.int32),
        "band_map": jax.random.permutation(key_of[4], ROWS).astype(jnp.int32),
        "row_len": draw_row_len(jax.random.fold_in(key_of[6], 71), 0),
    }


EXACT_DOT = lax.Precision.HIGHEST
FULL_TURN = 2.0 * math.pi


def pair_masks(pair_ids, wave_count, pack_len):
    position = jnp.arange(pack_len, dtype=jnp.int32)[None, :]
    boundary = (wave_count - pair_ids).astype(jnp.int32)[:, None]
    first_part = (position < boundary).astype(jnp.float32)
    second_part = 1.0 - first_part
    first_sign = (1 - 2 * (position % 2)).astype(jnp.float32)
    second_sign = (1 - 2 * ((position - boundary) % 2)).astype(jnp.float32)
    return jnp.stack([first_part, first_part * first_sign, second_part, second_part * second_sign], axis=1)


def row_angles(wave_ids, lon_ids, length):
    turns = (wave_ids * lon_ids) % length
    return turns.astype(jnp.float32) * (FULL_TURN / length.astype(jnp.float32))


def reference(spec_in, legendre, gauss, wave_map, band_map, row_len):
    masks = pair_masks(wave_map, WAVES, PACK)
    flat_in = spec_in.reshape(PAIRS, 4 * LEVELS, PACK)

    def inverse_pair(operands):
        coeff_rows, table, mask_rows = operands
        varied = coeff_rows[None, :, :] * mask_rows[:, None, :]
        return jnp.einsum("vcq,rq->vcr", varied, table, precision=EXACT_DOT, preferred_element_type=jnp.float32)

    values = lax.map(inverse_pair, (flat_in, legendre, masks))
    values = values.reshape(PAIRS, 2, 2, 4 * LEVELS, LATP).transpose(0, 1, 3, 2, 4)
    values = values.reshape(WAVES, 4 * LEVELS, ROWS)
    wave_of_slot = jnp.stack([wave_map, WAVES - 1 - wave_map], axis=1).reshape(WAVES).astype(jnp.int32)
    natural = jnp.zeros((WAVES, 4 * LEVELS, ROWS), jnp.float32).at[wave_of_slot].set(values)

    def grid_row(band_pos):
        row_id = band_map[band_pos]
        length = row_len[row_id % LATP]
        highest = jnp.minimum(WAVES - 1, (length - 1) // 2)
        column = lax.dynamic_index_in_dim(natural, row_id, 2, keepdims=False)
        parts = column.reshape(WAVES, 2, LEVELS, 2)
        real_rows = jnp.moveaxis(parts[..., 0], 0, -1).reshape(2 * LEVELS, WAVES)
        imag_rows = jnp.moveaxis(parts[..., 1], 0, -1).reshape(2 * LEVELS, WAVES)
        wave_ids = jnp.arange(WAVES, dtype=jnp.int32)
        lon_ids = jnp.arange(ROWPAD, dtype=jnp.int32)
        angle = row_angles(wave_ids[:, None], lon_ids[None, :], length)
        inside = ((lon_ids[None, :] < length) & (wave_ids[:, None] <= highest)).astype(jnp.float32)
        cos_table = jnp.cos(angle) * inside
        sin_table = jnp.sin(angle) * inside
        weight = jnp.where(wave_ids == 0, 1.0, 2.0).astype(jnp.float32)
        slope_weight = weight * wave_ids.astype(jnp.float32) / WAVES
        field = jnp.dot(real_rows * weight, cos_table, precision=EXACT_DOT, preferred_element_type=jnp.float32)
        field = field + jnp.dot(-imag_rows * weight, sin_table, precision=EXACT_DOT, preferred_element_type=jnp.float32)
        slope = jnp.dot(-imag_rows * slope_weight, cos_table, precision=EXACT_DOT, preferred_element_type=jnp.float32)
        slope = slope + jnp.dot(-real_rows * slope_weight, sin_table, precision=EXACT_DOT, preferred_element_type=jnp.float32)
        field = field.reshape(2, LEVELS, ROWPAD)
        slope = slope.reshape(2, LEVELS, ROWPAD)
        fluxes = jnp.concatenate([field[0] * field[0], field[0] * field[1], field[1] * field[1], field[0] * slope[0], field[0] * slope[1]], axis=0)
        cos_sums = jnp.dot(fluxes, cos_table.T, precision=EXACT_DOT, preferred_element_type=jnp.float32)
        sin_sums = jnp.dot(fluxes, sin_table.T, precision=EXACT_DOT, preferred_element_type=jnp.float32)
        scale = length.astype(jnp.float32)
        back = jnp.stack([cos_sums / scale, -sin_sums / scale], axis=1).reshape(5, LEVELS, 2, WAVES)
        return field, back

    grid_out, back = lax.map(grid_row, jnp.arange(ROWS, dtype=jnp.int32))
    row_order = jnp.zeros((ROWS,), jnp.int32).at[band_map].set(jnp.arange(ROWS, dtype=jnp.int32))
    back_natural = jnp.take(back, row_order, axis=0)
    weights = jnp.concatenate([gauss, gauss])
    weighted = back_natural * weights[:, None, None, None, None]

    def direct_pair(operands):
        pair_id, table, mask_rows = operands
        first_wave = lax.dynamic_index_in_dim(weighted, pair_id, 4, keepdims=False)
        second_wave = lax.dynamic_index_in_dim(weighted, WAVES - 1 - pair_id, 4, keepdims=False)
        stacked = jnp.stack([first_wave, second_wave]).reshape(2, 2, LATP, 10 * LEVELS)
        stacked = stacked.transpose(0, 1, 3, 2).reshape(4, 10 * LEVELS, LATP)
        result = jnp.einsum("vcr,rq->vcq", stacked, table, precision=EXACT_DOT, preferred_element_type=jnp.float32)
        return jnp.sum(result * mask_rows[:, None, :], axis=0).reshape(5, LEVELS, 2, PACK)

    spec_out = lax.map(direct_pair, (wave_map, legendre, masks))
    return grid_out, spec_out
```

```python
import functools
import math

import jax
import jax.numpy as jnp
from jax import lax
from jax.experimental import pallas as pl
from jax.experimental.pallas import tpu as pltpu
from jax.sharding import PartitionSpec as P

F32 = jnp.float32
BF16 = jnp.bfloat16
LANES = 128
MIB = 1 << 20
SIN_TERMS = [(-1.0) ** i / math.factorial(2 * i + 1) for i in range(6)]
COS_TERMS = [(-1.0) ** i / math.factorial(2 * i) for i in range(7)]
NT = (((1,), (1,)), ((), ()))
NN = (((1,), (0,)), ((), ()))


def dot(a, b, dims):
    return lax.dot_general(a, b, dims, preferred_element_type=F32)


def split(x):
    high = x.astype(BF16)
    return high, (x - high.astype(F32)).astype(BF16)


def horner(terms, x):
    total = jnp.full_like(x, terms[-1])
    for term in reversed(terms[:-1]):
        total = total * x + term
    return total


def turn_trig(steps, length, inverse):
    left = steps - jnp.floor(steps * inverse + 0.5) * length
    half = left * (inverse * math.pi)
    square = half * half
    sine = half * horner(SIN_TERMS, square)
    cosine = horner(COS_TERMS, square)
    return 1.0 - 2.0 * sine * sine, 2.0 * sine * cosine


def inverse_kernel(group, wave_ref, band_ref, spec_ref, leg_ref, out_ref, flat, sums, rows):
    step = pl.program_id(0)
    slots = sums.shape[0] // 32
    pack = leg_ref.shape[2]
    wave_pos = lax.axis_index("wave")
    position = lax.broadcasted_iota(jnp.int32, (8, pack), 1)
    for g in range(group):
        slot = step * group + g
        first_wave = wave_ref[wave_pos * slots + slot]
        boundary = (pack - 1) - first_wave
        for pair in range(4):
            flat[2 * pair : 2 * pair + 2, :] = spec_ref[g, pair // 2, pair % 2]
        x = flat[...]
        in_first = position < boundary
        parity = jnp.where(in_first, position, position + boundary) & 1
        in_even = in_first == ((first_wave & 1) == 0)
        high = x.astype(BF16).astype(F32)
        parts = []
        for part in (high, x - high):
            signed = jnp.where(parity == 0, part, -part)
            for kept in (in_even, jnp.logical_not(in_even)):
                parts += [jnp.where(kept, part, 0.0), jnp.where(kept, signed, 0.0)]
        left = jnp.concatenate(parts, axis=0).astype(BF16)
        right = jnp.concatenate(split(leg_ref[g]), axis=0)
        both = dot(left, right, NT)
        both = both[:32] + both[32:]
        sums[pl.ds(pl.multiple_of(slot * 32, 32), 32), :] = both + pltpu.roll(both, 64, 1)

    @pl.when(step == pl.num_programs(0) - 1)
    def _():
        north = lax.broadcasted_iota(jnp.int32, (slots, LANES), 1) < 64
        for c in range(8):
            v = [sums[pl.ds(8 * i + c, slots, stride=32), :] for i in range(4)]
            block = jnp.concatenate(
                [
                    jnp.where(north, v[0], v[1]),
                    jnp.where(north, v[2], v[3]),
                    jnp.zeros((LANES - 2 * slots, LANES), F32),
                ],
                axis=0,
            )
            rows[pl.ds(c, LANES, stride=8), :] = block.T

        @pl.loop(0, out_ref.shape[0], unroll=8)
        def _(i):
            out_ref[i] = rows[pl.ds(pl.multiple_of(band_ref[i] * 8, 8), 8), :]


def row_kernel(
    band_ref, len_ref, gauss_ref, row_ref, col_ref, in_ref, grid_ref, out_ref,
    sorted_x, even_x, odd_x, even_l, odd_l, even_hi, even_lo, odd_hi, odd_lo, segs, even_f, odd_f, acc, back, packed,
):
    here = lax.axis_index("wave") * lax.axis_size("level") + lax.axis_index("level")
    row = band_ref[here] & 63
    length = len_ref[row]
    quarter = lax.shift_right_logical(length, 2)
    wave_top = 2 * row_ref.shape[1] - 1
    length_f = jnp.full((1, LANES), length.astype(F32))
    inverse = 1.0 / length_f
    half_waves = row_ref.shape[1]
    blocks = half_waves // LANES
    devices = in_ref.shape[0]
    share = half_waves // devices
    tiles = even_hi.shape[1] // LANES
    lane = lax.broadcasted_iota(jnp.int32, (1, LANES), 1)

    @pl.loop(0, half_waves // 32)
    def _(group):
        block, inner = group // 4, group % 4
        at_cos = pl.multiple_of(block * 256 + inner * 32, 32)
        at_sin = pl.multiple_of(block * 256 + LANES + inner * 32, 32)
        evens = jnp.broadcast_to(col_ref[pl.ds(pl.multiple_of(group * 32, 32), 32), :], (32, LANES))
        for waves, table_hi, table_lo in ((evens, even_hi, even_lo), (wave_top - evens, odd_hi, odd_lo)):
            cosine, sine = turn_trig(waves * lane.astype(F32), length_f, inverse)
            turn_cos, turn_sin = turn_trig(waves * float(LANES), length_f, inverse)
            for tile in range(tiles):
                at = slice(tile * LANES, (tile + 1) * LANES)
                high, low = split(cosine)
                table_hi[pl.ds(at_cos, 32), at] = high
                table_lo[pl.ds(at_cos, 32), at] = low
                high, low = split(sine)
                table_hi[pl.ds(at_sin, 32), at] = high
                table_lo[pl.ds(at_sin, 32), at] = low
                if tile < tiles - 1:
                    cosine, sine = (
                        cosine * turn_cos - sine * turn_sin,
                        sine * turn_cos + cosine * turn_sin,
                    )

    for dev in range(devices):
        for c in range(8):
            f, lv, part = c // 4, c // 2 % 2, c % 2
            piece = in_ref[dev, pl.ds(c, 8, stride=8), :]
            sorted_x[dev % 4, pl.ds(32 * part + 16 * f + lv, 8, stride=2), :] = piece
        at = slice(dev * share, (dev + 1) * share)
        even_x[:, at] = sorted_x[dev % 4, :, :share]
        odd_x[:, at] = sorted_x[dev % 4, :, share : 2 * share]

    highest = jnp.minimum(wave_top, lax.shift_right_logical(length - 1, 1))
    for block in range(blocks):
        at = slice(block * LANES, (block + 1) * LANES)
        evens = row_ref[:, at]
        for odd, x_ref, l_ref in ((False, even_x, even_l), (True, odd_x, odd_l)):
            wave = wave_top - evens if odd else evens
            kept = (wave <= highest).astype(F32)
            weight = jnp.where(wave == 0, 1.0, 2.0) * kept
            slope_weight = weight * wave.astype(F32) / (wave_top + 1.0)
            real, imag = x_ref[0:32, at], x_ref[32:64, at]
            a = jnp.concatenate([real * weight, -imag * slope_weight], axis=0)
            b = jnp.concatenate([imag * weight, real * slope_weight], axis=0)
            flip = (1 - (wave & 2)).astype(F32)
            if odd:
                on_cos = jnp.concatenate([a, flip * b], axis=0)
                on_sin = jnp.concatenate([-b, flip * a], axis=0)
            else:
                on_cos = jnp.concatenate([a, flip * a], axis=0)
                on_sin = jnp.concatenate([-b, -flip * b], axis=0)
            for offset, value in ((0, on_cos), (LANES, on_sin)):
                to = slice(block * 256 + offset, block * 256 + offset + LANES)
                high, low = split(value)
                l_ref[0:128, to] = high
                l_ref[128:256, to] = low

    start = 0
    while start < tiles * LANES:
        width = min(256, tiles * LANES - start)
        at = slice(start, start + width)
        start += width
        halves = []
        for l_ref, table_hi, table_lo in ((even_l, even_hi, even_lo), (odd_l, odd_hi, odd_lo)):
            whole = dot(l_ref[...], table_hi[:, at], NN)
            halves.append(whole[:128] + whole[128:] + dot(l_ref[0:128, :], table_lo[:, at], NN))
        inside = (at.start + lax.broadcasted_iota(jnp.int32, (1, width), 1)) < quarter
        even, odd = (jnp.where(inside, half, 0.0) for half in halves)
        quarters = [even[:64] + odd[:64], even[64:] - odd[64:], even[:64] - odd[:64], even[64:] + odd[64:]]
        fluxes = []
        for i, values in enumerate(quarters):
            segs[i, :, at] = values[:32]
            u, v, su, sv = (values[16 * n : 16 * n + 16] for n in range(4))
            fluxes.append(jnp.concatenate([u * u, u * v, v * v, u * su, u * sv], axis=0))
        for f_ref, sign in ((even_f, 1.0), (odd_f, -1.0)):
            for n in range(2):
                value = fluxes[n] + fluxes[n + 2] if sign > 0 else fluxes[n] - fluxes[n + 2]
                high, low = split(value)
                f_ref[80 * n : 80 * n + 80, at] = high
                f_ref[160 + 80 * n : 240 + 80 * n, at] = low

    acc[...] = jnp.zeros_like(acc)
    for i in range(4):
        begin = i * quarter
        shift = begin & (LANES - 1)
        base = lax.shift_right_logical(begin, 7)
        before = jnp.zeros((32, LANES), F32)
        for tile in range(tiles + 1):
            if tile < tiles:
                rolled = pltpu.roll(segs[i, :, tile * LANES : (tile + 1) * LANES], shift, 1)
            else:
                rolled = jnp.zeros((32, LANES), F32)
            at = pl.ds(pl.multiple_of((base + tile) * LANES, LANES), LANES)
            acc[:, at] += jnp.where(lane < shift, before, rolled)
            before = rolled
    pad_len = grid_ref.shape[3]
    for f in range(2):
        grid_ref[0, f] = acc[16 * f : 16 * f + 16, :pad_len]

    scale = gauss_ref[row] * inverse
    for block in range(blocks):
        at = slice(block * LANES, (block + 1) * LANES)
        rows = slice(block * 256, (block + 1) * 256)
        evens = row_ref[:, at]
        for odd, f_ref, table_hi, table_lo in ((0, even_f, even_hi, even_lo), (1, odd_f, odd_hi, odd_lo)):
            whole = dot(f_ref[...], table_hi[rows, :], NT)
            total = whole[:160] + whole[160:] + dot(f_ref[0:160, :], table_lo[rows, :], NT)
            wave = wave_top - evens if odd else evens
            kept = jnp.where(wave <= highest, scale, 0.0)
            flip = (1 - (wave & 2)).astype(F32)
            first_cos, first_sin = total[:80, :LANES], total[:80, LANES:]
            second_cos, second_sin = total[80:, :LANES] * flip, total[80:, LANES:] * flip
            if odd:
                back[2, :, at] = (first_cos - second_sin) * kept
                back[3, :, at] = -(first_sin + second_cos) * kept
            else:
                back[0, :, at] = (first_cos + second_cos) * kept
                back[1, :, at] = -(first_sin + second_sin) * kept

    for dev in range(devices):
        at = slice(dev * share, (dev + 1) * share)
        for part in range(2):
            even, odd = back[part, :, at], back[2 + part, :, at]
            packed[part, :, 0:share] = even[:64]
            packed[part, :, share : 2 * share] = odd[:64]
            packed[part, 0:16, 2 * share : 3 * share] = even[64:]
            packed[part, 16:32, 2 * share : 3 * share] = odd[64:]
            for n in range(8):
                out_ref[dev, pl.ds(2 * n + part, 8, stride=16), :] = packed[
                    part, pl.ds(n // 2 * 16 + n % 2, 8, stride=2), :
                ]


def direct_kernel(group, wave_ref, band_ref, in_ref, leg_ref, out_ref, natural, turned):
    step = pl.program_id(0)
    pack = leg_ref.shape[2]
    slots = pl.num_programs(0) * group
    wave_pos = lax.axis_index("wave")

    @pl.when(step == 0)
    def _():
        @pl.loop(0, in_ref.shape[0], unroll=8)
        def _(i):
            natural[pl.ds(pl.multiple_of(band_ref[i] * 16, 16), 16), :] = in_ref[i]

        for n in range(16):
            turned[pl.ds(n, LANES, stride=16), :] = natural[pl.ds(n, LANES, stride=16), :].T

    position = lax.broadcasted_iota(jnp.int32, (1, pack), 1)
    south = lax.broadcasted_iota(jnp.int32, (1, LANES), 1) >= 64
    for g in range(group):
        slot = step * group + g
        first_wave = wave_ref[wave_pos * slots + slot]
        boundary = (pack - 1) - first_wave

        def of_lane(extra, count):
            return turned[pl.ds(pl.multiple_of((slot + extra) * 16, 16), count), :]

        x = jnp.concatenate([of_lane(0, 16), of_lane(slots, 16), of_lane(2 * slots, 8)], axis=0)
        other = pltpu.roll(x, 64, 1)
        difference = x - other
        y = jnp.concatenate([x + other, jnp.where(south, -difference, difference)], axis=0)
        left = jnp.concatenate(split(y), axis=0)
        right = jnp.concatenate(split(leg_ref[g]), axis=0)
        both = dot(left, right, NN)
        both = both[:80] + both[80:]
        in_first = position < boundary
        parity = jnp.where(in_first, position, position + boundary) & 1
        in_even = in_first == ((first_wave & 1) == 0)
        chosen = jnp.where(parity == 0, both[:40], both[40:])
        main = jnp.where(in_even, chosen[:16], chosen[16:32])
        last = jnp.where(in_even, chosen[32:36], chosen[36:40])
        for n in range(8):
            out_ref[g, n // 2, n % 2] = main[2 * n : 2 * n + 2]
        for n in range(2):
            out_ref[g, 4, n] = last[2 * n : 2 * n + 2]


def shards(spec_in, legendre, gauss, wave_map, band_map, row_len):
    axes = ("wave", "level")
    wave_devices = lax.axis_size("wave")
    devices = wave_devices * lax.axis_size("level")
    slots, _, _, _, pack = spec_in.shape
    waves = pack - 1
    lat_pairs = legendre.shape[1]
    pad_len = (20 + 4 * (waves - 1) + 127) // 128 * 128
    table_len = (pad_len // 4 + 127) // 128 * 128
    smem = pl.BlockSpec(memory_space=pltpu.SMEM)
    vmem = pl.BlockSpec(memory_space=pltpu.VMEM)
    group = 4

    outgoing = pl.pallas_call(
        functools.partial(inverse_kernel, group),
        out_shape=jax.ShapeDtypeStruct((devices, 8, LANES), F32),
        grid=(slots // group,),
        in_specs=[
            smem,
            smem,
            pl.BlockSpec((group, 2, 2, 2, pack), lambda s: (s, 0, 0, 0, 0)),
            pl.BlockSpec((group, lat_pairs, pack), lambda s: (s, 0, 0)),
        ],
        out_specs=pl.BlockSpec((devices, 8, LANES), lambda s: (0, 0, 0)),
        scratch_shapes=[
            pltpu.VMEM((8, pack), F32),
            pltpu.VMEM((slots * 32, LANES), F32),
            pltpu.VMEM((LANES * 8, LANES), F32),
        ],
        compiler_params=pltpu.CompilerParams(vmem_limit_bytes=32 * MIB),
        name="inverse",
    )(wave_map, band_map, spec_in, legendre)

    arrived = lax.all_to_all(outgoing, axes, split_axis=0, concat_axis=0, tiled=True)
    arrived = arrived.reshape(wave_devices, 64, LANES)
    evens = jnp.where(wave_map % 2 == 0, wave_map, waves - 1 - wave_map)
    grid_out, returning = pl.pallas_call(
        row_kernel,
        out_shape=(
            jax.ShapeDtypeStruct((1, 2, 16, pad_len), F32),
            jax.ShapeDtypeStruct((wave_devices, 128, LANES), F32),
        ),
        in_specs=[smem, smem, smem, vmem, vmem, vmem],
        out_specs=(vmem, vmem),
        scratch_shapes=[
            pltpu.VMEM((4, 64, LANES), F32),
            pltpu.VMEM((64, waves // 2), F32),
            pltpu.VMEM((64, waves // 2), F32),
            pltpu.VMEM((256, waves), BF16),
            pltpu.VMEM((256, waves), BF16),
            pltpu.VMEM((waves, table_len), BF16),
            pltpu.VMEM((waves, table_len), BF16),
            pltpu.VMEM((waves, table_len), BF16),
            pltpu.VMEM((waves, table_len), BF16),
            pltpu.VMEM((4, 32, table_len), F32),
            pltpu.VMEM((320, table_len), BF16),
            pltpu.VMEM((320, table_len), BF16),
            pltpu.VMEM((32, 4 * table_len), F32),
            pltpu.VMEM((4, 80, waves // 2), F32),
            pltpu.VMEM((2, 64, LANES), F32),
        ],
        compiler_params=pltpu.CompilerParams(vmem_limit_bytes=48 * MIB),
        name="rows",
    )(band_map, row_len, gauss, evens[None, :], evens[:, None].astype(F32), arrived)

    returning = returning.reshape(devices, 16, LANES)
    returned = lax.all_to_all(returning, axes, split_axis=0, concat_axis=0, tiled=True)
    spec_out = pl.pallas_call(
        functools.partial(direct_kernel, group),
        out_shape=jax.ShapeDtypeStruct((slots, 5, 2, 2, pack), F32),
        grid=(slots // group,),
        in_specs=[
            smem,
            smem,
            pl.BlockSpec((devices, 16, LANES), lambda s: (0, 0, 0)),
            pl.BlockSpec((group, lat_pairs, pack), lambda s: (s, 0, 0)),
        ],
        out_specs=pl.BlockSpec((group, 5, 2, 2, pack), lambda s: (s, 0, 0, 0, 0)),
        scratch_shapes=[
            pltpu.VMEM((LANES * 16, LANES), F32),
            pltpu.VMEM((LANES * 16, LANES), F32),
        ],
        compiler_params=pltpu.CompilerParams(vmem_limit_bytes=32 * MIB),
        name="direct",
    )(wave_map, band_map, returned, legendre)
    return (grid_out, spec_out)


def solution(mesh):
    in_specs = (P("wave", None, "level", None, None), P("wave", None, None), P(), P(), P(), P())
    out_specs = (P(("wave", "level"), None, None, None), P("wave", None, "level", None, None))
    return jax.shard_map(shards, mesh=mesh, in_specs=in_specs, out_specs=out_specs, check_vma=False)
```

```python
import functools
import math

import jax
import jax.numpy as jnp
from jax import lax
from jax.experimental import pallas as pl
from jax.experimental.pallas import tpu as pltpu
from jax.sharding import PartitionSpec as P

F32 = jnp.float32
BF16 = jnp.bfloat16
LANES = 128
MIB = 1 << 20
SIN_TERMS = [(-1.0) ** i / math.factorial(2 * i + 1) for i in range(6)]
COS_TERMS = [(-1.0) ** i / math.factorial(2 * i) for i in range(7)]
MESH = pl.DeviceIdType.MESH
NT = (((1,), (1,)), ((), ()))
NN = (((1,), (0,)), ((), ()))


def dot(a, b, dims):
    return lax.dot_general(a, b, dims, preferred_element_type=F32)


def split(x):
    high = x.astype(BF16)
    return high, (x - high.astype(F32)).astype(BF16)


def horner(terms, x):
    total = jnp.full_like(x, terms[-1])
    for term in reversed(terms[:-1]):
        total = total * x + term
    return total


def turn_trig(steps, length, inverse):
    left = steps - jnp.floor(steps * inverse + 0.5) * length
    half = left * (inverse * math.pi)
    square = half * half
    sine = half * horner(SIN_TERMS, square)
    cosine = horner(COS_TERMS, square)
    return 1.0 - 2.0 * sine * sine, 2.0 * sine * cosine


def peer(k):
    wave, level = lax.axis_index("wave"), lax.axis_index("level")
    core, y, x, z = k % 2, k // 2 % 4, k // 8 % 4, k // 32
    return (wave // 4 + z) % 4 * 4 + (wave % 4 + x) % 4, (level // 2 + y) % 4 * 2 + (level % 2 + core) % 2


def send(source, target, sems, device):
    return pltpu.make_async_remote_copy(
        src_ref=source, dst_ref=target, send_sem=sems.at[0], recv_sem=sems.at[1], device_id=device, device_id_type=MESH
    )


def inverse_step(group, wave_ref, spec_ref, leg_ref, flat, sums):
    step = pl.program_id(0)
    slots = sums.shape[0] // 32
    pack = leg_ref.shape[2]
    wave_pos = lax.axis_index("wave")
    position = lax.broadcasted_iota(jnp.int32, (8, pack), 1)
    for g in range(group):
        slot = step * group + g
        first_wave = wave_ref[wave_pos * slots + slot]
        boundary = (pack - 1) - first_wave
        for pair in range(4):
            flat[2 * pair : 2 * pair + 2, :] = spec_ref[g, pair // 2, pair % 2]
        x = flat[...]
        in_first = position < boundary
        parity = jnp.where(in_first, position, position + boundary) & 1
        in_even = in_first == ((first_wave & 1) == 0)
        high = x.astype(BF16).astype(F32)
        parts = []
        for part in (high, x - high):
            signed = jnp.where(parity == 0, part, -part)
            for kept in (in_even, jnp.logical_not(in_even)):
                parts += [jnp.where(kept, part, 0.0), jnp.where(kept, signed, 0.0)]
        left = jnp.concatenate(parts, axis=0).astype(BF16)
        right = jnp.concatenate(split(leg_ref[g]), axis=0)
        both = dot(left, right, NT)
        both = both[:32] + both[32:]
        sums[pl.ds(pl.multiple_of(slot * 32, 32), 32), :] = both + pltpu.roll(both, 64, 1)


def sort_rows(band_ref, sums, flat_rows, rows, out_ref):
    slots = sums.shape[0] // 32
    north = lax.broadcasted_iota(jnp.int32, (slots, LANES), 1) < 64
    for c in range(8):
        v = [sums[pl.ds(8 * i + c, slots, stride=32), :] for i in range(4)]
        block = jnp.concatenate(
            [
                jnp.where(north, v[0], v[1]),
                jnp.where(north, v[2], v[3]),
                jnp.zeros((LANES - 2 * slots, LANES), F32),
            ],
            axis=0,
        )
        flat_rows[pl.ds(c, LANES, stride=8), :] = block.T

    @pl.loop(0, LANES, unroll=8)
    def _(i):
        rows[i] = flat_rows[pl.ds(pl.multiple_of(i * 8, 8), 8), :]

    @pl.loop(0, out_ref.shape[0], unroll=8)
    def _(i):
        out_ref[i] = rows[band_ref[i]]


def main_kernel(
    group, wave_ref, band_ref, len_ref, gauss_ref, map_ref, spec_ref, leg_ref, segs_ref, out_ref,
    flat, sums, flat_rows, rows, row_ref, col_ref, send_ref, in_ref, sorted_x, even_x, odd_x, even_l, odd_l,
    even_hi, even_lo, odd_hi, odd_lo, segs, even_f, odd_f, back, packed, back_ref, sems, back_sems, local_sems,
):
    step = pl.program_id(0)
    steps = pl.num_programs(0)
    devices = send_ref.shape[0]
    barrier = pltpu.get_barrier_semaphore()

    for n in range(13):
        k = step * 13 + n + 1

        @pl.when(k < devices)
        def _():
            pl.semaphore_signal(barrier, inc=1, device_id=peer(k), device_id_type=MESH)

    inverse_step(group, wave_ref, spec_ref, leg_ref, flat, sums)

    @pl.when(step == steps - 1)
    def _():
        sort_rows(band_ref, sums, flat_rows, rows, send_ref)
        pl.semaphore_wait(barrier, devices - 1)
        row_part(
            band_ref, len_ref, gauss_ref, map_ref, row_ref, col_ref, segs_ref, out_ref, send_ref, in_ref, sorted_x,
            even_x, odd_x, even_l, odd_l, even_hi, even_lo, odd_hi, odd_lo, segs, even_f, odd_f, back, packed,
            back_ref, sems, back_sems, local_sems,
        )


def row_part(
    band_ref, len_ref, gauss_ref, map_ref, row_ref, col_ref, segs_ref, out_ref, send_ref, in_ref, sorted_x,
    even_x, odd_x, even_l, odd_l, even_hi, even_lo, odd_hi, odd_lo, segs, even_f, odd_f, back, packed,
    back_ref, sems, back_sems, local_sems,
):
    my_wave, my_level = lax.axis_index("wave"), lax.axis_index("level")
    levels = lax.axis_size("level")
    here = my_wave * levels + my_level
    row = band_ref[here] & 63
    length = len_ref[row]
    quarter = lax.shift_right_logical(length, 2)
    wave_top = 2 * row_ref.shape[1] - 1
    length_f = jnp.full((1, LANES), length.astype(F32))
    inverse = 1.0 / length_f
    half_waves = row_ref.shape[1]
    blocks = half_waves // LANES
    devices = in_ref.shape[0]
    everyone = devices * levels
    share = half_waves // devices
    tiles = even_hi.shape[1] // LANES
    lane = lax.broadcasted_iota(jnp.int32, (1, LANES), 1)

    mapped = map_ref[...]
    row_ref[...] = jnp.where((mapped & 1) == 0, mapped, wave_top - mapped)
    for block in range(blocks):
        at = slice(block * LANES, (block + 1) * LANES)
        col_ref[at, :] = jnp.broadcast_to(row_ref[:, at].astype(F32), (LANES, LANES)).T

    def start_send(k):
        to_wave, to_level = peer(k)
        mine = in_ref.at[my_wave, pl.ds(pl.multiple_of(my_level * 8, 8), 8), :]
        send(send_ref.at[to_wave * levels + to_level], mine, sems, (to_wave, to_level)).start()

    def make_tables(group):
        block, inner = group // 4, group % 4
        at_cos = pl.multiple_of(block * 256 + inner * 32, 32)
        at_sin = pl.multiple_of(block * 256 + LANES + inner * 32, 32)
        evens = col_ref[pl.ds(pl.multiple_of(group * 32, 32), 32), :]
        for waves, table_hi, table_lo in ((evens, even_hi, even_lo), (wave_top - evens, odd_hi, odd_lo)):
            cosine, sine = turn_trig(waves * lane.astype(F32), length_f, inverse)
            turn_cos, turn_sin = turn_trig(waves * float(LANES), length_f, inverse)
            for tile in range(tiles):
                at = slice(tile * LANES, (tile + 1) * LANES)
                high, low = split(cosine)
                table_hi[pl.ds(at_cos, 32), at] = high
                table_lo[pl.ds(at_cos, 32), at] = low
                high, low = split(sine)
                table_hi[pl.ds(at_sin, 32), at] = high
                table_lo[pl.ds(at_sin, 32), at] = low
                if tile < tiles - 1:
                    cosine, sine = (
                        cosine * turn_cos - sine * turn_sin,
                        sine * turn_cos + cosine * turn_sin,
                    )

    in_ref[my_wave, pl.ds(pl.multiple_of(my_level * 8, 8), 8), :] = send_ref[here]
    start_send(1)

    @pl.loop(0, 18)
    def _(group):
        for n in range(7):
            start_send(group * 7 + n + 2)
        make_tables(group)

    @pl.loop(18, half_waves // 32)
    def _(group):
        make_tables(group)

    landed = send_ref.at[pl.ds(0, everyone - 1)]
    arrival = send(landed, landed, sems, (my_wave, my_level))
    arrival.wait_recv()

    for dev in range(devices):
        for c in range(8):
            f, lv, part = c // 4, c // 2 % 2, c % 2
            piece = in_ref[dev, pl.ds(c, 8, stride=8), :]
            sorted_x[dev % 4, pl.ds(32 * part + 16 * f + lv, 8, stride=2), :] = piece
        at = slice(dev * share, (dev + 1) * share)
        even_x[:, at] = sorted_x[dev % 4, :, :share]
        odd_x[:, at] = sorted_x[dev % 4, :, share : 2 * share]

    highest = jnp.minimum(wave_top, lax.shift_right_logical(length - 1, 1))
    for block in range(blocks):
        at = slice(block * LANES, (block + 1) * LANES)
        evens = row_ref[:, at]
        for odd, x_ref, l_ref in ((False, even_x, even_l), (True, odd_x, odd_l)):
            wave = wave_top - evens if odd else evens
            kept = (wave <= highest).astype(F32)
            weight = jnp.where(wave == 0, 1.0, 2.0) * kept
            slope_weight = weight * wave.astype(F32) / (wave_top + 1.0)
            real, imag = x_ref[0:32, at], x_ref[32:64, at]
            a = jnp.concatenate([real * weight, -imag * slope_weight], axis=0)
            b = jnp.concatenate([imag * weight, real * slope_weight], axis=0)
            flip = (1 - (wave & 2)).astype(F32)
            if odd:
                on_cos = jnp.concatenate([a, flip * b], axis=0)
                on_sin = jnp.concatenate([-b, flip * a], axis=0)
            else:
                on_cos = jnp.concatenate([a, flip * a], axis=0)
                on_sin = jnp.concatenate([-b, -flip * b], axis=0)
            for offset, value in ((0, on_cos), (LANES, on_sin)):
                to = slice(block * 256 + offset, block * 256 + offset + LANES)
                high, low = split(value)
                l_ref[0:128, to] = high
                l_ref[128:256, to] = low

    start = 0
    while start < tiles * LANES:
        width = min(256, tiles * LANES - start)
        at = slice(start, start + width)
        start += width
        halves = []
        for l_ref, table_hi, table_lo in ((even_l, even_hi, even_lo), (odd_l, odd_hi, odd_lo)):
            whole = dot(l_ref[...], table_hi[:, at], NN)
            halves.append(whole[:128] + whole[128:] + dot(l_ref[0:128, :], table_lo[:, at], NN))
        inside = (at.start + lax.broadcasted_iota(jnp.int32, (1, width), 1)) < quarter
        even, odd = (jnp.where(inside, half, 0.0) for half in halves)
        quarters = [even[:64] + odd[:64], even[64:] - odd[64:], even[:64] - odd[:64], even[64:] + odd[64:]]
        fluxes = []
        for i, values in enumerate(quarters):
            segs[i, :, at] = values[:32]
            u, v, su, sv = (values[16 * n : 16 * n + 16] for n in range(4))
            fluxes.append(jnp.concatenate([u * u, u * v, v * v, u * su, u * sv], axis=0))
        for f_ref, sign in ((even_f, 1.0), (odd_f, -1.0)):
            for n in range(2):
                value = fluxes[n] + fluxes[n + 2] if sign > 0 else fluxes[n] - fluxes[n + 2]
                high, low = split(value)
                f_ref[80 * n : 80 * n + 80, at] = high
                f_ref[160 + 80 * n : 240 + 80 * n, at] = low

    grid_copy = pltpu.make_async_copy(segs, segs_ref, local_sems.at[0])
    grid_copy.start()

    scale = gauss_ref[row] * inverse
    for block in range(blocks):
        at = slice(block * LANES, (block + 1) * LANES)
        rows = slice(block * 256, (block + 1) * 256)
        evens = row_ref[:, at]
        for odd, f_ref, table_hi, table_lo in ((0, even_f, even_hi, even_lo), (1, odd_f, odd_hi, odd_lo)):
            whole = dot(f_ref[...], table_hi[rows, :], NT)
            total = whole[:160] + whole[160:] + dot(f_ref[0:160, :], table_lo[rows, :], NT)
            wave = wave_top - evens if odd else evens
            kept = jnp.where(wave <= highest, scale, 0.0)
            flip = (1 - (wave & 2)).astype(F32)
            first_cos, first_sin = total[:80, :LANES], total[:80, LANES:]
            second_cos, second_sin = total[80:, :LANES] * flip, total[80:, LANES:] * flip
            if odd:
                back[2, :, at] = (first_cos - second_sin) * kept
                back[3, :, at] = -(first_sin + second_cos) * kept
            else:
                back[0, :, at] = (first_cos + second_cos) * kept
                back[1, :, at] = -(first_sin + second_sin) * kept

    for dev in range(devices):
        at = slice(dev * share, (dev + 1) * share)
        for part in range(2):
            even, odd = back[part, :, at], back[2 + part, :, at]
            packed[part, :, 0:share] = even[:64]
            packed[part, :, share : 2 * share] = odd[:64]
            packed[part, 0:16, 2 * share : 3 * share] = even[64:]
            packed[part, 16:32, 2 * share : 3 * share] = odd[64:]
            for n in range(8):
                back_ref[dev, pl.ds(2 * n + part, 8, stride=16), :] = packed[
                    part, pl.ds(n // 2 * 16 + n % 2, 8, stride=2), :
                ]

    own_rows = pl.ds(pl.multiple_of(my_level * 16, 16), 16)
    own = pltpu.make_async_copy(back_ref.at[my_wave, own_rows, :], out_ref.at[here], local_sems.at[1])
    own.start()

    @pl.loop(1, everyone)
    def _(k):
        to_wave, to_level = peer(k)
        block = back_ref.at[to_wave, pl.ds(pl.multiple_of(to_level * 16, 16), 16), :]
        send(block, out_ref.at[here], back_sems, (to_wave, to_level)).start()

    arrival.wait_send()
    landed = out_ref.at[pl.ds(0, everyone - 1)]
    arrival = send(landed, landed, back_sems, (my_wave, my_level))
    arrival.wait_recv()
    arrival.wait_send()
    own.wait()
    grid_copy.wait()


def lay_quarters(quarter, segs, acc, grid_ref):
    tiles = segs.shape[2] // LANES
    lane = lax.broadcasted_iota(jnp.int32, (1, LANES), 1)
    acc[...] = jnp.zeros_like(acc)
    for i in range(4):
        begin = i * quarter
        shift = begin & (LANES - 1)
        base = lax.shift_right_logical(begin, 7)
        before = jnp.zeros((32, LANES), F32)
        for tile in range(tiles + 1):
            if tile < tiles:
                rolled = pltpu.roll(segs[i, :, tile * LANES : (tile + 1) * LANES], shift, 1)
            else:
                rolled = jnp.zeros((32, LANES), F32)
            at = pl.ds(pl.multiple_of((base + tile) * LANES, LANES), LANES)
            acc[:, at] += jnp.where(lane < shift, before, rolled)
            before = rolled
    pad_len = grid_ref.shape[3]
    for f in range(2):
        grid_ref[0, f] = acc[16 * f : 16 * f + 16, :pad_len]


def direct_kernel(
    group, wave_ref, band_ref, len_ref, in_ref, segs_ref, leg_ref, out_ref, grid_ref, natural, turned, acc
):
    step = pl.program_id(0)
    pack = leg_ref.shape[2]
    slots = pl.num_programs(0) * group
    wave_pos = lax.axis_index("wave")

    @pl.when(step == 0)
    def _():
        row = band_ref[wave_pos * lax.axis_size("level") + lax.axis_index("level")] & 63
        lay_quarters(lax.shift_right_logical(len_ref[row], 2), segs_ref, acc, grid_ref)

        @pl.loop(0, in_ref.shape[0], unroll=8)
        def _(i):
            natural[pl.ds(pl.multiple_of(band_ref[i] * 16, 16), 16), :] = in_ref[i]

        for n in range(16):
            turned[pl.ds(n, LANES, stride=16), :] = natural[pl.ds(n, LANES, stride=16), :].T

    position = lax.broadcasted_iota(jnp.int32, (1, pack), 1)
    south = lax.broadcasted_iota(jnp.int32, (1, LANES), 1) >= 64
    for g in range(group):
        slot = step * group + g
        first_wave = wave_ref[wave_pos * slots + slot]
        boundary = (pack - 1) - first_wave

        def of_lane(extra, count):
            return turned[pl.ds(pl.multiple_of((slot + extra) * 16, 16), count), :]

        x = jnp.concatenate([of_lane(0, 16), of_lane(slots, 16), of_lane(2 * slots, 8)], axis=0)
        other = pltpu.roll(x, 64, 1)
        difference = x - other
        y = jnp.concatenate([x + other, jnp.where(south, -difference, difference)], axis=0)
        left = jnp.concatenate(split(y), axis=0)
        right = jnp.concatenate(split(leg_ref[g]), axis=0)
        both = dot(left, right, NN)
        both = both[:80] + both[80:]
        in_first = position < boundary
        parity = jnp.where(in_first, position, position + boundary) & 1
        in_even = in_first == ((first_wave & 1) == 0)
        chosen = jnp.where(parity == 0, both[:40], both[40:])
        main = jnp.where(in_even, chosen[:16], chosen[16:32])
        last = jnp.where(in_even, chosen[32:36], chosen[36:40])
        for n in range(8):
            out_ref[g, n // 2, n % 2] = main[2 * n : 2 * n + 2]
        for n in range(2):
            out_ref[g, 4, n] = last[2 * n : 2 * n + 2]


def shards(spec_in, legendre, gauss, wave_map, band_map, row_len):
    wave_devices = lax.axis_size("wave")
    devices = wave_devices * lax.axis_size("level")
    slots, _, _, _, pack = spec_in.shape
    waves = pack - 1
    lat_pairs = legendre.shape[1]
    pad_len = (20 + 4 * (waves - 1) + 127) // 128 * 128
    table_len = (pad_len // 4 + 127) // 128 * 128
    smem = pl.BlockSpec(memory_space=pltpu.SMEM)
    group = 4

    def whole(*shape):
        return pl.BlockSpec(shape, lambda s: (0,) * len(shape))

    anywhere = pl.BlockSpec(memory_space=pl.ANY)
    half = waves // 2
    table = pltpu.VMEM((waves, table_len), BF16)
    segs, returned = pl.pallas_call(
        functools.partial(main_kernel, group),
        out_shape=(
            jax.ShapeDtypeStruct((4, 32, table_len), F32),
            jax.ShapeDtypeStruct((devices, 16, LANES), F32),
        ),
        grid=(slots // group,),
        in_specs=[
            smem,
            smem,
            smem,
            smem,
            whole(1, half),
            pl.BlockSpec((group, 2, 2, 2, pack), lambda s: (s, 0, 0, 0, 0)),
            pl.BlockSpec((group, lat_pairs, pack), lambda s: (s, 0, 0)),
        ],
        out_specs=(anywhere, anywhere),
        scratch_shapes=[
            pltpu.VMEM((8, pack), F32),
            pltpu.VMEM((slots * 32, LANES), F32),
            pltpu.VMEM((LANES * 8, LANES), F32),
            pltpu.VMEM((LANES, 8, LANES), F32),
            pltpu.VMEM((1, half), jnp.int32),
            pltpu.VMEM((half, LANES), F32),
            pltpu.VMEM((devices, 8, LANES), F32),
            pltpu.VMEM((wave_devices, 64, LANES), F32),
            pltpu.VMEM((4, 64, LANES), F32),
            pltpu.VMEM((64, half), F32),
            pltpu.VMEM((64, half), F32),
            pltpu.VMEM((256, waves), BF16),
            pltpu.VMEM((256, waves), BF16),
            table,
            table,
            table,
            table,
            pltpu.VMEM((4, 32, table_len), F32),
            pltpu.VMEM((320, table_len), BF16),
            pltpu.VMEM((320, table_len), BF16),
            pltpu.VMEM((4, 80, half), F32),
            pltpu.VMEM((2, 64, LANES), F32),
            pltpu.VMEM((wave_devices, 128, LANES), F32),
            pltpu.SemaphoreType.DMA((2,)),
            pltpu.SemaphoreType.DMA((2,)),
            pltpu.SemaphoreType.DMA((2,)),
        ],
        compiler_params=pltpu.CompilerParams(
            collective_id=0, has_side_effects=True, vmem_limit_bytes=56 * MIB
        ),
        name="rows",
    )(wave_map, band_map, row_len, gauss, wave_map[None, :], spec_in, legendre)

    spec_out, grid_out = pl.pallas_call(
        functools.partial(direct_kernel, group),
        out_shape=(
            jax.ShapeDtypeStruct((slots, 5, 2, 2, pack), F32),
            jax.ShapeDtypeStruct((1, 2, 16, pad_len), F32),
        ),
        grid=(slots // group,),
        in_specs=[
            smem,
            smem,
            smem,
            whole(devices, 16, LANES),
            whole(4, 32, table_len),
            pl.BlockSpec((group, lat_pairs, pack), lambda s: (s, 0, 0)),
        ],
        out_specs=(
            pl.BlockSpec((group, 5, 2, 2, pack), lambda s: (s, 0, 0, 0, 0)),
            whole(1, 2, 16, pad_len),
        ),
        scratch_shapes=[
            pltpu.VMEM((LANES * 16, LANES), F32),
            pltpu.VMEM((LANES * 16, LANES), F32),
            pltpu.VMEM((32, 4 * table_len), F32),
        ],
        compiler_params=pltpu.CompilerParams(vmem_limit_bytes=56 * MIB),
        name="direct",
    )(wave_map, band_map, row_len, returned, segs, legendre)
    return (grid_out, spec_out)


def solution(mesh):
    in_specs = (P("wave", None, "level", None, None), P("wave", None, None), P(), P(), P(), P())
    out_specs = (P(("wave", "level"), None, None, None), P("wave", None, "level", None, None))
    return jax.shard_map(shards, mesh=mesh, in_specs=in_specs, out_specs=out_specs, check_vma=False)
```

```python
import functools
import math

import jax
import jax.numpy as jnp
from jax import lax
from jax.experimental import pallas as pl
from jax.experimental.pallas import tpu as pltpu
from jax.sharding import PartitionSpec as P

F32 = jnp.float32
BF16 = jnp.bfloat16
LANES = 128
MIB = 1 << 20
STEPS = 10
SIN_TERMS = [(-1.0) ** i / math.factorial(2 * i + 1) for i in range(6)]
COS_TERMS = [(-1.0) ** i / math.factorial(2 * i) for i in range(7)]
MESH = pl.DeviceIdType.MESH
NT = (((1,), (1,)), ((), ()))
NN = (((1,), (0,)), ((), ()))
COEF_UNITS = [(f, part, odd) for f in range(2) for part in range(2) for odd in range(2)]
COEF_ROWS = [COEF_UNITS[i : i + 3] for i in range(0, 8, 3)]
FLUX_UNITS = [(x, odd) for x in range(5) for odd in range(2)]
FLUX_ROWS = [FLUX_UNITS[i : i + 3] for i in range(0, 9, 3)]


def dot(a, b, dims):
    return lax.dot_general(a, b, dims, preferred_element_type=F32)


def split(x):
    high = x.astype(BF16)
    return high, (x - high.astype(F32)).astype(BF16)


def horner(terms, x):
    total = jnp.full_like(x, terms[-1])
    for term in reversed(terms[:-1]):
        total = total * x + term
    return total


def turn_trig(steps, length, inverse):
    left = steps - jnp.floor(steps * inverse + 0.5) * length
    half = left * (inverse * math.pi)
    square = half * half
    sine = half * horner(SIN_TERMS, square)
    cosine = horner(COS_TERMS, square)
    return 1.0 - 2.0 * sine * sine, 2.0 * sine * cosine


def peer(k):
    wave, level = lax.axis_index("wave"), lax.axis_index("level")
    core, y, x, z = k % 2, k // 2 % 4, k // 8 % 4, k // 32
    return (wave // 4 + z) % 4 * 4 + (wave % 4 + x) % 4, (level // 2 + y) % 4 * 2 + (level % 2 + core) % 2


def send(source, target, sems, device):
    return pltpu.make_async_remote_copy(
        src_ref=source, dst_ref=target, send_sem=sems.at[0], recv_sem=sems.at[1], device_id=device, device_id_type=MESH
    )


def inverse_step(group, wave_ref, spec_ref, leg_ref, flat, sums):
    step = pl.program_id(0)
    slots = sums.shape[0] // 32
    pack = leg_ref.shape[2]
    wave_pos = lax.axis_index("wave")
    position = lax.broadcasted_iota(jnp.int32, (8, pack), 1)
    for g in range(group):
        slot = step * group + g
        first_wave = wave_ref[wave_pos * slots + slot]
        boundary = (pack - 1) - first_wave
        for pair in range(4):
            flat[2 * pair : 2 * pair + 2, :] = spec_ref[g, pair // 2, pair % 2]
        x = flat[...]
        in_first = position < boundary
        parity = jnp.where(in_first, position, position + boundary) & 1
        in_even = in_first == ((first_wave & 1) == 0)
        high = x.astype(BF16).astype(F32)
        parts = []
        for part in (high, x - high):
            signed = jnp.where(parity == 0, part, -part)
            for kept in (in_even, jnp.logical_not(in_even)):
                parts += [jnp.where(kept, part, 0.0), jnp.where(kept, signed, 0.0)]
        left = jnp.concatenate(parts, axis=0).astype(BF16)
        right = jnp.concatenate(split(leg_ref[g]), axis=0)
        both = dot(left, right, NT)
        both = both[:32] + both[32:]
        sums[pl.ds(pl.multiple_of(slot * 32, 32), 32), :] = both + pltpu.roll(both, 64, 1)


def sort_rows(band_ref, sums, flat_rows, rows, out_ref):
    slots = sums.shape[0] // 32
    north = lax.broadcasted_iota(jnp.int32, (slots, LANES), 1) < 64

    def piece(f, lv, part, odd):
        at = 16 * odd + 4 * f + 2 * lv + part
        south_at = at + 8
        return jnp.where(
            north, sums[pl.ds(at, slots, stride=32), :], sums[pl.ds(south_at, slots, stride=32), :]
        )

    for lv in range(2):
        for j, units in enumerate(COEF_ROWS):
            pieces = [piece(f, lv, part, odd) for f, part, odd in units]
            pieces.append(jnp.zeros((LANES - len(units) * slots, LANES), F32))
            flat_rows[pl.ds(3 * lv + j, LANES, stride=8), :] = jnp.concatenate(pieces, axis=0).T

    @pl.loop(0, LANES, unroll=8)
    def _(i):
        rows[i] = flat_rows[pl.ds(pl.multiple_of(i * 8, 8), 8), :]

    @pl.loop(0, out_ref.shape[0], unroll=8)
    def _(i):
        out_ref[i] = rows[band_ref[i]]


def main_kernel(
    group, wave_ref, band_ref, len_ref, gauss_ref, map_ref, spec_ref, leg_ref, segs_ref, out_ref,
    flat, sums, flat_rows, rows, row_ref, col_ref, send_ref, in_ref, sorted_x, even_x, odd_x, even_l, odd_l,
    even_hi, even_lo, odd_hi, odd_lo, segs, turned, even_f, odd_f, back, packed, back_ref, sems, back_sems, local_sems,
):
    step = pl.program_id(0)
    devices = send_ref.shape[0]
    barrier = pltpu.get_barrier_semaphore()

    greeted = (devices - 1) // STEPS
    for n in range(greeted):
        k = step * greeted + n + 1
        pl.semaphore_signal(barrier, inc=1, device_id=peer(k), device_id_type=MESH)

    inverse_step(group, wave_ref, spec_ref, leg_ref, flat, sums)

    @pl.when(step == STEPS - 1)
    def _():
        for k in range(STEPS * greeted + 1, devices):
            pl.semaphore_signal(barrier, inc=1, device_id=peer(k), device_id_type=MESH)
        sort_rows(band_ref, sums, flat_rows, rows, send_ref)
        pl.semaphore_wait(barrier, devices - 1)
        row_part(
            band_ref, len_ref, gauss_ref, map_ref, row_ref, col_ref, segs_ref, out_ref, send_ref, in_ref, sorted_x,
            even_x, odd_x, even_l, odd_l, even_hi, even_lo, odd_hi, odd_lo, segs, turned, even_f, odd_f, back, packed,
            back_ref, sems, back_sems, local_sems,
        )


def row_part(
    band_ref, len_ref, gauss_ref, map_ref, row_ref, col_ref, segs_ref, out_ref, send_ref, in_ref, sorted_x,
    even_x, odd_x, even_l, odd_l, even_hi, even_lo, odd_hi, odd_lo, segs, turned, even_f, odd_f, back, packed,
    back_ref, sems, back_sems, local_sems,
):
    my_wave, my_level = lax.axis_index("wave"), lax.axis_index("level")
    levels = lax.axis_size("level")
    here = my_wave * levels + my_level
    row = band_ref[here] & 63
    length = len_ref[row]
    quarter = lax.shift_right_logical(length, 2)
    wave_top = 2 * row_ref.shape[1] - 1
    length_f = jnp.full((1, LANES), length.astype(F32))
    inverse = 1.0 / length_f
    half_waves = row_ref.shape[1]
    blocks = half_waves // LANES
    devices = in_ref.shape[0]
    everyone = devices * levels
    share = half_waves // devices
    tiles = even_hi.shape[1] // LANES
    lane = lax.broadcasted_iota(jnp.int32, (1, LANES), 1)

    mapped = map_ref[...]
    row_ref[...] = jnp.where((mapped & 1) == 0, mapped, wave_top - mapped)
    for block in range(blocks):
        at = slice(block * LANES, (block + 1) * LANES)
        col_ref[at, :] = jnp.broadcast_to(row_ref[:, at].astype(F32), (LANES, LANES)).T

    def start_send(k):
        to_wave, to_level = peer(k)
        mine = in_ref.at[my_wave, pl.ds(pl.multiple_of(my_level * 8, 8), 6), :]
        send(send_ref.at[to_wave * levels + to_level, pl.ds(0, 6), :], mine, sems, (to_wave, to_level)).start()

    def make_tables(group):
        block, inner = group // 4, group % 4
        at_cos = pl.multiple_of(block * 256 + inner * 32, 32)
        at_sin = pl.multiple_of(block * 256 + LANES + inner * 32, 32)
        evens = col_ref[pl.ds(pl.multiple_of(group * 32, 32), 32), :]
        for waves, table_hi, table_lo in ((evens, even_hi, even_lo), (wave_top - evens, odd_hi, odd_lo)):
            cosine, sine = turn_trig(waves * lane.astype(F32), length_f, inverse)
            turn_cos, turn_sin = turn_trig(waves * float(LANES), length_f, inverse)
            for tile in range(tiles):
                at = slice(tile * LANES, (tile + 1) * LANES)
                high, low = split(cosine)
                table_hi[pl.ds(at_cos, 32), at] = high
                table_lo[pl.ds(at_cos, 32), at] = low
                high, low = split(sine)
                table_hi[pl.ds(at_sin, 32), at] = high
                table_lo[pl.ds(at_sin, 32), at] = low
                if tile < tiles - 1:
                    cosine, sine = (
                        cosine * turn_cos - sine * turn_sin,
                        sine * turn_cos + cosine * turn_sin,
                    )

    in_ref[my_wave, pl.ds(pl.multiple_of(my_level * 8, 8), 8), :] = send_ref[here]
    start_send(1)

    @pl.loop(0, 9)
    def _(group):
        for n in range(14):
            start_send(group * 14 + n + 2)
        make_tables(group)

    @pl.loop(9, half_waves // 32)
    def _(group):
        make_tables(group)

    landed = send_ref.at[pl.ds(0, everyone - 1), pl.ds(0, 6), :]
    arrival = send(landed, landed, sems, (my_wave, my_level))
    arrival.wait_recv()

    for dev in range(devices):
        at = slice(dev * share, (dev + 1) * share)
        for j, units in enumerate(COEF_ROWS):
            for lv in range(2):
                sorted_x[dev % 4, j, pl.ds(lv, 8, stride=2), :] = in_ref[dev, pl.ds(3 * lv + j, 8, stride=8), :]
            for n, (f, part, odd) in enumerate(units):
                to = slice(32 * part + 16 * f, 32 * part + 16 * f + 16)
                x_ref = odd_x if odd else even_x
                x_ref[to, at] = sorted_x[dev % 4, j, :, n * share : (n + 1) * share]

    highest = jnp.minimum(wave_top, lax.shift_right_logical(length - 1, 1))
    for block in range(blocks):
        at = slice(block * LANES, (block + 1) * LANES)
        evens = row_ref[:, at]
        for odd, x_ref, l_ref in ((False, even_x, even_l), (True, odd_x, odd_l)):
            wave = wave_top - evens if odd else evens
            kept = (wave <= highest).astype(F32)
            weight = jnp.where(wave == 0, 1.0, 2.0) * kept
            slope_weight = weight * wave.astype(F32) / (wave_top + 1.0)
            real, imag = x_ref[0:32, at], x_ref[32:64, at]
            a = jnp.concatenate([real * weight, -imag * slope_weight], axis=0)
            b = jnp.concatenate([imag * weight, real * slope_weight], axis=0)
            flip = (1 - (wave & 2)).astype(F32)
            if odd:
                on_cos = jnp.concatenate([a, flip * b], axis=0)
                on_sin = jnp.concatenate([-b, flip * a], axis=0)
            else:
                on_cos = jnp.concatenate([a, flip * a], axis=0)
                on_sin = jnp.concatenate([-b, -flip * b], axis=0)
            for offset, value in ((0, on_cos), (LANES, on_sin)):
                to = slice(block * 256 + offset, block * 256 + offset + LANES)
                high, low = split(value)
                l_ref[0:128, to] = high
                l_ref[128:256, to] = low

    start = 0
    while start < tiles * LANES:
        width = min(256, tiles * LANES - start)
        at = slice(start, start + width)
        start += width
        halves = []
        for l_ref, table_hi, table_lo in ((even_l, even_hi, even_lo), (odd_l, odd_hi, odd_lo)):
            whole = dot(l_ref[...], table_hi[:, at], NN)
            halves.append(whole[:128] + whole[128:] + dot(l_ref[0:128, :], table_lo[:, at], NN))
        inside = (at.start + lax.broadcasted_iota(jnp.int32, (1, width), 1)) < quarter
        even, odd = (jnp.where(inside, half, 0.0) for half in halves)
        quarters = [even[:64] + odd[:64], even[64:] - odd[64:], even[:64] - odd[:64], even[64:] + odd[64:]]
        fluxes = []
        for i, values in enumerate(quarters):
            segs[i, :, at] = values[:32]
            u, v, su, sv = (values[16 * n : 16 * n + 16] for n in range(4))
            fluxes.append(jnp.concatenate([u * u, u * v, v * v, u * su, u * sv], axis=0))
        for f_ref, sign in ((even_f, 1.0), (odd_f, -1.0)):
            for n in range(2):
                value = fluxes[n] + fluxes[n + 2] if sign > 0 else fluxes[n] - fluxes[n + 2]
                high, low = split(value)
                f_ref[80 * n : 80 * n + 80, at] = high
                f_ref[160 + 80 * n : 240 + 80 * n, at] = low

    scale = gauss_ref[row] * inverse

    def fourier_sums(block):
        at = pl.ds(pl.multiple_of(block * LANES, LANES), LANES)
        rows = pl.ds(pl.multiple_of(block * 256, 256), 256)
        evens = row_ref[:, at]
        for odd, f_ref, table_hi, table_lo in ((0, even_f, even_hi, even_lo), (1, odd_f, odd_hi, odd_lo)):
            whole = dot(f_ref[...], table_hi[rows, :], NT)
            total = whole[:160] + whole[160:] + dot(f_ref[0:160, :], table_lo[rows, :], NT)
            waves = wave_top - evens if odd else evens
            kept = jnp.where(waves <= highest, scale, 0.0)
            flip = (1 - (waves & 2)).astype(F32)
            first_cos, first_sin = total[:80, :LANES], total[:80, LANES:]
            second_cos, second_sin = total[80:, :LANES] * flip, total[80:, LANES:] * flip
            if odd:
                back[2, :, at] = (first_cos - second_sin) * kept
                back[3, :, at] = -(first_sin + second_cos) * kept
            else:
                back[0, :, at] = (first_cos + second_cos) * kept
                back[1, :, at] = -(first_sin + second_sin) * kept

    def send_back(dev):
        begin = dev * share
        base = lax.shift_right_logical(begin, 7)
        offset = begin & (LANES - 1)
        tiles_at = [pl.ds(pl.multiple_of((base + n) * LANES, LANES), LANES) for n in range(2)]

        def unit(x, odd, part, place):
            to = place * share
            shift = (to - offset + LANES) & (LANES - 1)
            rolled = [pltpu.roll(back[2 * odd + part, 16 * x : 16 * x + 16, at], shift, 1) for at in tiles_at]
            return jnp.where(lane - to + offset < LANES, rolled[0], rolled[1])

        def joined(units):
            value = units[0]
            for n, other in enumerate(units[1:]):
                value = jnp.where(lane < (n + 1) * share, value, other)
            return value

        for part in range(2):
            for j, units in enumerate(FLUX_ROWS):
                packed[3 * part + j] = joined([unit(x, odd, part, n) for n, (x, odd) in enumerate(units)])
        packed[6] = joined([unit(4, 1, part, part) for part in range(2)])
        for lv in range(2):
            for part in range(2):
                for j in range(3):
                    back_ref[dev, pl.ds(6 * lv + 3 * part + j, 8, stride=16), :] = packed[
                        3 * part + j, pl.ds(lv, 8, stride=2), :
                    ]
            back_ref[dev, pl.ds(12 + lv, 8, stride=16), :] = packed[6, pl.ds(lv, 8, stride=2), :]

        def start_block(to_level):
            block = back_ref.at[dev, pl.ds(pl.multiple_of(to_level * 16, 16), 14), :]
            send(block, out_ref.at[here, pl.ds(0, 14), :], back_sems, (dev, to_level)).start()

        for n in range(1, 8):
            start_block((my_level + n) % levels)

        @pl.when(dev != my_wave)
        def _():
            start_block(my_level)

    first = my_wave * blocks // devices

    @pl.loop(0, blocks)
    def _(turn):
        block = (turn + first) % blocks
        fourier_sums(block)
        low = jnp.where((turn == 0) & (block > 0), 3 * block + 1, 3 * block)
        high = jnp.where(block == blocks - 1, devices, 3 * block + 3)

        @pl.loop(low, high)
        def _(dev):
            send_back(dev)

        @pl.when((turn == blocks - 1) & (first > 0))
        def _():
            send_back(3 * first)

    own_rows = pl.ds(pl.multiple_of(my_level * 16, 16), 16)
    own = pltpu.make_async_copy(back_ref.at[my_wave, own_rows, :], out_ref.at[here], local_sems.at[1])
    own.start()

    for i in range(4):
        shift = (i * quarter) & (LANES - 1)
        before = jnp.zeros((32, LANES), F32)
        for tile in range(tiles + 1):
            at = slice(tile * LANES, (tile + 1) * LANES)
            rolled = pltpu.roll(segs[i, :, at], shift, 1) if tile < tiles else jnp.zeros((32, LANES), F32)
            turned[i, :, at] = jnp.where(lane < shift, before, rolled)
            before = rolled
    grid_copy = pltpu.make_async_copy(turned, segs_ref, local_sems.at[0])
    grid_copy.start()

    arrival.wait_send()
    landed = out_ref.at[pl.ds(0, everyone - 1), pl.ds(0, 14), :]
    arrival = send(landed, landed, back_sems, (my_wave, my_level))
    arrival.wait_recv()
    arrival.wait_send()
    own.wait()
    grid_copy.wait()


def lay_quarters(quarter, segs, acc, grid_ref):
    pad_len = grid_ref.shape[3]
    acc[...] = jnp.zeros_like(acc)
    for i in range(4):
        base = lax.shift_right_logical(i * quarter, 7)
        for tile in range(segs.shape[2] // LANES):
            at = pl.ds(pl.multiple_of((base + tile) * LANES, LANES), LANES)
            acc[:, at] += segs[i, :, tile * LANES : (tile + 1) * LANES]
    for f in range(2):
        grid_ref[0, f] = acc[16 * f : 16 * f + 16, :pad_len]


def direct_kernel(
    group, wave_ref, band_ref, len_ref, in_ref, segs_ref, leg_ref, out_ref, grid_ref, natural, turned, acc
):
    step = pl.program_id(0)
    pack = leg_ref.shape[2]
    slots = STEPS * group
    wave_pos = lax.axis_index("wave")

    @pl.when(step == 0)
    def _():
        row = band_ref[wave_pos * lax.axis_size("level") + lax.axis_index("level")] & 63
        lay_quarters(lax.shift_right_logical(len_ref[row], 2), segs_ref, acc, grid_ref)

        @pl.loop(0, in_ref.shape[0], unroll=8)
        def _(i):
            natural[pl.ds(pl.multiple_of(band_ref[i] * 16, 16), 16), :] = in_ref[i]

        for lv in range(2):
            lines = [(3 * p + j, p, FLUX_ROWS[j]) for p in range(2) for j in range(3)]
            for line, part, units in [(6 * lv + n, p, u) for n, p, u in lines] + [(12 + lv, None, ())]:
                block = natural[pl.ds(line, LANES, stride=16), :].T
                placed = [(x, odd, part) for x, odd in units] or [(4, 1, 0), (4, 1, 1)]
                for n, (x, odd, p) in enumerate(placed):
                    to = 4 * x + 2 * lv + p + (16 if x < 4 else 4) * odd + (16 if x == 4 else 0)
                    turned[pl.ds(to, slots, stride=40), :] = block[n * slots : (n + 1) * slots]

    position = lax.broadcasted_iota(jnp.int32, (1, pack), 1)
    south = lax.broadcasted_iota(jnp.int32, (1, LANES), 1) >= 64
    for g in range(group):
        slot = step * group + g
        first_wave = wave_ref[wave_pos * slots + slot]
        boundary = (pack - 1) - first_wave

        x = turned[pl.ds(pl.multiple_of(slot * 40, 8), 40), :]
        other = pltpu.roll(x, 64, 1)
        difference = x - other
        y = jnp.concatenate([x + other, jnp.where(south, -difference, difference)], axis=0)
        left = jnp.concatenate(split(y), axis=0)
        right = jnp.concatenate(split(leg_ref[g]), axis=0)
        both = dot(left, right, NN)
        both = both[:80] + both[80:]
        in_first = position < boundary
        parity = jnp.where(in_first, position, position + boundary) & 1
        in_even = in_first == ((first_wave & 1) == 0)
        chosen = jnp.where(parity == 0, both[:40], both[40:])
        main = jnp.where(in_even, chosen[:16], chosen[16:32])
        last = jnp.where(in_even, chosen[32:36], chosen[36:40])
        for n in range(8):
            out_ref[g, n // 2, n % 2] = main[2 * n : 2 * n + 2]
        for n in range(2):
            out_ref[g, 4, n] = last[2 * n : 2 * n + 2]


def shards(spec_in, legendre, gauss, wave_map, band_map, row_len):
    wave_devices = lax.axis_size("wave")
    devices = wave_devices * lax.axis_size("level")
    slots, _, _, _, pack = spec_in.shape
    waves = pack - 1
    lat_pairs = legendre.shape[1]
    pad_len = (20 + 4 * (waves - 1) + 127) // 128 * 128
    table_len = (pad_len // 4 + 127) // 128 * 128
    smem = pl.BlockSpec(memory_space=pltpu.SMEM)
    group = slots // STEPS

    def whole(*shape):
        return pl.BlockSpec(shape, lambda s: (0,) * len(shape))

    anywhere = pl.BlockSpec(memory_space=pl.ANY)
    half = waves // 2
    table = pltpu.VMEM((waves, table_len), BF16)
    segs, returned = pl.pallas_call(
        functools.partial(main_kernel, group),
        out_shape=(
            jax.ShapeDtypeStruct((4, 32, table_len + LANES), F32),
            jax.ShapeDtypeStruct((devices, 16, LANES), F32),
        ),
        grid=(slots // group,),
        in_specs=[
            smem,
            smem,
            smem,
            smem,
            whole(1, half),
            pl.BlockSpec((group, 2, 2, 2, pack), lambda s: (s, 0, 0, 0, 0)),
            pl.BlockSpec((group, lat_pairs, pack), lambda s: (s, 0, 0)),
        ],
        out_specs=(anywhere, anywhere),
        scratch_shapes=[
            pltpu.VMEM((8, pack), F32),
            pltpu.VMEM((slots * 32, LANES), F32),
            pltpu.VMEM((LANES * 8, LANES), F32),
            pltpu.VMEM((LANES, 8, LANES), F32),
            pltpu.VMEM((1, half), jnp.int32),
            pltpu.VMEM((half, LANES), F32),
            pltpu.VMEM((devices, 8, LANES), F32),
            pltpu.VMEM((wave_devices, 64, LANES), F32),
            pltpu.VMEM((4, 3, 16, LANES), F32),
            pltpu.VMEM((64, half), F32),
            pltpu.VMEM((64, half), F32),
            pltpu.VMEM((256, waves), BF16),
            pltpu.VMEM((256, waves), BF16),
            table,
            table,
            table,
            table,
            pltpu.VMEM((4, 32, table_len), F32),
            pltpu.VMEM((4, 32, table_len + LANES), F32),
            pltpu.VMEM((320, table_len), BF16),
            pltpu.VMEM((320, table_len), BF16),
            pltpu.VMEM((4, 80, half + LANES), F32),
            pltpu.VMEM((7, 16, LANES), F32),
            pltpu.VMEM((wave_devices, 128, LANES), F32),
            pltpu.SemaphoreType.DMA((2,)),
            pltpu.SemaphoreType.DMA((2,)),
            pltpu.SemaphoreType.DMA((2,)),
        ],
        compiler_params=pltpu.CompilerParams(
            collective_id=0, has_side_effects=True, vmem_limit_bytes=56 * MIB
        ),
        name="rows",
    )(wave_map, band_map, row_len, gauss, wave_map[None, :], spec_in, legendre)

    spec_out, grid_out = pl.pallas_call(
        functools.partial(direct_kernel, group),
        out_shape=(
            jax.ShapeDtypeStruct((slots, 5, 2, 2, pack), F32),
            jax.ShapeDtypeStruct((1, 2, 16, pad_len), F32),
        ),
        grid=(slots // group,),
        in_specs=[
            smem,
            smem,
            smem,
            whole(devices, 16, LANES),
            whole(4, 32, table_len + LANES),
            pl.BlockSpec((group, lat_pairs, pack), lambda s: (s, 0, 0)),
        ],
        out_specs=(
            pl.BlockSpec((group, 5, 2, 2, pack), lambda s: (s, 0, 0, 0, 0)),
            whole(1, 2, 16, pad_len),
        ),
        scratch_shapes=[
            pltpu.VMEM((LANES * 16, LANES), F32),
            pltpu.VMEM((slots * 40, LANES), F32),
            pltpu.VMEM((32, 4 * table_len), F32),
        ],
        compiler_params=pltpu.CompilerParams(vmem_limit_bytes=56 * MIB),
        name="direct",
    )(wave_map, band_map, row_len, returned, segs, legendre)
    return (grid_out, spec_out)


def solution(mesh):
    in_specs = (P("wave", None, "level", None, None), P("wave", None, None), P(), P(), P(), P())
    out_specs = (P(("wave", "level"), None, None, None), P("wave", None, "level", None, None))
    return jax.shard_map(shards, mesh=mesh, in_specs=in_specs, out_specs=out_specs, check_vma=False)
```

```python
import functools
import math

import jax
import jax.numpy as jnp
from jax import lax
from jax.experimental import pallas as pl
from jax.experimental.pallas import tpu as pltpu
from jax.sharding import PartitionSpec as P

F32 = jnp.float32
BF16 = jnp.bfloat16
LANES = 128
MIB = 1 << 20
STEPS = 10
SIN_TERMS = [(-1.0) ** i / math.factorial(2 * i + 1) for i in range(6)]
COS_TERMS = [(-1.0) ** i / math.factorial(2 * i) for i in range(7)]
MESH = pl.DeviceIdType.MESH
NT = (((1,), (1,)), ((), ()))
NN = (((1,), (0,)), ((), ()))
COEF_UNITS = [(f, part, odd) for f in range(2) for part in range(2) for odd in range(2)]
COEF_ROWS = [COEF_UNITS[i : i + 3] for i in range(0, 8, 3)]
FLUX_UNITS = [(x, odd) for x in range(5) for odd in range(2)]
FLUX_ROWS = [FLUX_UNITS[i : i + 3] for i in range(0, 9, 3)]


def dot(a, b, dims):
    return lax.dot_general(a, b, dims, preferred_element_type=F32)


def split(x):
    high = x.astype(BF16)
    return high, (x - high.astype(F32)).astype(BF16)


def horner(terms, x):
    total = jnp.full_like(x, terms[-1])
    for term in reversed(terms[:-1]):
        total = total * x + term
    return total


def turn_trig(steps, length, inverse):
    left = steps - jnp.floor(steps * inverse + 0.5) * length
    half = left * (inverse * math.pi)
    square = half * half
    sine = half * horner(SIN_TERMS, square)
    cosine = horner(COS_TERMS, square)
    return 1.0 - 2.0 * sine * sine, 2.0 * sine * cosine


def peer(k):
    wave, level = lax.axis_index("wave"), lax.axis_index("level")
    core, y, x, z = k % 2, k // 2 % 4, k // 8 % 4, k // 32
    return (wave // 4 + z) % 4 * 4 + (wave % 4 + x) % 4, (level // 2 + y) % 4 * 2 + (level % 2 + core) % 2


def send(source, target, sems, device):
    return pltpu.make_async_remote_copy(
        src_ref=source, dst_ref=target, send_sem=sems.at[0], recv_sem=sems.at[1], device_id=device, device_id_type=MESH
    )


def group_copies(group, sources, targets, sems):
    def copies(n):
        at = pl.ds(n * group, group)
        return [
            pltpu.make_async_copy(source.at[at], target.at[at], sems.at[i, n])
            for i, (source, target) in enumerate(zip(sources, targets))
        ]

    return copies


def inverse_step(step, group, wave_ref, spec_ref, leg_ref, flat, sums):
    slots = sums.shape[0] // 32
    pack = leg_ref.shape[2]
    wave_pos = lax.axis_index("wave")
    position = lax.broadcasted_iota(jnp.int32, (8, pack), 1)
    for g in range(group):
        slot = step * group + g
        first_wave = wave_ref[wave_pos * slots + slot]
        boundary = (pack - 1) - first_wave
        for pair in range(4):
            flat[g, 2 * pair : 2 * pair + 2, :] = spec_ref[slot, pair // 2, pair % 2]
        x = flat[g]
        in_first = position < boundary
        parity = jnp.where(in_first, position, position + boundary) & 1
        in_even = in_first == ((first_wave & 1) == 0)
        high = x.astype(BF16).astype(F32)
        parts = []
        for part in (high, x - high):
            signed = jnp.where(parity == 0, part, -part)
            for kept in (in_even, jnp.logical_not(in_even)):
                parts += [jnp.where(kept, part, 0.0), jnp.where(kept, signed, 0.0)]
        left = jnp.concatenate(parts, axis=0).astype(BF16)
        right = jnp.concatenate(split(leg_ref[slot]), axis=0)
        both = dot(left, right, NT)
        both = both[:32] + both[32:]
        sums[pl.ds(pl.multiple_of(slot * 32, 32), 32), :] = both + pltpu.roll(both, 64, 1)


def sort_rows(band_ref, sums, flat_rows, rows, out_ref):
    slots = sums.shape[0] // 32
    north = lax.broadcasted_iota(jnp.int32, (slots, LANES), 1) < 64

    def piece(f, lv, part, odd):
        at = 16 * odd + 4 * f + 2 * lv + part
        south_at = at + 8
        return jnp.where(
            north, sums[pl.ds(at, slots, stride=32), :], sums[pl.ds(south_at, slots, stride=32), :]
        )

    for lv in range(2):
        for j, units in enumerate(COEF_ROWS):
            pieces = [piece(f, lv, part, odd) for f, part, odd in units]
            pieces.append(jnp.zeros((LANES - len(units) * slots, LANES), F32))
            flat_rows[pl.ds(3 * lv + j, LANES, stride=8), :] = jnp.concatenate(pieces, axis=0).T

    @pl.loop(0, LANES, unroll=8)
    def _(i):
        rows[i] = flat_rows[pl.ds(pl.multiple_of(i * 8, 8), 8), :]

    @pl.loop(0, out_ref.shape[0], unroll=8)
    def _(i):
        out_ref[i] = rows[band_ref[i]]


def main_kernel(
    group, wave_ref, band_ref, len_ref, gauss_ref, map_ref, spec_hbm, leg_hbm, segs_ref, out_ref, spec_ref, leg_ref,
    flat, sums, flat_rows, rows, row_ref, col_ref, send_ref, in_ref, sorted_x, even_x, odd_x, even_l, odd_l,
    even_hi, even_lo, odd_hi, odd_lo, segs, turned, even_f, odd_f, back, packed, back_ref,
    load_sems, sems, back_sems, local_sems,
):
    devices = send_ref.shape[0]
    barrier = pltpu.get_barrier_semaphore()
    copies = group_copies(group, (spec_hbm, leg_hbm), (spec_ref, leg_ref), load_sems)
    for n in range(STEPS):
        for copy in copies(n):
            copy.start()
    greeted = (devices - 1) // STEPS

    def greet(k):
        pl.semaphore_signal(barrier, inc=1, device_id=peer(k), device_id_type=MESH)

    @pl.loop(0, STEPS)
    def _(step):
        for copy in copies(step):
            copy.wait()
        for n in range(greeted):
            greet(step * greeted + n + 1)
        inverse_step(step, group, wave_ref, spec_ref, leg_ref, flat, sums)

    for k in range(STEPS * greeted + 1, devices):
        greet(k)
    sort_rows(band_ref, sums, flat_rows, rows, send_ref)
    pl.semaphore_wait(barrier, devices - 1)
    row_part(
        band_ref, len_ref, gauss_ref, map_ref, row_ref, col_ref, segs_ref, out_ref, send_ref, in_ref, sorted_x,
        even_x, odd_x, even_l, odd_l, even_hi, even_lo, odd_hi, odd_lo, segs, turned, even_f, odd_f, back, packed,
        back_ref, sems, back_sems, local_sems,
    )


def row_part(
    band_ref, len_ref, gauss_ref, map_ref, row_ref, col_ref, segs_ref, out_ref, send_ref, in_ref, sorted_x,
    even_x, odd_x, even_l, odd_l, even_hi, even_lo, odd_hi, odd_lo, segs, turned, even_f, odd_f, back, packed,
    back_ref, sems, back_sems, local_sems,
):
    my_wave, my_level = lax.axis_index("wave"), lax.axis_index("level")
    levels = lax.axis_size("level")
    here = my_wave * levels + my_level
    row = band_ref[here] & 63
    length = len_ref[row]
    quarter = lax.shift_right_logical(length, 2)
    wave_top = 2 * row_ref.shape[1] - 1
    length_f = jnp.full((1, LANES), length.astype(F32))
    inverse = 1.0 / length_f
    half_waves = row_ref.shape[1]
    blocks = half_waves // LANES
    devices = in_ref.shape[0]
    everyone = devices * levels
    share = half_waves // devices
    tiles = even_hi.shape[1] // LANES
    lane = lax.broadcasted_iota(jnp.int32, (1, LANES), 1)

    mapped = map_ref[...]
    row_ref[...] = jnp.where((mapped & 1) == 0, mapped, wave_top - mapped)
    for block in range(blocks):
        at = slice(block * LANES, (block + 1) * LANES)
        col_ref[at, :] = jnp.broadcast_to(row_ref[:, at].astype(F32), (LANES, LANES)).T

    def start_send(k):
        to_wave, to_level = peer(k)
        mine = in_ref.at[my_wave, pl.ds(pl.multiple_of(my_level * 8, 8), 6), :]
        send(send_ref.at[to_wave * levels + to_level, pl.ds(0, 6), :], mine, sems, (to_wave, to_level)).start()

    def make_tables(group):
        block, inner = group // 4, group % 4
        at_cos = pl.multiple_of(block * 256 + inner * 32, 32)
        at_sin = pl.multiple_of(block * 256 + LANES + inner * 32, 32)
        evens = col_ref[pl.ds(pl.multiple_of(group * 32, 32), 32), :]
        for waves, table_hi, table_lo in ((evens, even_hi, even_lo), (wave_top - evens, odd_hi, odd_lo)):
            cosine, sine = turn_trig(waves * lane.astype(F32), length_f, inverse)
            turn_cos, turn_sin = turn_trig(waves * float(LANES), length_f, inverse)
            for tile in range(tiles):
                at = slice(tile * LANES, (tile + 1) * LANES)
                high, low = split(cosine)
                table_hi[pl.ds(at_cos, 32), at] = high
                table_lo[pl.ds(at_cos, 32), at] = low
                high, low = split(sine)
                table_hi[pl.ds(at_sin, 32), at] = high
                table_lo[pl.ds(at_sin, 32), at] = low
                if tile < tiles - 1:
                    cosine, sine = (
                        cosine * turn_cos - sine * turn_sin,
                        sine * turn_cos + cosine * turn_sin,
                    )

    in_ref[my_wave, pl.ds(pl.multiple_of(my_level * 8, 8), 8), :] = send_ref[here]
    start_send(1)

    @pl.loop(0, 9)
    def _(group):
        for n in range(14):
            start_send(group * 14 + n + 2)
        make_tables(group)

    @pl.loop(9, half_waves // 32)
    def _(group):
        make_tables(group)

    landed = send_ref.at[pl.ds(0, everyone - 1), pl.ds(0, 6), :]
    arrival = send(landed, landed, sems, (my_wave, my_level))
    arrival.wait_recv()

    for dev in range(devices):
        at = slice(dev * share, (dev + 1) * share)
        for j, units in enumerate(COEF_ROWS):
            for lv in range(2):
                sorted_x[dev % 4, j, pl.ds(lv, 8, stride=2), :] = in_ref[dev, pl.ds(3 * lv + j, 8, stride=8), :]
            for n, (f, part, odd) in enumerate(units):
                to = slice(32 * part + 16 * f, 32 * part + 16 * f + 16)
                x_ref = odd_x if odd else even_x
                x_ref[to, at] = sorted_x[dev % 4, j, :, n * share : (n + 1) * share]

    highest = jnp.minimum(wave_top, lax.shift_right_logical(length - 1, 1))
    for block in range(blocks):
        at = slice(block * LANES, (block + 1) * LANES)
        evens = row_ref[:, at]
        for odd, x_ref, l_ref in ((False, even_x, even_l), (True, odd_x, odd_l)):
            wave = wave_top - evens if odd else evens
            kept = (wave <= highest).astype(F32)
            weight = jnp.where(wave == 0, 1.0, 2.0) * kept
            slope_weight = weight * wave.astype(F32) / (wave_top + 1.0)
            real, imag = x_ref[0:32, at], x_ref[32:64, at]
            a = jnp.concatenate([real * weight, -imag * slope_weight], axis=0)
            b = jnp.concatenate([imag * weight, real * slope_weight], axis=0)
            flip = (1 - (wave & 2)).astype(F32)
            if odd:
                on_cos = jnp.concatenate([a, flip * b], axis=0)
                on_sin = jnp.concatenate([-b, flip * a], axis=0)
            else:
                on_cos = jnp.concatenate([a, flip * a], axis=0)
                on_sin = jnp.concatenate([-b, -flip * b], axis=0)
            for offset, value in ((0, on_cos), (LANES, on_sin)):
                to = slice(block * 256 + offset, block * 256 + offset + LANES)
                high, low = split(value)
                l_ref[0:128, to] = high
                l_ref[128:256, to] = low

    start = 0
    while start < tiles * LANES:
        width = min(256, tiles * LANES - start)
        at = slice(start, start + width)
        start += width
        halves = []
        for l_ref, table_hi, table_lo in ((even_l, even_hi, even_lo), (odd_l, odd_hi, odd_lo)):
            whole = dot(l_ref[...], table_hi[:, at], NN)
            halves.append(whole[:128] + whole[128:] + dot(l_ref[0:128, :], table_lo[:, at], NN))
        inside = (at.start + lax.broadcasted_iota(jnp.int32, (1, width), 1)) < quarter
        even, odd = (jnp.where(inside, half, 0.0) for half in halves)
        quarters = [even[:64] + odd[:64], even[64:] - odd[64:], even[:64] - odd[:64], even[64:] + odd[64:]]
        fluxes = []
        for i, values in enumerate(quarters):
            segs[i, :, at] = values[:32]
            u, v, su, sv = (values[16 * n : 16 * n + 16] for n in range(4))
            fluxes.append(jnp.concatenate([u * u, u * v, v * v, u * su, u * sv], axis=0))
        for f_ref, sign in ((even_f, 1.0), (odd_f, -1.0)):
            for n in range(2):
                value = fluxes[n] + fluxes[n + 2] if sign > 0 else fluxes[n] - fluxes[n + 2]
                high, low = split(value)
                f_ref[80 * n : 80 * n + 80, at] = high
                f_ref[160 + 80 * n : 240 + 80 * n, at] = low

    scale = gauss_ref[row] * inverse

    def fourier_sums(block):
        at = pl.ds(pl.multiple_of(block * LANES, LANES), LANES)
        rows = pl.ds(pl.multiple_of(block * 256, 256), 256)
        evens = row_ref[:, at]
        for odd, f_ref, table_hi, table_lo in ((0, even_f, even_hi, even_lo), (1, odd_f, odd_hi, odd_lo)):
            whole = dot(f_ref[...], table_hi[rows, :], NT)
            total = whole[:160] + whole[160:] + dot(f_ref[0:160, :], table_lo[rows, :], NT)
            waves = wave_top - evens if odd else evens
            kept = jnp.where(waves <= highest, scale, 0.0)
            flip = (1 - (waves & 2)).astype(F32)
            first_cos, first_sin = total[:80, :LANES], total[:80, LANES:]
            second_cos, second_sin = total[80:, :LANES] * flip, total[80:, LANES:] * flip
            if odd:
                back[2, :, at] = (first_cos - second_sin) * kept
                back[3, :, at] = -(first_sin + second_cos) * kept
            else:
                back[0, :, at] = (first_cos + second_cos) * kept
                back[1, :, at] = -(first_sin + second_sin) * kept

    def send_back(dev):
        begin = dev * share
        base = lax.shift_right_logical(begin, 7)
        offset = begin & (LANES - 1)
        tiles_at = [pl.ds(pl.multiple_of((base + n) * LANES, LANES), LANES) for n in range(2)]

        def unit(x, odd, part, place):
            to = place * share
            shift = (to - offset + LANES) & (LANES - 1)
            rolled = [pltpu.roll(back[2 * odd + part, 16 * x : 16 * x + 16, at], shift, 1) for at in tiles_at]
            return jnp.where(lane - to + offset < LANES, rolled[0], rolled[1])

        def joined(units):
            value = units[0]
            for n, other in enumerate(units[1:]):
                value = jnp.where(lane < (n + 1) * share, value, other)
            return value

        for part in range(2):
            for j, units in enumerate(FLUX_ROWS):
                packed[3 * part + j] = joined([unit(x, odd, part, n) for n, (x, odd) in enumerate(units)])
        packed[6] = joined([unit(4, 1, part, part) for part in range(2)])
        for lv in range(2):
            for part in range(2):
                for j in range(3):
                    back_ref[dev, pl.ds(6 * lv + 3 * part + j, 8, stride=16), :] = packed[
                        3 * part + j, pl.ds(lv, 8, stride=2), :
                    ]
            back_ref[dev, pl.ds(12 + lv, 8, stride=16), :] = packed[6, pl.ds(lv, 8, stride=2), :]

        def start_block(to_level):
            block = back_ref.at[dev, pl.ds(pl.multiple_of(to_level * 16, 16), 14), :]
            send(block, out_ref.at[here, pl.ds(0, 14), :], back_sems, (dev, to_level)).start()

        for n in range(1, 8):
            start_block((my_level + n) % levels)

        @pl.when(dev != my_wave)
        def _():
            start_block(my_level)

    first = my_wave * blocks // devices

    @pl.loop(0, blocks)
    def _(turn):
        block = (turn + first) % blocks
        fourier_sums(block)
        low = jnp.where((turn == 0) & (block > 0), 3 * block + 1, 3 * block)
        high = jnp.where(block == blocks - 1, devices, 3 * block + 3)

        @pl.loop(low, high)
        def _(dev):
            send_back(dev)

        @pl.when((turn == blocks - 1) & (first > 0))
        def _():
            send_back(3 * first)

    own_rows = pl.ds(pl.multiple_of(my_level * 16, 16), 16)
    own = pltpu.make_async_copy(back_ref.at[my_wave, own_rows, :], out_ref.at[here], local_sems.at[1])
    own.start()

    for i in range(4):
        shift = (i * quarter) & (LANES - 1)
        before = jnp.zeros((32, LANES), F32)
        for tile in range(tiles + 1):
            at = slice(tile * LANES, (tile + 1) * LANES)
            rolled = pltpu.roll(segs[i, :, at], shift, 1) if tile < tiles else jnp.zeros((32, LANES), F32)
            turned[i, :, at] = jnp.where(lane < shift, before, rolled)
            before = rolled
    grid_copy = pltpu.make_async_copy(turned, segs_ref, local_sems.at[0])
    grid_copy.start()

    arrival.wait_send()
    landed = out_ref.at[pl.ds(0, everyone - 1), pl.ds(0, 14), :]
    arrival = send(landed, landed, back_sems, (my_wave, my_level))
    arrival.wait_recv()
    arrival.wait_send()
    own.wait()
    grid_copy.wait()


def lay_quarters(quarter, segs, acc, grid_ref):
    pad_len = grid_ref.shape[3]
    acc[...] = jnp.zeros_like(acc)
    for i in range(4):
        base = lax.shift_right_logical(i * quarter, 7)
        for tile in range(segs.shape[2] // LANES):
            at = pl.ds(pl.multiple_of((base + tile) * LANES, LANES), LANES)
            acc[:, at] += segs[i, :, tile * LANES : (tile + 1) * LANES]
    for f in range(2):
        grid_ref[0, f] = acc[16 * f : 16 * f + 16, :pad_len]


def direct_kernel(
    group, wave_ref, band_ref, len_ref, in_ref, segs_ref, leg_hbm, spec_hbm, grid_hbm,
    leg_ref, spec_ref, grid_ref, natural, turned, acc, load_sems, store_sems, grid_sem,
):
    pack = leg_ref.shape[2]
    slots = STEPS * group
    wave_pos = lax.axis_index("wave")
    loads = group_copies(group, (leg_hbm,), (leg_ref,), load_sems)
    stores = group_copies(group, (spec_ref,), (spec_hbm,), store_sems)
    for n in range(STEPS):
        loads(n)[0].start()

    @pl.loop(0, in_ref.shape[0], unroll=8)
    def _(i):
        natural[pl.ds(pl.multiple_of(band_ref[i] * 16, 16), 16), :] = in_ref[i]

    for lv in range(2):
        lines = [(3 * p + j, p, FLUX_ROWS[j]) for p in range(2) for j in range(3)]
        for line, part, units in [(6 * lv + n, p, u) for n, p, u in lines] + [(12 + lv, None, ())]:
            block = natural[pl.ds(line, LANES, stride=16), :].T
            placed = [(x, odd, part) for x, odd in units] or [(4, 1, 0), (4, 1, 1)]
            for n, (x, odd, p) in enumerate(placed):
                to = 4 * x + 2 * lv + p + (16 if x < 4 else 4) * odd + (16 if x == 4 else 0)
                turned[pl.ds(to, slots, stride=40), :] = block[n * slots : (n + 1) * slots]

    row = band_ref[wave_pos * lax.axis_size("level") + lax.axis_index("level")] & 63
    lay_quarters(lax.shift_right_logical(len_ref[row], 2), segs_ref, acc, grid_ref)
    grid_copy = pltpu.make_async_copy(grid_ref, grid_hbm, grid_sem)
    grid_copy.start()

    position = lax.broadcasted_iota(jnp.int32, (1, pack), 1)
    south = lax.broadcasted_iota(jnp.int32, (1, LANES), 1) >= 64

    @pl.loop(0, STEPS)
    def _(step):
        loads(step)[0].wait()
        for g in range(group):
            slot = step * group + g
            first_wave = wave_ref[wave_pos * slots + slot]
            boundary = (pack - 1) - first_wave

            x = turned[pl.ds(pl.multiple_of(slot * 40, 8), 40), :]
            other = pltpu.roll(x, 64, 1)
            difference = x - other
            y = jnp.concatenate([x + other, jnp.where(south, -difference, difference)], axis=0)
            left = jnp.concatenate(split(y), axis=0)
            right = jnp.concatenate(split(leg_ref[slot]), axis=0)
            both = dot(left, right, NN)
            both = both[:80] + both[80:]
            in_first = position < boundary
            parity = jnp.where(in_first, position, position + boundary) & 1
            in_even = in_first == ((first_wave & 1) == 0)
            chosen = jnp.where(parity == 0, both[:40], both[40:])
            main = jnp.where(in_even, chosen[:16], chosen[16:32])
            last = jnp.where(in_even, chosen[32:36], chosen[36:40])
            for n in range(8):
                spec_ref[slot, n // 2, n % 2] = main[2 * n : 2 * n + 2]
            for n in range(2):
                spec_ref[slot, 4, n] = last[2 * n : 2 * n + 2]
        stores(step)[0].start()

    for n in range(STEPS):
        stores(n)[0].wait()
    grid_copy.wait()


def shards(spec_in, legendre, gauss, wave_map, band_map, row_len):
    wave_devices = lax.axis_size("wave")
    devices = wave_devices * lax.axis_size("level")
    slots, _, _, _, pack = spec_in.shape
    waves = pack - 1
    lat_pairs = legendre.shape[1]
    pad_len = (20 + 4 * (waves - 1) + 127) // 128 * 128
    table_len = (pad_len // 4 + 127) // 128 * 128
    smem = pl.BlockSpec(memory_space=pltpu.SMEM)
    group = slots // STEPS

    vmem = pl.BlockSpec(memory_space=pltpu.VMEM)
    anywhere = pl.BlockSpec(memory_space=pl.ANY)
    half = waves // 2
    table = pltpu.VMEM((waves, table_len), BF16)
    segs, returned = pl.pallas_call(
        functools.partial(main_kernel, group),
        out_shape=(
            jax.ShapeDtypeStruct((4, 32, table_len + LANES), F32),
            jax.ShapeDtypeStruct((devices, 16, LANES), F32),
        ),
        in_specs=[
            smem,
            smem,
            smem,
            smem,
            vmem,
            anywhere,
            anywhere,
        ],
        out_specs=(anywhere, anywhere),
        scratch_shapes=[
            pltpu.VMEM((slots, 2, 2, 2, pack), F32),
            pltpu.VMEM((slots, lat_pairs, pack), F32),
            pltpu.VMEM((group, 8, pack), F32),
            pltpu.VMEM((slots * 32, LANES), F32),
            pltpu.VMEM((LANES * 8, LANES), F32),
            pltpu.VMEM((LANES, 8, LANES), F32),
            pltpu.VMEM((1, half), jnp.int32),
            pltpu.VMEM((half, LANES), F32),
            pltpu.VMEM((devices, 8, LANES), F32),
            pltpu.VMEM((wave_devices, 64, LANES), F32),
            pltpu.VMEM((4, 3, 16, LANES), F32),
            pltpu.VMEM((64, half), F32),
            pltpu.VMEM((64, half), F32),
            pltpu.VMEM((256, waves), BF16),
            pltpu.VMEM((256, waves), BF16),
            table,
            table,
            table,
            table,
            pltpu.VMEM((4, 32, table_len), F32),
            pltpu.VMEM((4, 32, table_len + LANES), F32),
            pltpu.VMEM((320, table_len), BF16),
            pltpu.VMEM((320, table_len), BF16),
            pltpu.VMEM((4, 80, half + LANES), F32),
            pltpu.VMEM((7, 16, LANES), F32),
            pltpu.VMEM((wave_devices, 128, LANES), F32),
            pltpu.SemaphoreType.DMA((2, STEPS)),
            pltpu.SemaphoreType.DMA((2,)),
            pltpu.SemaphoreType.DMA((2,)),
            pltpu.SemaphoreType.DMA((2,)),
        ],
        compiler_params=pltpu.CompilerParams(
            collective_id=0, has_side_effects=True, vmem_limit_bytes=56 * MIB
        ),
        name="rows",
    )(wave_map, band_map, row_len, gauss, wave_map[None, :], spec_in, legendre)

    spec_out, grid_out = pl.pallas_call(
        functools.partial(direct_kernel, group),
        out_shape=(
            jax.ShapeDtypeStruct((slots, 5, 2, 2, pack), F32),
            jax.ShapeDtypeStruct((1, 2, 16, pad_len), F32),
        ),
        in_specs=[
            smem,
            smem,
            smem,
            vmem,
            vmem,
            anywhere,
        ],
        out_specs=(anywhere, anywhere),
        scratch_shapes=[
            pltpu.VMEM((slots, lat_pairs, pack), F32),
            pltpu.VMEM((slots, 5, 2, 2, pack), F32),
            pltpu.VMEM((1, 2, 16, pad_len), F32),
            pltpu.VMEM((LANES * 16, LANES), F32),
            pltpu.VMEM((slots * 40, LANES), F32),
            pltpu.VMEM((32, 4 * table_len), F32),
            pltpu.SemaphoreType.DMA((1, STEPS)),
            pltpu.SemaphoreType.DMA((1, STEPS)),
            pltpu.SemaphoreType.DMA,
        ],
        compiler_params=pltpu.CompilerParams(vmem_limit_bytes=56 * MIB),
        name="direct",
    )(wave_map, band_map, row_len, returned, segs, legendre)
    return (grid_out, spec_out)


def solution(mesh):
    in_specs = (P("wave", None, "level", None, None), P("wave", None, None), P(), P(), P(), P())
    out_specs = (P(("wave", "level"), None, None, None), P("wave", None, "level", None, None))
    return jax.shard_map(shards, mesh=mesh, in_specs=in_specs, out_specs=out_specs, check_vma=False)
```

```python
import functools
import math

import jax
import jax.numpy as jnp
from jax import lax
from jax.experimental import pallas as pl
from jax.experimental.pallas import tpu as pltpu
from jax.sharding import PartitionSpec as P

F32 = jnp.float32
BF16 = jnp.bfloat16
LANES = 128
MIB = 1 << 20
STEPS = 10
SIN_TERMS = [(-1.0) ** i / math.factorial(2 * i + 1) for i in range(6)]
COS_TERMS = [(-1.0) ** i / math.factorial(2 * i) for i in range(7)]
MESH = pl.DeviceIdType.MESH
NT = (((1,), (1,)), ((), ()))
NN = (((1,), (0,)), ((), ()))
COEF_UNITS = [(f, part, odd) for f in range(2) for part in range(2) for odd in range(2)]
COEF_ROWS = [COEF_UNITS[i : i + 3] for i in range(0, 8, 3)]
FLUX_UNITS = [(x, odd) for x in range(5) for odd in range(2)]
FLUX_ROWS = [FLUX_UNITS[i : i + 3] for i in range(0, 9, 3)]


def dot(a, b, dims):
    return lax.dot_general(a, b, dims, preferred_element_type=F32)


def split(x):
    high = x.astype(BF16)
    return high, (x - high.astype(F32)).astype(BF16)


def horner(terms, x):
    total = jnp.full_like(x, terms[-1])
    for term in reversed(terms[:-1]):
        total = total * x + term
    return total


def turn_trig(steps, length, inverse):
    left = steps - jnp.floor(steps * inverse + 0.5) * length
    half = left * (inverse * math.pi)
    square = half * half
    sine = half * horner(SIN_TERMS, square)
    cosine = horner(COS_TERMS, square)
    return 1.0 - 2.0 * sine * sine, 2.0 * sine * cosine


def peer(k):
    mask = (k * 37) & 127
    return lax.axis_index("wave") ^ (mask >> 3), lax.axis_index("level") ^ (mask & 7)


def holder(place):
    return (place & 3) * 4 + ((place + (place >> 2)) & 3)


def send(source, target, sems, device):
    return pltpu.make_async_remote_copy(
        src_ref=source, dst_ref=target, send_sem=sems.at[0], recv_sem=sems.at[1], device_id=device, device_id_type=MESH
    )


def group_copies(group, sources, targets, sems):
    def copies(n):
        at = pl.ds(n * group, group)
        return [
            pltpu.make_async_copy(source.at[at], target.at[at], sems.at[i, n])
            for i, (source, target) in enumerate(zip(sources, targets))
        ]

    return copies


def inverse_step(step, group, wave_ref, spec_ref, leg_ref, flat, sums):
    slots = sums.shape[0] // 32
    pack = leg_ref.shape[2]
    wave_pos = lax.axis_index("wave")
    position = lax.broadcasted_iota(jnp.int32, (8, pack), 1)
    for g in range(group):
        slot = step * group + g
        first_wave = wave_ref[wave_pos * slots + slot]
        boundary = (pack - 1) - first_wave
        for pair in range(4):
            flat[g, 2 * pair : 2 * pair + 2, :] = spec_ref[slot, pair // 2, pair % 2]
        x = flat[g]
        in_first = position < boundary
        parity = jnp.where(in_first, position, position + boundary) & 1
        in_even = in_first == ((first_wave & 1) == 0)
        high = x.astype(BF16).astype(F32)
        parts = []
        for part in (high, x - high):
            signed = jnp.where(parity == 0, part, -part)
            for kept in (in_even, jnp.logical_not(in_even)):
                parts += [jnp.where(kept, part, 0.0), jnp.where(kept, signed, 0.0)]
        left = jnp.concatenate(parts, axis=0).astype(BF16)
        right = jnp.concatenate(split(leg_ref[slot]), axis=0)
        both = dot(left, right, NT)
        both = both[:32] + both[32:]
        sums[pl.ds(pl.multiple_of(slot * 32, 32), 32), :] = both + pltpu.roll(both, 64, 1)


def sort_rows(band_ref, sums, flat_rows, rows, out_ref):
    slots = sums.shape[0] // 32
    north = lax.broadcasted_iota(jnp.int32, (slots, LANES), 1) < 64

    def piece(f, lv, part, odd):
        at = 16 * odd + 4 * f + 2 * lv + part
        south_at = at + 8
        return jnp.where(
            north, sums[pl.ds(at, slots, stride=32), :], sums[pl.ds(south_at, slots, stride=32), :]
        )

    for lv in range(2):
        for j, units in enumerate(COEF_ROWS):
            pieces = [piece(f, lv, part, odd) for f, part, odd in units]
            pieces.append(jnp.zeros((LANES - len(units) * slots, LANES), F32))
            flat_rows[pl.ds(3 * lv + j, LANES, stride=8), :] = jnp.concatenate(pieces, axis=0).T

    @pl.loop(0, LANES, unroll=8)
    def _(i):
        rows[i] = flat_rows[pl.ds(pl.multiple_of(i * 8, 8), 8), :]

    @pl.loop(0, out_ref.shape[0], unroll=8)
    def _(i):
        out_ref[i] = rows[band_ref[i]]


def main_kernel(
    group, wave_ref, band_ref, len_ref, gauss_ref, map_hbm, spec_hbm, leg_hbm, segs_ref, out_ref, spec_ref, leg_ref,
    flat, sums, flat_rows, rows, map_ref, mapped, row_ref, col_ref, send_ref, in_ref, sorted_x, even_x, odd_x, even_l, odd_l,
    even_hi, even_lo, odd_hi, odd_lo, segs, turned, even_f, odd_f, back, packed, back_ref,
    map_sems, load_sems, sems, back_sems, local_sems,
):
    devices = send_ref.shape[0]
    barrier = pltpu.get_barrier_semaphore()
    copies = group_copies(group, (spec_hbm, leg_hbm), (spec_ref, leg_ref), load_sems)
    for n in range(STEPS):
        for copy in copies(n):
            copy.start()
    map_copies = [
        pltpu.make_async_copy(map_hbm.at[pl.ds(n * LANES, LANES)], map_ref.at[n], map_sems.at[n])
        for n in range(map_ref.shape[0])
    ]
    for copy in map_copies:
        copy.start()
    greeted = (devices - 1) // STEPS

    def greet(k):
        pl.semaphore_signal(barrier, inc=1, device_id=peer(k), device_id_type=MESH)

    @pl.loop(0, STEPS)
    def _(step):
        for copy in copies(step):
            copy.wait()
        for n in range(greeted):
            greet(step * greeted + n + 1)
        inverse_step(step, group, wave_ref, spec_ref, leg_ref, flat, sums)

    for k in range(STEPS * greeted + 1, devices):
        greet(k)
    sort_rows(band_ref, sums, flat_rows, rows, send_ref)
    for copy in map_copies:
        copy.wait()
    pl.semaphore_wait(barrier, devices - 1)
    row_part(
        band_ref, len_ref, gauss_ref, map_ref, mapped, row_ref, col_ref, segs_ref, out_ref, send_ref, in_ref, sorted_x,
        even_x, odd_x, even_l, odd_l, even_hi, even_lo, odd_hi, odd_lo, segs, turned, even_f, odd_f, back, packed,
        back_ref, sems, back_sems, local_sems,
    )


def row_part(
    band_ref, len_ref, gauss_ref, map_ref, mapped, row_ref, col_ref, segs_ref, out_ref, send_ref, in_ref, sorted_x,
    even_x, odd_x, even_l, odd_l, even_hi, even_lo, odd_hi, odd_lo, segs, turned, even_f, odd_f, back, packed,
    back_ref, sems, back_sems, local_sems,
):
    my_wave, my_level = lax.axis_index("wave"), lax.axis_index("level")
    levels = lax.axis_size("level")
    here = my_wave * levels + my_level
    row = band_ref[here] & 63
    length = len_ref[row]
    quarter = lax.shift_right_logical(length, 2)
    wave_top = 2 * row_ref.shape[1] - 1
    length_f = jnp.full((1, LANES), length.astype(F32))
    inverse = 1.0 / length_f
    half_waves = row_ref.shape[1]
    blocks = half_waves // LANES
    devices = in_ref.shape[0]
    everyone = devices * levels
    share = half_waves // devices
    tiles = even_hi.shape[1] // LANES
    lane = lax.broadcasted_iota(jnp.int32, (1, LANES), 1)

    for block in range(blocks):
        mapped[:, block * LANES : (block + 1) * LANES] = map_ref[block : block + 1, :]
    for place in range(devices):
        begin = holder(place) * share
        first = mapped[:, begin : begin + share]
        row_ref[:, place * share : (place + 1) * share] = jnp.where((first & 1) == 0, first, wave_top - first)
    for block in range(blocks):
        at = slice(block * LANES, (block + 1) * LANES)
        col_ref[at, :] = jnp.broadcast_to(row_ref[:, at].astype(F32), (LANES, LANES)).T

    def start_send(k):
        to_wave, to_level = peer(k)
        mine = in_ref.at[my_wave, pl.ds(pl.multiple_of(my_level * 8, 8), 6), :]
        send(send_ref.at[to_wave * levels + to_level, pl.ds(0, 6), :], mine, sems, (to_wave, to_level)).start()

    def make_tables(group):
        block, inner = group // 4, group % 4
        at_cos = pl.multiple_of(block * 256 + inner * 32, 32)
        at_sin = pl.multiple_of(block * 256 + LANES + inner * 32, 32)
        evens = col_ref[pl.ds(pl.multiple_of(group * 32, 32), 32), :]
        for waves, table_hi, table_lo in ((evens, even_hi, even_lo), (wave_top - evens, odd_hi, odd_lo)):
            cosine, sine = turn_trig(waves * lane.astype(F32), length_f, inverse)
            turn_cos, turn_sin = turn_trig(waves * float(LANES), length_f, inverse)
            for tile in range(tiles):
                at = slice(tile * LANES, (tile + 1) * LANES)
                high, low = split(cosine)
                table_hi[pl.ds(at_cos, 32), at] = high
                table_lo[pl.ds(at_cos, 32), at] = low
                high, low = split(sine)
                table_hi[pl.ds(at_sin, 32), at] = high
                table_lo[pl.ds(at_sin, 32), at] = low
                if tile < tiles - 1:
                    cosine, sine = (
                        cosine * turn_cos - sine * turn_sin,
                        sine * turn_cos + cosine * turn_sin,
                    )

    in_ref[my_wave, pl.ds(pl.multiple_of(my_level * 8, 8), 8), :] = send_ref[here]
    start_send(1)

    @pl.loop(0, 9)
    def _(group):
        for n in range(14):
            start_send(group * 14 + n + 2)
        make_tables(group)

    @pl.loop(9, half_waves // 32)
    def _(group):
        make_tables(group)

    landed = send_ref.at[pl.ds(0, everyone - 1), pl.ds(0, 6), :]
    arrival = send(landed, landed, sems, (my_wave, my_level))
    arrival.wait_recv()

    for dev in range(devices):
        at = slice(dev * share, (dev + 1) * share)
        for j, units in enumerate(COEF_ROWS):
            for lv in range(2):
                sorted_x[dev % 4, j, pl.ds(lv, 8, stride=2), :] = in_ref[holder(dev), pl.ds(3 * lv + j, 8, stride=8), :]
            for n, (f, part, odd) in enumerate(units):
                to = slice(32 * part + 16 * f, 32 * part + 16 * f + 16)
                x_ref = odd_x if odd else even_x
                x_ref[to, at] = sorted_x[dev % 4, j, :, n * share : (n + 1) * share]

    highest = jnp.minimum(wave_top, lax.shift_right_logical(length - 1, 1))
    for block in range(blocks):
        at = slice(block * LANES, (block + 1) * LANES)
        evens = row_ref[:, at]
        for odd, x_ref, l_ref in ((False, even_x, even_l), (True, odd_x, odd_l)):
            wave = wave_top - evens if odd else evens
            kept = (wave <= highest).astype(F32)
            weight = jnp.where(wave == 0, 1.0, 2.0) * kept
            slope_weight = weight * wave.astype(F32) / (wave_top + 1.0)
            real, imag = x_ref[0:32, at], x_ref[32:64, at]
            a = jnp.concatenate([real * weight, -imag * slope_weight], axis=0)
            b = jnp.concatenate([imag * weight, real * slope_weight], axis=0)
            flip = (1 - (wave & 2)).astype(F32)
            if odd:
                on_cos = jnp.concatenate([a, flip * b], axis=0)
                on_sin = jnp.concatenate([-b, flip * a], axis=0)
            else:
                on_cos = jnp.concatenate([a, flip * a], axis=0)
                on_sin = jnp.concatenate([-b, -flip * b], axis=0)
            for offset, value in ((0, on_cos), (LANES, on_sin)):
                to = slice(block * 256 + offset, block * 256 + offset + LANES)
                high, low = split(value)
                l_ref[0:128, to] = high
                l_ref[128:256, to] = low

    start = 0
    while start < tiles * LANES:
        width = min(256, tiles * LANES - start)
        at = slice(start, start + width)
        start += width
        halves = []
        for l_ref, table_hi, table_lo in ((even_l, even_hi, even_lo), (odd_l, odd_hi, odd_lo)):
            whole = dot(l_ref[...], table_hi[:, at], NN)
            halves.append(whole[:128] + whole[128:] + dot(l_ref[0:128, :], table_lo[:, at], NN))
        inside = (at.start + lax.broadcasted_iota(jnp.int32, (1, width), 1)) < quarter
        even, odd = (jnp.where(inside, half, 0.0) for half in halves)
        quarters = [even[:64] + odd[:64], even[64:] - odd[64:], even[:64] - odd[:64], even[64:] + odd[64:]]
        fluxes = []
        for i, values in enumerate(quarters):
            segs[i, :, at] = values[:32]
            u, v, su, sv = (values[16 * n : 16 * n + 16] for n in range(4))
            fluxes.append(jnp.concatenate([u * u, u * v, v * v, u * su, u * sv], axis=0))
        for f_ref, sign in ((even_f, 1.0), (odd_f, -1.0)):
            for n in range(2):
                value = fluxes[n] + fluxes[n + 2] if sign > 0 else fluxes[n] - fluxes[n + 2]
                high, low = split(value)
                f_ref[80 * n : 80 * n + 80, at] = high
                f_ref[160 + 80 * n : 240 + 80 * n, at] = low

    scale = gauss_ref[row] * inverse

    def fourier_sums(block):
        at = pl.ds(pl.multiple_of(block * LANES, LANES), LANES)
        rows = pl.ds(pl.multiple_of(block * 256, 256), 256)
        evens = row_ref[:, at]
        for odd, f_ref, table_hi, table_lo in ((0, even_f, even_hi, even_lo), (1, odd_f, odd_hi, odd_lo)):
            whole = dot(f_ref[...], table_hi[rows, :], NT)
            total = whole[:160] + whole[160:] + dot(f_ref[0:160, :], table_lo[rows, :], NT)
            waves = wave_top - evens if odd else evens
            kept = jnp.where(waves <= highest, scale, 0.0)
            flip = (1 - (waves & 2)).astype(F32)
            first_cos, first_sin = total[:80, :LANES], total[:80, LANES:]
            second_cos, second_sin = total[80:, :LANES] * flip, total[80:, LANES:] * flip
            if odd:
                back[2, :, at] = (first_cos - second_sin) * kept
                back[3, :, at] = -(first_sin + second_cos) * kept
            else:
                back[0, :, at] = (first_cos + second_cos) * kept
                back[1, :, at] = -(first_sin + second_sin) * kept

    def send_back(dev):
        begin = dev * share
        base = lax.shift_right_logical(begin, 7)
        offset = begin & (LANES - 1)
        tiles_at = [pl.ds(pl.multiple_of((base + n) * LANES, LANES), LANES) for n in range(2)]

        def unit(x, odd, part, place):
            low, high = (back[2 * odd + part, 16 * x : 16 * x + 16, at] for at in tiles_at)
            shift = (place * share - offset + LANES) & (LANES - 1)
            return pltpu.roll(jnp.where(lane < offset, high, low), shift, 1)

        def joined(units):
            value = units[0]
            for n, other in enumerate(units[1:]):
                value = jnp.where(lane < (n + 1) * share, value, other)
            return value

        for part in range(2):
            for j, units in enumerate(FLUX_ROWS):
                packed[3 * part + j] = joined([unit(x, odd, part, n) for n, (x, odd) in enumerate(units)])
        packed[6] = joined([unit(4, 1, part, part) for part in range(2)])
        for lv in range(2):
            for part in range(2):
                for j in range(3):
                    back_ref[dev, pl.ds(6 * lv + 3 * part + j, 8, stride=16), :] = packed[
                        3 * part + j, pl.ds(lv, 8, stride=2), :
                    ]
            back_ref[dev, pl.ds(12 + lv, 8, stride=16), :] = packed[6, pl.ds(lv, 8, stride=2), :]

        to_wave = holder(dev)

        def start_block(to_level):
            block = back_ref.at[dev, pl.ds(pl.multiple_of(to_level * 16, 16), 14), :]
            send(block, out_ref.at[here, pl.ds(0, 14), :], back_sems, (to_wave, to_level)).start()

        for n in range(1, 8):
            start_block(my_level ^ n)

        @pl.when(to_wave != my_wave)
        def _():
            start_block(my_level)

    first = my_wave * blocks // devices

    @pl.loop(0, blocks)
    def _(turn):
        block = (turn + first) % blocks
        fourier_sums(block)
        low = jnp.where((turn == 0) & (block > 0), 3 * block + 1, 3 * block)
        high = jnp.where(block == blocks - 1, devices, 3 * block + 3)

        @pl.loop(low, high)
        def _(dev):
            send_back(dev)

        @pl.when((turn == blocks - 1) & (first > 0))
        def _():
            send_back(3 * first)

    my_place = ((my_wave - (my_wave >> 2)) & 3) * 4 + (my_wave >> 2)
    own_rows = pl.ds(pl.multiple_of(my_level * 16, 16), 16)
    own = pltpu.make_async_copy(back_ref.at[my_place, own_rows, :], out_ref.at[here], local_sems.at[1])
    own.start()

    for i in range(4):
        shift = (i * quarter) & (LANES - 1)
        before = jnp.zeros((32, LANES), F32)
        for tile in range(tiles + 1):
            at = slice(tile * LANES, (tile + 1) * LANES)
            rolled = pltpu.roll(segs[i, :, at], shift, 1) if tile < tiles else jnp.zeros((32, LANES), F32)
            turned[i, :, at] = jnp.where(lane < shift, before, rolled)
            before = rolled
    grid_copy = pltpu.make_async_copy(turned, segs_ref, local_sems.at[0])
    grid_copy.start()

    arrival.wait_send()
    landed = out_ref.at[pl.ds(0, everyone - 1), pl.ds(0, 14), :]
    arrival = send(landed, landed, back_sems, (my_wave, my_level))
    arrival.wait_recv()
    arrival.wait_send()
    own.wait()
    grid_copy.wait()


def lay_quarters(quarter, segs, acc, grid_ref):
    pad_len = grid_ref.shape[3]
    acc[...] = jnp.zeros_like(acc)
    for i in range(4):
        base = lax.shift_right_logical(i * quarter, 7)
        for tile in range(segs.shape[2] // LANES):
            at = pl.ds(pl.multiple_of((base + tile) * LANES, LANES), LANES)
            acc[:, at] += segs[i, :, tile * LANES : (tile + 1) * LANES]
    for f in range(2):
        grid_ref[0, f] = acc[16 * f : 16 * f + 16, :pad_len]


def direct_kernel(
    group, wave_ref, band_ref, len_ref, in_ref, segs_ref, leg_hbm, spec_hbm, grid_hbm,
    leg_ref, spec_ref, grid_ref, natural, turned, acc, load_sems, store_sems, grid_sem,
):
    pack = leg_ref.shape[2]
    slots = STEPS * group
    wave_pos = lax.axis_index("wave")
    loads = group_copies(group, (leg_hbm,), (leg_ref,), load_sems)
    stores = group_copies(group, (spec_ref,), (spec_hbm,), store_sems)
    for n in range(STEPS):
        loads(n)[0].start()

    @pl.loop(0, in_ref.shape[0], unroll=8)
    def _(i):
        natural[pl.ds(pl.multiple_of(band_ref[i] * 16, 16), 16), :] = in_ref[i]

    for lv in range(2):
        lines = [(3 * p + j, p, FLUX_ROWS[j]) for p in range(2) for j in range(3)]
        for line, part, units in [(6 * lv + n, p, u) for n, p, u in lines] + [(12 + lv, None, ())]:
            block = natural[pl.ds(line, LANES, stride=16), :].T
            placed = [(x, odd, part) for x, odd in units] or [(4, 1, 0), (4, 1, 1)]
            for n, (x, odd, p) in enumerate(placed):
                to = 4 * x + 2 * lv + p + (16 if x < 4 else 4) * odd + (16 if x == 4 else 0)
                turned[pl.ds(to, slots, stride=40), :] = block[n * slots : (n + 1) * slots]

    row = band_ref[wave_pos * lax.axis_size("level") + lax.axis_index("level")] & 63
    lay_quarters(lax.shift_right_logical(len_ref[row], 2), segs_ref, acc, grid_ref)
    grid_copy = pltpu.make_async_copy(grid_ref, grid_hbm, grid_sem)
    grid_copy.start()

    position = lax.broadcasted_iota(jnp.int32, (1, pack), 1)
    south = lax.broadcasted_iota(jnp.int32, (1, LANES), 1) >= 64

    @pl.loop(0, STEPS)
    def _(step):
        loads(step)[0].wait()
        for g in range(group):
            slot = step * group + g
            first_wave = wave_ref[wave_pos * slots + slot]
            boundary = (pack - 1) - first_wave

            x = turned[pl.ds(pl.multiple_of(slot * 40, 8), 40), :]
            other = pltpu.roll(x, 64, 1)
            difference = x - other
            y = jnp.concatenate([x + other, jnp.where(south, -difference, difference)], axis=0)
            left = jnp.concatenate(split(y), axis=0)
            right = jnp.concatenate(split(leg_ref[slot]), axis=0)
            both = dot(left, right, NN)
            both = both[:80] + both[80:]
            in_first = position < boundary
            parity = jnp.where(in_first, position, position + boundary) & 1
            in_even = in_first == ((first_wave & 1) == 0)
            chosen = jnp.where(parity == 0, both[:40], both[40:])
            main = jnp.where(in_even, chosen[:16], chosen[16:32])
            last = jnp.where(in_even, chosen[32:36], chosen[36:40])
            for n in range(8):
                spec_ref[slot, n // 2, n % 2] = main[2 * n : 2 * n + 2]
            for n in range(2):
                spec_ref[slot, 4, n] = last[2 * n : 2 * n + 2]
        stores(step)[0].start()

    for n in range(STEPS):
        stores(n)[0].wait()
    grid_copy.wait()


def shards(spec_in, legendre, gauss, wave_map, band_map, row_len):
    wave_devices = lax.axis_size("wave")
    devices = wave_devices * lax.axis_size("level")
    slots, _, _, _, pack = spec_in.shape
    waves = pack - 1
    lat_pairs = legendre.shape[1]
    pad_len = (20 + 4 * (waves - 1) + 127) // 128 * 128
    table_len = (pad_len // 4 + 127) // 128 * 128
    smem = pl.BlockSpec(memory_space=pltpu.SMEM)
    group = slots // STEPS

    vmem = pl.BlockSpec(memory_space=pltpu.VMEM)
    anywhere = pl.BlockSpec(memory_space=pl.ANY)
    half = waves // 2
    table = pltpu.VMEM((waves, table_len), BF16)
    segs, returned = pl.pallas_call(
        functools.partial(main_kernel, group),
        out_shape=(
            jax.ShapeDtypeStruct((4, 32, table_len + LANES), F32),
            jax.ShapeDtypeStruct((devices, 16, LANES), F32),
        ),
        in_specs=[
            smem,
            smem,
            smem,
            smem,
            anywhere,
            anywhere,
            anywhere,
        ],
        out_specs=(anywhere, anywhere),
        scratch_shapes=[
            pltpu.VMEM((slots, 2, 2, 2, pack), F32),
            pltpu.VMEM((slots, lat_pairs, pack), F32),
            pltpu.VMEM((group, 8, pack), F32),
            pltpu.VMEM((slots * 32, LANES), F32),
            pltpu.VMEM((LANES * 8, LANES), F32),
            pltpu.VMEM((LANES, 8, LANES), F32),
            pltpu.VMEM((half // LANES, LANES), jnp.int32),
            pltpu.VMEM((1, half), jnp.int32),
            pltpu.VMEM((1, half), jnp.int32),
            pltpu.VMEM((half, LANES), F32),
            pltpu.VMEM((devices, 8, LANES), F32),
            pltpu.VMEM((wave_devices, 64, LANES), F32),
            pltpu.VMEM((4, 3, 16, LANES), F32),
            pltpu.VMEM((64, half), F32),
            pltpu.VMEM((64, half), F32),
            pltpu.VMEM((256, waves), BF16),
            pltpu.VMEM((256, waves), BF16),
            table,
            table,
            table,
            table,
            pltpu.VMEM((4, 32, table_len), F32),
            pltpu.VMEM((4, 32, table_len + LANES), F32),
            pltpu.VMEM((320, table_len), BF16),
            pltpu.VMEM((320, table_len), BF16),
            pltpu.VMEM((4, 80, half + LANES), F32),
            pltpu.VMEM((7, 16, LANES), F32),
            pltpu.VMEM((wave_devices, 128, LANES), F32),
            pltpu.SemaphoreType.DMA((half // LANES,)),
            pltpu.SemaphoreType.DMA((2, STEPS)),
            pltpu.SemaphoreType.DMA((2,)),
            pltpu.SemaphoreType.DMA((2,)),
            pltpu.SemaphoreType.DMA((2,)),
        ],
        compiler_params=pltpu.CompilerParams(
            collective_id=0, has_side_effects=True, vmem_limit_bytes=56 * MIB
        ),
        name="rows",
    )(wave_map, band_map, row_len, gauss, wave_map, spec_in, legendre)

    spec_out, grid_out = pl.pallas_call(
        functools.partial(direct_kernel, group),
        out_shape=(
            jax.ShapeDtypeStruct((slots, 5, 2, 2, pack), F32),
            jax.ShapeDtypeStruct((1, 2, 16, pad_len), F32),
        ),
        in_specs=[
            smem,
            smem,
            smem,
            vmem,
            vmem,
            anywhere,
        ],
        out_specs=(anywhere, anywhere),
        scratch_shapes=[
            pltpu.VMEM((slots, lat_pairs, pack), F32),
            pltpu.VMEM((slots, 5, 2, 2, pack), F32),
            pltpu.VMEM((1, 2, 16, pad_len), F32),
            pltpu.VMEM((LANES * 16, LANES), F32),
            pltpu.VMEM((slots * 40, LANES), F32),
            pltpu.VMEM((32, 4 * table_len), F32),
            pltpu.SemaphoreType.DMA((1, STEPS)),
            pltpu.SemaphoreType.DMA((1, STEPS)),
            pltpu.SemaphoreType.DMA,
        ],
        compiler_params=pltpu.CompilerParams(vmem_limit_bytes=56 * MIB),
        name="direct",
    )(wave_map, band_map, row_len, returned, segs, legendre)
    return (grid_out, spec_out)


def solution(mesh):
    in_specs = (P("wave", None, "level", None, None), P("wave", None, None), P(), P(), P(), P())
    out_specs = (P(("wave", "level"), None, None, None), P("wave", None, "level", None, None))
    return jax.shard_map(shards, mesh=mesh, in_specs=in_specs, out_specs=out_specs, check_vma=False)
```

```python
import functools
import math

import jax
import jax.numpy as jnp
from jax import lax
from jax.experimental import pallas as pl
from jax.experimental.pallas import tpu as pltpu
from jax.sharding import PartitionSpec as P

F32 = jnp.float32
BF16 = jnp.bfloat16
LANES = 128
MIB = 1 << 20
INVERSE_STEPS = 4
DIRECT_STEPS = 5
TOGETHER = 2
SIN_TERMS = [(-1.0) ** i / math.factorial(2 * i + 1) for i in range(6)]
COS_TERMS = [(-1.0) ** i / math.factorial(2 * i) for i in range(7)]
MESH = pl.DeviceIdType.MESH
NT = (((1,), (1,)), ((), ()))
NN = (((1,), (0,)), ((), ()))
COEF_UNITS = [(f, part, odd) for f in range(2) for part in range(2) for odd in range(2)]
COEF_ROWS = [COEF_UNITS[i : i + 3] for i in range(0, 8, 3)]
FLUX_UNITS = [(x, odd) for x in range(5) for odd in range(2)]
FLUX_ROWS = [FLUX_UNITS[i : i + 3] for i in range(0, 9, 3)]


def dot(a, b, dims):
    return lax.dot_general(a, b, dims, preferred_element_type=F32)


def split(x):
    high = x.astype(BF16)
    return high, (x - high.astype(F32)).astype(BF16)


def horner(terms, x):
    total = jnp.full_like(x, terms[-1])
    for term in reversed(terms[:-1]):
        total = total * x + term
    return total


def turn_trig(steps, length, inverse):
    left = steps - jnp.floor(steps * inverse + 0.5) * length
    half = left * (inverse * math.pi)
    square = half * half
    sine = half * horner(SIN_TERMS, square)
    cosine = horner(COS_TERMS, square)
    return 1.0 - 2.0 * sine * sine, 2.0 * sine * cosine


def peer(k):
    mask = (k * 37) & 127
    return lax.axis_index("wave") ^ (mask >> 3), lax.axis_index("level") ^ (mask & 7)


def holder(place):
    return (place & 3) * 4 + ((place + (place >> 2)) & 3)


def send(source, target, sems, device):
    return pltpu.make_async_remote_copy(
        src_ref=source, dst_ref=target, send_sem=sems.at[0], recv_sem=sems.at[1], device_id=device, device_id_type=MESH
    )


def chunks_of(pack):
    ends = list(range(256, pack - 255, 256)) + [pack]
    return list(zip([0] + ends[:-1], ends))


def group_copies(group, sources, targets, sems):
    def copies(n):
        at = pl.ds(n * group, group)
        return [
            pltpu.make_async_copy(source.at[at], target.at[at], sems.at[i, n])
            for i, (source, target) in enumerate(zip(sources, targets))
        ]

    return copies


def inverse_step(step, group, wave_ref, spec_ref, leg_ref, flat, sums):
    slots = sums.shape[0] // 32
    pack = leg_ref.shape[2]
    wave_pos = lax.axis_index("wave")
    for g in range(group):
        for pair in range(4):
            flat[g, 2 * pair : 2 * pair + 2, :] = spec_ref[step * group + g, pair // 2, pair % 2]
    results = []
    for g in range(0, group, TOGETHER):
        both = None
        for begin, end in chunks_of(pack):
            at = slice(begin, end)
            position = begin + lax.broadcasted_iota(jnp.int32, (8, end - begin), 1)
            parts, tables = [], []
            for n in range(g, g + TOGETHER):
                first_wave = wave_ref[wave_pos * slots + step * group + n]
                boundary = (pack - 1) - first_wave
                in_first = position < boundary
                parity = jnp.where(in_first, position, position + boundary) & 1
                in_even = in_first == ((first_wave & 1) == 0)
                x = flat[n, :, at]
                high = x.astype(BF16).astype(F32)
                for part in (high, x - high):
                    signed = jnp.where(parity == 0, part, -part)
                    for kept in (in_even, jnp.logical_not(in_even)):
                        parts += [jnp.where(kept, part, 0.0), jnp.where(kept, signed, 0.0)]
                tables += split(leg_ref[step * group + n, :, at])
            left = jnp.concatenate(parts, axis=0).astype(BF16)
            product = dot(left, jnp.concatenate(tables, axis=0), NT)
            both = product if both is None else both + product
        for n in range(TOGETHER):
            own = both[64 * n : 64 * n + 64, LANES * n : LANES * n + LANES]
            own = own[:32] + own[32:]
            results.append(own + pltpu.roll(own, 64, 1))
    sums[pl.ds(pl.multiple_of(step * (32 * group), 32), 32 * group), :] = jnp.concatenate(results, axis=0)


def sort_rows(band_ref, sums, flat_rows, rows, out_ref):
    slots = sums.shape[0] // 32
    north = lax.broadcasted_iota(jnp.int32, (slots, LANES), 1) < 64

    def piece(f, lv, part, odd):
        at = 16 * odd + 4 * f + 2 * lv + part
        south_at = at + 8
        return jnp.where(
            north, sums[pl.ds(at, slots, stride=32), :], sums[pl.ds(south_at, slots, stride=32), :]
        )

    for lv in range(2):
        for j, units in enumerate(COEF_ROWS):
            pieces = [piece(f, lv, part, odd) for f, part, odd in units]
            pieces.append(jnp.zeros((LANES - len(units) * slots, LANES), F32))
            flat_rows[pl.ds(3 * lv + j, LANES, stride=8), :] = jnp.concatenate(pieces, axis=0).T

    @pl.loop(0, LANES, unroll=8)
    def _(i):
        rows[i] = flat_rows[pl.ds(pl.multiple_of(i * 8, 8), 8), :]

    @pl.loop(0, out_ref.shape[0], unroll=8)
    def _(i):
        out_ref[i] = rows[band_ref[i]]


def main_kernel(
    group, wave_ref, band_ref, len_ref, gauss_ref, map_hbm, spec_hbm, leg_hbm, segs_ref, out_ref, spec_ref, leg_ref,
    flat, sums, flat_rows, rows, map_ref, mapped, row_ref, col_ref, send_ref, in_ref, sorted_x, even_x, odd_x, even_l, odd_l,
    even_hi, even_lo, odd_hi, odd_lo, segs, turned, even_f, odd_f, back, packed, back_ref,
    map_sems, load_sems, sems, back_sems, local_sems,
):
    devices = send_ref.shape[0]
    barrier = pltpu.get_barrier_semaphore()
    copies = group_copies(group, (spec_hbm, leg_hbm), (spec_ref, leg_ref), load_sems)
    for n in range(INVERSE_STEPS):
        for copy in copies(n):
            copy.start()
    map_copies = [
        pltpu.make_async_copy(map_hbm.at[pl.ds(n * LANES, LANES)], map_ref.at[n], map_sems.at[n])
        for n in range(map_ref.shape[0])
    ]
    for copy in map_copies:
        copy.start()

    def greet(k):
        pl.semaphore_signal(barrier, inc=1, device_id=peer(k), device_id_type=MESH)

    greet(1)

    @pl.loop(2, devices, unroll=14)
    def _(k):
        greet(k)

    @pl.loop(0, INVERSE_STEPS)
    def _(step):
        for copy in copies(step):
            copy.wait()
        inverse_step(step, group, wave_ref, spec_ref, leg_ref, flat, sums)

    sort_rows(band_ref, sums, flat_rows, rows, send_ref)
    for copy in map_copies:
        copy.wait()
    pl.semaphore_wait(barrier, devices - 1)
    row_part(
        band_ref, len_ref, gauss_ref, map_ref, mapped, row_ref, col_ref, segs_ref, out_ref, send_ref, in_ref, sorted_x,
        even_x, odd_x, even_l, odd_l, even_hi, even_lo, odd_hi, odd_lo, segs, turned, even_f, odd_f, back, packed,
        back_ref, sems, back_sems, local_sems,
    )


def row_part(
    band_ref, len_ref, gauss_ref, map_ref, mapped, row_ref, col_ref, segs_ref, out_ref, send_ref, in_ref, sorted_x,
    even_x, odd_x, even_l, odd_l, even_hi, even_lo, odd_hi, odd_lo, segs, turned, even_f, odd_f, back, packed,
    back_ref, sems, back_sems, local_sems,
):
    my_wave, my_level = lax.axis_index("wave"), lax.axis_index("level")
    levels = lax.axis_size("level")
    here = my_wave * levels + my_level
    row = band_ref[here] & 63
    length = len_ref[row]
    quarter = lax.shift_right_logical(length, 2)
    wave_top = 2 * row_ref.shape[1] - 1
    length_f = jnp.full((1, LANES), length.astype(F32))
    inverse = 1.0 / length_f
    half_waves = row_ref.shape[1]
    blocks = half_waves // LANES
    devices = in_ref.shape[0]
    everyone = devices * levels
    share = half_waves // devices
    tiles = even_hi.shape[1] // LANES
    lane = lax.broadcasted_iota(jnp.int32, (1, LANES), 1)

    for block in range(blocks):
        mapped[:, block * LANES : (block + 1) * LANES] = map_ref[block : block + 1, :]
    for place in range(devices):
        begin = holder(place) * share
        first = mapped[:, begin : begin + share]
        row_ref[:, place * share : (place + 1) * share] = jnp.where((first & 1) == 0, first, wave_top - first)
    for block in range(blocks):
        at = slice(block * LANES, (block + 1) * LANES)
        col_ref[at, :] = jnp.broadcast_to(row_ref[:, at].astype(F32), (LANES, LANES)).T

    def start_send(k):
        to_wave, to_level = peer(k)
        mine = in_ref.at[my_wave, pl.ds(pl.multiple_of(my_level * 8, 8), 6), :]
        send(send_ref.at[to_wave * levels + to_level, pl.ds(0, 6), :], mine, sems, (to_wave, to_level)).start()

    def make_tables(group):
        block, inner = group // 4, group % 4
        at_cos = pl.multiple_of(block * 256 + inner * 32, 32)
        at_sin = pl.multiple_of(block * 256 + LANES + inner * 32, 32)
        evens = col_ref[pl.ds(pl.multiple_of(group * 32, 32), 32), :]
        for waves, table_hi, table_lo in ((evens, even_hi, even_lo), (wave_top - evens, odd_hi, odd_lo)):
            cosine, sine = turn_trig(waves * lane.astype(F32), length_f, inverse)
            turn_cos, turn_sin = turn_trig(waves * float(LANES), length_f, inverse)
            for tile in range(tiles):
                at = slice(tile * LANES, (tile + 1) * LANES)
                high, low = split(cosine)
                table_hi[pl.ds(at_cos, 32), at] = high
                table_lo[pl.ds(at_cos, 32), at] = low
                high, low = split(sine)
                table_hi[pl.ds(at_sin, 32), at] = high
                table_lo[pl.ds(at_sin, 32), at] = low
                if tile < tiles - 1:
                    cosine, sine = (
                        cosine * turn_cos - sine * turn_sin,
                        sine * turn_cos + cosine * turn_sin,
                    )

    in_ref[my_wave, pl.ds(pl.multiple_of(my_level * 8, 8), 8), :] = send_ref[here]
    start_send(1)

    @pl.loop(0, 9)
    def _(group):
        for n in range(14):
            start_send(group * 14 + n + 2)
        make_tables(group)

    @pl.loop(9, half_waves // 32)
    def _(group):
        make_tables(group)

    landed = send_ref.at[pl.ds(0, everyone - 1), pl.ds(0, 6), :]
    arrival = send(landed, landed, sems, (my_wave, my_level))
    arrival.wait_recv()

    for dev in range(devices):
        at = slice(dev * share, (dev + 1) * share)
        for j, units in enumerate(COEF_ROWS):
            for lv in range(2):
                sorted_x[dev % 4, j, pl.ds(lv, 8, stride=2), :] = in_ref[holder(dev), pl.ds(3 * lv + j, 8, stride=8), :]
            for n, (f, part, odd) in enumerate(units):
                to = slice(32 * part + 16 * f, 32 * part + 16 * f + 16)
                x_ref = odd_x if odd else even_x
                x_ref[to, at] = sorted_x[dev % 4, j, :, n * share : (n + 1) * share]

    highest = jnp.minimum(wave_top, lax.shift_right_logical(length - 1, 1))
    @pl.loop(0, blocks)
    def _(block):
        at = pl.ds(pl.multiple_of(block * LANES, LANES), LANES)
        evens = row_ref[:, at]
        for odd, x_ref, l_ref in ((False, even_x, even_l), (True, odd_x, odd_l)):
            wave = wave_top - evens if odd else evens
            kept = (wave <= highest).astype(F32)
            weight = jnp.where(wave == 0, 1.0, 2.0) * kept
            slope_weight = weight * wave.astype(F32) / (wave_top + 1.0)
            real, imag = x_ref[0:32, at], x_ref[32:64, at]
            a = jnp.concatenate([real * weight, -imag * slope_weight], axis=0)
            b = jnp.concatenate([imag * weight, real * slope_weight], axis=0)
            flip = (1 - (wave & 2)).astype(F32)
            if odd:
                on_cos = jnp.concatenate([a, flip * b], axis=0)
                on_sin = jnp.concatenate([-b, flip * a], axis=0)
            else:
                on_cos = jnp.concatenate([a, flip * a], axis=0)
                on_sin = jnp.concatenate([-b, -flip * b], axis=0)
            for offset, value in ((0, on_cos), (LANES, on_sin)):
                to = pl.ds(pl.multiple_of(block * 256 + offset, LANES), LANES)
                high, low = split(value)
                l_ref[0:128, to] = high
                l_ref[128:256, to] = low

    def grid_values(start, width):
        at = pl.ds(pl.multiple_of(start, LANES), width)
        halves = []
        for l_ref, table_hi, table_lo in ((even_l, even_hi, even_lo), (odd_l, odd_hi, odd_lo)):
            whole = dot(l_ref[...], table_hi[:, at], NN)
            halves.append(whole[:128] + whole[128:] + dot(l_ref[0:128, :], table_lo[:, at], NN))
        inside = (start + lax.broadcasted_iota(jnp.int32, (1, width), 1)) < quarter
        even, odd = (jnp.where(inside, half, 0.0) for half in halves)
        quarters = [even[:64] + odd[:64], even[64:] - odd[64:], even[:64] - odd[:64], even[64:] + odd[64:]]
        fluxes = []
        for i, values in enumerate(quarters):
            segs[i, :, at] = values[:32]
            u, v, su, sv = (values[16 * n : 16 * n + 16] for n in range(4))
            fluxes.append(jnp.concatenate([u * u, u * v, v * v, u * su, u * sv], axis=0))
        for f_ref, sign in ((even_f, 1.0), (odd_f, -1.0)):
            for n in range(2):
                value = fluxes[n] + fluxes[n + 2] if sign > 0 else fluxes[n] - fluxes[n + 2]
                high, low = split(value)
                f_ref[80 * n : 80 * n + 80, at] = high
                f_ref[160 + 80 * n : 240 + 80 * n, at] = low

    @pl.loop(0, tiles // 2)
    def _(pair):
        grid_values(pair * 256, 256)

    if tiles % 2:
        grid_values((tiles - 1) * LANES, LANES)

    scale = gauss_ref[row] * inverse

    def fourier_sums(block):
        at = pl.ds(pl.multiple_of(block * LANES, LANES), LANES)
        rows = pl.ds(pl.multiple_of(block * 256, 256), 256)
        evens = row_ref[:, at]
        for odd, f_ref, table_hi, table_lo in ((0, even_f, even_hi, even_lo), (1, odd_f, odd_hi, odd_lo)):
            whole = dot(f_ref[...], table_hi[rows, :], NT)
            total = whole[:160] + whole[160:] + dot(f_ref[0:160, :], table_lo[rows, :], NT)
            waves = wave_top - evens if odd else evens
            kept = jnp.where(waves <= highest, scale, 0.0)
            flip = (1 - (waves & 2)).astype(F32)
            first_cos, first_sin = total[:80, :LANES], total[:80, LANES:]
            second_cos, second_sin = total[80:, :LANES] * flip, total[80:, LANES:] * flip
            if odd:
                back[2, :, at] = (first_cos - second_sin) * kept
                back[3, :, at] = -(first_sin + second_cos) * kept
            else:
                back[0, :, at] = (first_cos + second_cos) * kept
                back[1, :, at] = -(first_sin + second_sin) * kept

    def send_back(dev):
        begin = dev * share
        base = lax.shift_right_logical(begin, 7)
        offset = begin & (LANES - 1)
        tiles_at = [pl.ds(pl.multiple_of((base + n) * LANES, LANES), LANES) for n in range(2)]

        def unit(x, odd, part, place):
            low, high = (back[2 * odd + part, 16 * x : 16 * x + 16, at] for at in tiles_at)
            shift = (place * share - offset + LANES) & (LANES - 1)
            return pltpu.roll(jnp.where(lane < offset, high, low), shift, 1)

        def joined(units):
            value = units[0]
            for n, other in enumerate(units[1:]):
                value = jnp.where(lane < (n + 1) * share, value, other)
            return value

        for part in range(2):
            for j, units in enumerate(FLUX_ROWS):
                packed[3 * part + j] = joined([unit(x, odd, part, n) for n, (x, odd) in enumerate(units)])
        packed[6] = joined([unit(4, 1, part, part) for part in range(2)])
        for lv in range(2):
            for part in range(2):
                for j in range(3):
                    back_ref[dev, pl.ds(6 * lv + 3 * part + j, 8, stride=16), :] = packed[
                        3 * part + j, pl.ds(lv, 8, stride=2), :
                    ]
            back_ref[dev, pl.ds(12 + lv, 8, stride=16), :] = packed[6, pl.ds(lv, 8, stride=2), :]

        to_wave = holder(dev)

        def start_block(to_level):
            block = back_ref.at[dev, pl.ds(pl.multiple_of(to_level * 16, 16), 14), :]
            send(block, out_ref.at[here, pl.ds(0, 14), :], back_sems, (to_wave, to_level)).start()

        for n in range(1, 8):
            start_block(my_level ^ n)

        @pl.when(to_wave != my_wave)
        def _():
            start_block(my_level)

    first = my_wave * blocks // devices

    @pl.loop(0, blocks)
    def _(turn):
        block = (turn + first) % blocks
        fourier_sums(block)
        low = jnp.where((turn == 0) & (block > 0), 3 * block + 1, 3 * block)
        high = jnp.where(block == blocks - 1, devices, 3 * block + 3)

        extra = jnp.where((turn == blocks - 1) & (first > 0), 1, 0)

        @pl.loop(low, high + extra)
        def _(n):
            send_back(jnp.where(n == high, 3 * first, n))

    my_place = ((my_wave - (my_wave >> 2)) & 3) * 4 + (my_wave >> 2)
    own_rows = pl.ds(pl.multiple_of(my_level * 16, 16), 16)
    own = pltpu.make_async_copy(back_ref.at[my_place, own_rows, :], out_ref.at[here], local_sems.at[1])
    own.start()

    @pl.loop(0, 4)
    def _(i):
        shift = (i * quarter) & (LANES - 1)
        before = jnp.zeros((32, LANES), F32)
        for tile in range(tiles + 1):
            at = slice(tile * LANES, (tile + 1) * LANES)
            rolled = pltpu.roll(segs[i, :, at], shift, 1) if tile < tiles else jnp.zeros((32, LANES), F32)
            turned[i, :, at] = jnp.where(lane < shift, before, rolled)
            before = rolled

    grid_copy = pltpu.make_async_copy(turned, segs_ref, local_sems.at[0])
    grid_copy.start()

    arrival.wait_send()
    landed = out_ref.at[pl.ds(0, everyone - 1), pl.ds(0, 14), :]
    arrival = send(landed, landed, back_sems, (my_wave, my_level))
    arrival.wait_recv()
    arrival.wait_send()
    own.wait()
    grid_copy.wait()


def lay_quarters(quarter, segs, acc, grid_ref):
    pad_len = grid_ref.shape[3]
    acc[...] = jnp.zeros_like(acc)
    for i in range(4):
        base = lax.shift_right_logical(i * quarter, 7)
        for tile in range(segs.shape[2] // LANES):
            at = pl.ds(pl.multiple_of((base + tile) * LANES, LANES), LANES)
            acc[:, at] += segs[i, :, tile * LANES : (tile + 1) * LANES]
    for f in range(2):
        grid_ref[0, f] = acc[16 * f : 16 * f + 16, :pad_len]


def direct_kernel(
    group, wave_ref, band_ref, len_ref, in_ref, segs_ref, leg_hbm, spec_hbm, grid_hbm,
    leg_ref, spec_ref, grid_ref, natural, turned, acc, load_sems, store_sems, grid_sem,
):
    pack = leg_ref.shape[2]
    slots = DIRECT_STEPS * group
    wave_pos = lax.axis_index("wave")
    loads = group_copies(group, (leg_hbm,), (leg_ref,), load_sems)
    stores = group_copies(group, (spec_ref,), (spec_hbm,), store_sems)
    for n in range(DIRECT_STEPS):
        loads(n)[0].start()

    @pl.loop(0, in_ref.shape[0], unroll=8)
    def _(i):
        natural[pl.ds(pl.multiple_of(band_ref[i] * 16, 16), 16), :] = in_ref[i]

    for lv in range(2):
        lines = [(3 * p + j, p, FLUX_ROWS[j]) for p in range(2) for j in range(3)]
        for line, part, units in [(6 * lv + n, p, u) for n, p, u in lines] + [(12 + lv, None, ())]:
            block = natural[pl.ds(line, LANES, stride=16), :].T
            placed = [(x, odd, part) for x, odd in units] or [(4, 1, 0), (4, 1, 1)]
            for n, (x, odd, p) in enumerate(placed):
                to = 4 * x + 2 * lv + p + 24 * odd
                turned[pl.ds(to, slots, stride=48), :] = block[n * slots : (n + 1) * slots]

    row = band_ref[wave_pos * lax.axis_size("level") + lax.axis_index("level")] & 63
    lay_quarters(lax.shift_right_logical(len_ref[row], 2), segs_ref, acc, grid_ref)
    grid_copy = pltpu.make_async_copy(grid_ref, grid_hbm, grid_sem)
    grid_copy.start()

    south = lax.broadcasted_iota(jnp.int32, (1, LANES), 1) >= 64

    def both_parities(x):
        other = pltpu.roll(x, 64, 1)
        difference = x - other
        y = jnp.concatenate([x + other, jnp.where(south, -difference, difference)], axis=0)
        return jnp.concatenate(split(y), axis=0)

    def store_chunk(both, slot, boundary, begin, end):
        position = begin + lax.broadcasted_iota(jnp.int32, (1, end - begin), 1)
        rows = both.shape[0] // 2
        both = both[:rows] + both[rows:]
        if end <= pack // 2:
            chosen = jnp.where((position & 1) == 0, both[:24], both[24:])
            main, last = chosen[:16], chosen[16:20]
        else:
            in_first = position < boundary
            parity = jnp.where(in_first, position, position + boundary) & 1
            chosen = jnp.where(parity == 0, both[:40], both[40:])
            main = jnp.where(in_first, chosen[:16], chosen[16:32])
            last = jnp.where(in_first, chosen[32:36], chosen[36:40])
        for n in range(10):
            value = main[2 * n : 2 * n + 2] if n < 8 else last[2 * n - 16 : 2 * n - 14]
            spec_ref[slot, n // 2, n % 2, :, begin:end] = value

    @pl.loop(0, DIRECT_STEPS)
    def _(step):
        loads(step)[0].wait()
        stored = None
        for g in range(group):
            slot = step * group + g
            first_wave = wave_ref[wave_pos * slots + slot]
            boundary = (pack - 1) - first_wave
            first_at = slot * 48 + (first_wave & 1) * 24
            x = turned[pl.ds(pl.multiple_of(first_at, 8), 24), :]
            second_x = turned[pl.ds(pl.multiple_of(slot * 96 + 24 - first_at, 8), 24), :]
            last = jnp.concatenate([x[16:20], second_x[16:20]], axis=0)
            first_left = both_parities(x)
            left = both_parities(jnp.concatenate([x[:16], second_x[:16], last], axis=0))
            for begin, end in chunks_of(pack):
                at = slice(begin, end)
                right = jnp.concatenate(split(leg_ref[slot, :, at]), axis=0)
                both = dot(first_left if end <= pack // 2 else left, right, NN)
                if stored is not None:
                    store_chunk(*stored)
                stored = (both, slot, boundary, begin, end)
        store_chunk(*stored)
        stores(step)[0].start()

    for n in range(DIRECT_STEPS):
        stores(n)[0].wait()
    grid_copy.wait()


def shards(spec_in, legendre, gauss, wave_map, band_map, row_len):
    wave_devices = lax.axis_size("wave")
    devices = wave_devices * lax.axis_size("level")
    slots, _, _, _, pack = spec_in.shape
    waves = pack - 1
    lat_pairs = legendre.shape[1]
    pad_len = (20 + 4 * (waves - 1) + 127) // 128 * 128
    table_len = (pad_len // 4 + 127) // 128 * 128
    smem = pl.BlockSpec(memory_space=pltpu.SMEM)
    group = slots // INVERSE_STEPS

    vmem = pl.BlockSpec(memory_space=pltpu.VMEM)
    anywhere = pl.BlockSpec(memory_space=pl.ANY)
    half = waves // 2
    table = pltpu.VMEM((waves, table_len), BF16)
    segs, returned = pl.pallas_call(
        functools.partial(main_kernel, group),
        out_shape=(
            jax.ShapeDtypeStruct((4, 32, table_len + LANES), F32),
            jax.ShapeDtypeStruct((devices, 16, LANES), F32),
        ),
        in_specs=[
            smem,
            smem,
            smem,
            smem,
            anywhere,
            anywhere,
            anywhere,
        ],
        out_specs=(anywhere, anywhere),
        scratch_shapes=[
            pltpu.VMEM((slots, 2, 2, 2, pack), F32),
            pltpu.VMEM((slots, lat_pairs, pack), F32),
            pltpu.VMEM((group, 8, pack), F32),
            pltpu.VMEM((slots * 32, LANES), F32),
            pltpu.VMEM((LANES * 8, LANES), F32),
            pltpu.VMEM((LANES, 8, LANES), F32),
            pltpu.VMEM((half // LANES, LANES), jnp.int32),
            pltpu.VMEM((1, half), jnp.int32),
            pltpu.VMEM((1, half), jnp.int32),
            pltpu.VMEM((half, LANES), F32),
            pltpu.VMEM((devices, 8, LANES), F32),
            pltpu.VMEM((wave_devices, 64, LANES), F32),
            pltpu.VMEM((4, 3, 16, LANES), F32),
            pltpu.VMEM((64, half), F32),
            pltpu.VMEM((64, half), F32),
            pltpu.VMEM((256, waves), BF16),
            pltpu.VMEM((256, waves), BF16),
            table,
            table,
            table,
            table,
            pltpu.VMEM((4, 32, table_len), F32),
            pltpu.VMEM((4, 32, table_len + LANES), F32),
            pltpu.VMEM((320, table_len), BF16),
            pltpu.VMEM((320, table_len), BF16),
            pltpu.VMEM((4, 80, half + LANES), F32),
            pltpu.VMEM((7, 16, LANES), F32),
            pltpu.VMEM((wave_devices, 128, LANES), F32),
            pltpu.SemaphoreType.DMA((half // LANES,)),
            pltpu.SemaphoreType.DMA((2, INVERSE_STEPS)),
            pltpu.SemaphoreType.DMA((2,)),
            pltpu.SemaphoreType.DMA((2,)),
            pltpu.SemaphoreType.DMA((2,)),
        ],
        compiler_params=pltpu.CompilerParams(
            collective_id=0, has_side_effects=True, vmem_limit_bytes=56 * MIB
        ),
        name="rows",
    )(wave_map, band_map, row_len, gauss, wave_map, spec_in, legendre)

    spec_out, grid_out = pl.pallas_call(
        functools.partial(direct_kernel, slots // DIRECT_STEPS),
        out_shape=(
            jax.ShapeDtypeStruct((slots, 5, 2, 2, pack), F32),
            jax.ShapeDtypeStruct((1, 2, 16, pad_len), F32),
        ),
        in_specs=[
            smem,
            smem,
            smem,
            vmem,
            vmem,
            anywhere,
        ],
        out_specs=(anywhere, anywhere),
        scratch_shapes=[
            pltpu.VMEM((slots, lat_pairs, pack), F32),
            pltpu.VMEM((slots, 5, 2, 2, pack), F32),
            pltpu.VMEM((1, 2, 16, pad_len), F32),
            pltpu.VMEM((LANES * 16, LANES), F32),
            pltpu.VMEM((slots * 48, LANES), F32),
            pltpu.VMEM((32, 4 * table_len), F32),
            pltpu.SemaphoreType.DMA((1, DIRECT_STEPS)),
            pltpu.SemaphoreType.DMA((1, DIRECT_STEPS)),
            pltpu.SemaphoreType.DMA,
        ],
        compiler_params=pltpu.CompilerParams(vmem_limit_bytes=56 * MIB),
        name="direct",
    )(wave_map, band_map, row_len, returned, segs, legendre)
    return (grid_out, spec_out)


def solution(mesh):
    in_specs = (P("wave", None, "level", None, None), P("wave", None, None), P(), P(), P(), P())
    out_specs = (P(("wave", "level"), None, None, None), P("wave", None, "level", None, None))
    return jax.shard_map(shards, mesh=mesh, in_specs=in_specs, out_specs=out_specs, check_vma=False)
```

```python
import functools
import math

import jax
import jax.numpy as jnp
from jax import lax
from jax.experimental import pallas as pl
from jax.experimental.pallas import tpu as pltpu
from jax.sharding import PartitionSpec as P

F32 = jnp.float32
BF16 = jnp.bfloat16
LANES = 128
MIB = 1 << 20
INVERSE_STEPS = 4
DIRECT_STEPS = 5
AHEAD = 2
TOGETHER = 2
SIN_TERMS = [(-1.0) ** i / math.factorial(2 * i + 1) for i in range(6)]
COS_TERMS = [(-1.0) ** i / math.factorial(2 * i) for i in range(7)]
MESH = pl.DeviceIdType.MESH
NT = (((1,), (1,)), ((), ()))
NN = (((1,), (0,)), ((), ()))
COEF_UNITS = [(f, part, odd) for f in range(2) for part in range(2) for odd in range(2)]
COEF_ROWS = [COEF_UNITS[i : i + 3] for i in range(0, 8, 3)]
FLUX_UNITS = [(x, odd) for x in range(5) for odd in range(2)]
FLUX_ROWS = [FLUX_UNITS[i : i + 3] for i in range(0, 9, 3)]


def dot(a, b, dims):
    return lax.dot_general(a, b, dims, preferred_element_type=F32)


def split(x):
    high = x.astype(BF16)
    return high, (x - high.astype(F32)).astype(BF16)


def horner(terms, x):
    total = jnp.full_like(x, terms[-1])
    for term in reversed(terms[:-1]):
        total = total * x + term
    return total


def turn_trig(steps, length, inverse):
    left = steps - jnp.floor(steps * inverse + 0.5) * length
    half = left * (inverse * math.pi)
    square = half * half
    sine = half * horner(SIN_TERMS, square)
    cosine = horner(COS_TERMS, square)
    return 1.0 - 2.0 * sine * sine, 2.0 * sine * cosine


def peer(k):
    mask = (k * 37) & 127
    return lax.axis_index("wave") ^ (mask >> 3), lax.axis_index("level") ^ (mask & 7)


def holder(place):
    return (place & 3) * 4 + ((place + (place >> 2)) & 3)


def send(source, target, sems, device):
    return pltpu.make_async_remote_copy(
        src_ref=source, dst_ref=target, send_sem=sems.at[0], recv_sem=sems.at[1], device_id=device, device_id_type=MESH
    )


def chunks_of(pack):
    ends = list(range(256, pack - 255, 256)) + [pack]
    return list(zip([0] + ends[:-1], ends))


def group_copies(group, sources, targets, sems):
    def copies(n):
        at = pl.ds(n * group, group)
        return [
            pltpu.make_async_copy(source.at[at], target.at[at], sems.at[i, n])
            for i, (source, target) in enumerate(zip(sources, targets))
        ]

    return copies


def small_copies(sources, targets, sems):
    return [
        pltpu.make_async_copy(source, target, sems.at[i])
        for i, (source, target) in enumerate(zip(sources, targets))
    ]


def inverse_step(step, group, wave_ref, spec_ref, leg_ref, flat, sums):
    slots = sums.shape[0] // 32
    pack = leg_ref.shape[2]
    wave_pos = lax.axis_index("wave")
    for g in range(group):
        for pair in range(4):
            flat[g, 2 * pair : 2 * pair + 2, :] = spec_ref[step * group + g, pair // 2, pair % 2]
    results = []
    for g in range(0, group, TOGETHER):
        both = None
        for begin, end in chunks_of(pack):
            at = slice(begin, end)
            position = begin + lax.broadcasted_iota(jnp.int32, (8, end - begin), 1)
            parts, tables = [], []
            for n in range(g, g + TOGETHER):
                first_wave = wave_ref[wave_pos * slots + step * group + n]
                boundary = (pack - 1) - first_wave
                in_first = position < boundary
                parity = jnp.where(in_first, position, position + boundary) & 1
                in_even = in_first == ((first_wave & 1) == 0)
                x = flat[n, :, at]
                high = x.astype(BF16).astype(F32)
                for part in (high, x - high):
                    signed = jnp.where(parity == 0, part, -part)
                    for kept in (in_even, jnp.logical_not(in_even)):
                        parts += [jnp.where(kept, part, 0.0), jnp.where(kept, signed, 0.0)]
                tables += split(leg_ref[step * group + n, :, at])
            left = jnp.concatenate(parts, axis=0).astype(BF16)
            product = dot(left, jnp.concatenate(tables, axis=0), NT)
            both = product if both is None else both + product
        for n in range(TOGETHER):
            own = both[64 * n : 64 * n + 64, LANES * n : LANES * n + LANES]
            own = own[:32] + own[32:]
            results.append(own + pltpu.roll(own, 64, 1))
    sums[pl.ds(pl.multiple_of(step * (32 * group), 32), 32 * group), :] = jnp.concatenate(results, axis=0)


def sort_rows(band_ref, sums, flat_rows, rows, out_ref):
    slots = sums.shape[0] // 32
    north = lax.broadcasted_iota(jnp.int32, (slots, LANES), 1) < 64

    def piece(f, lv, part, odd):
        at = 16 * odd + 4 * f + 2 * lv + part
        south_at = at + 8
        return jnp.where(
            north, sums[pl.ds(at, slots, stride=32), :], sums[pl.ds(south_at, slots, stride=32), :]
        )

    for lv in range(2):
        for j, units in enumerate(COEF_ROWS):
            pieces = [piece(f, lv, part, odd) for f, part, odd in units]
            pieces.append(jnp.zeros((LANES - len(units) * slots, LANES), F32))
            flat_rows[pl.ds(3 * lv + j, LANES, stride=8), :] = jnp.concatenate(pieces, axis=0).T

    @pl.loop(0, LANES, unroll=8)
    def _(i):
        rows[i] = flat_rows[pl.ds(pl.multiple_of(i * 8, 8), 8), :]

    @pl.loop(0, out_ref.shape[0], unroll=8)
    def _(i):
        out_ref[i] = rows[band_ref[i]]


def main_kernel(
    group, wave_hbm, band_hbm, len_hbm, gauss_hbm, spec_hbm, leg_hbm, segs_ref, out_ref,
    wave_ref, band_ref, len_ref, gauss_ref, spec_ref, leg_ref,
    flat, sums, flat_rows, rows, map_ref, mapped, row_ref, col_ref, send_ref, in_ref, sorted_x, even_x, odd_x, even_l, odd_l,
    even_hi, even_lo, odd_hi, odd_lo, segs, turned, even_f, odd_f, back, packed, back_ref,
    small_sems, map_sems, load_sems, sems, back_sems, local_sems,
):
    devices = send_ref.shape[0]
    barrier = pltpu.get_barrier_semaphore()
    copies = group_copies(group, (spec_hbm, leg_hbm), (spec_ref, leg_ref), load_sems)
    for n in range(INVERSE_STEPS):
        for copy in copies(n):
            copy.start()
    map_copies = [
        pltpu.make_async_copy(wave_hbm.at[pl.ds(n * LANES, LANES)], map_ref.at[n], map_sems.at[n])
        for n in range(map_ref.shape[0])
    ]
    small = small_copies(
        (wave_hbm, band_hbm, len_hbm, gauss_hbm), (wave_ref, band_ref, len_ref, gauss_ref), small_sems
    )
    for copy in map_copies + small:
        copy.start()

    def greet(k):
        pl.semaphore_signal(barrier, inc=1, device_id=peer(k), device_id_type=MESH)

    greet(1)

    @pl.loop(2, devices, unroll=14)
    def _(k):
        greet(k)

    for copy in small:
        copy.wait()

    @pl.loop(0, INVERSE_STEPS)
    def _(step):
        for copy in copies(step):
            copy.wait()
        inverse_step(step, group, wave_ref, spec_ref, leg_ref, flat, sums)

    sort_rows(band_ref, sums, flat_rows, rows, send_ref)
    for copy in map_copies:
        copy.wait()
    pl.semaphore_wait(barrier, devices - 1)
    row_part(
        band_ref, len_ref, gauss_ref, map_ref, mapped, row_ref, col_ref, segs_ref, out_ref, send_ref, in_ref, sorted_x,
        even_x, odd_x, even_l, odd_l, even_hi, even_lo, odd_hi, odd_lo, segs, turned, even_f, odd_f, back, packed,
        back_ref, sems, back_sems, local_sems,
    )


def row_part(
    band_ref, len_ref, gauss_ref, map_ref, mapped, row_ref, col_ref, segs_ref, out_ref, send_ref, in_ref, sorted_x,
    even_x, odd_x, even_l, odd_l, even_hi, even_lo, odd_hi, odd_lo, segs, turned, even_f, odd_f, back, packed,
    back_ref, sems, back_sems, local_sems,
):
    my_wave, my_level = lax.axis_index("wave"), lax.axis_index("level")
    levels = lax.axis_size("level")
    here = my_wave * levels + my_level
    row = band_ref[here] & 63
    length = len_ref[row]
    quarter = lax.shift_right_logical(length, 2)
    wave_top = 2 * row_ref.shape[1] - 1
    length_f = jnp.full((1, LANES), length.astype(F32))
    inverse = 1.0 / length_f
    half_waves = row_ref.shape[1]
    blocks = half_waves // LANES
    devices = in_ref.shape[0]
    everyone = devices * levels
    share = half_waves // devices
    tiles = even_hi.shape[1] // LANES
    lane = lax.broadcasted_iota(jnp.int32, (1, LANES), 1)

    for block in range(blocks):
        mapped[:, block * LANES : (block + 1) * LANES] = map_ref[block : block + 1, :]
    for place in range(devices):
        begin = holder(place) * share
        first = mapped[:, begin : begin + share]
        row_ref[:, place * share : (place + 1) * share] = jnp.where((first & 1) == 0, first, wave_top - first)
    for block in range(blocks):
        at = slice(block * LANES, (block + 1) * LANES)
        col_ref[at, :] = jnp.broadcast_to(row_ref[:, at].astype(F32), (LANES, LANES)).T

    def start_send(k):
        to_wave, to_level = peer(k)
        mine = in_ref.at[my_wave, pl.ds(pl.multiple_of(my_level * 8, 8), 6), :]
        send(send_ref.at[to_wave * levels + to_level, pl.ds(0, 6), :], mine, sems, (to_wave, to_level)).start()

    def make_tables(group):
        block, inner = group // 4, group % 4
        at_cos = pl.multiple_of(block * 256 + inner * 32, 32)
        at_sin = pl.multiple_of(block * 256 + LANES + inner * 32, 32)
        evens = col_ref[pl.ds(pl.multiple_of(group * 32, 32), 32), :]
        for waves, table_hi, table_lo in ((evens, even_hi, even_lo), (wave_top - evens, odd_hi, odd_lo)):
            cosine, sine = turn_trig(waves * lane.astype(F32), length_f, inverse)
            turn_cos, turn_sin = turn_trig(waves * float(LANES), length_f, inverse)
            for tile in range(tiles):
                at = slice(tile * LANES, (tile + 1) * LANES)
                high, low = split(cosine)
                table_hi[pl.ds(at_cos, 32), at] = high
                table_lo[pl.ds(at_cos, 32), at] = low
                high, low = split(sine)
                table_hi[pl.ds(at_sin, 32), at] = high
                table_lo[pl.ds(at_sin, 32), at] = low
                if tile < tiles - 1:
                    cosine, sine = (
                        cosine * turn_cos - sine * turn_sin,
                        sine * turn_cos + cosine * turn_sin,
                    )

    in_ref[my_wave, pl.ds(pl.multiple_of(my_level * 8, 8), 8), :] = send_ref[here]
    start_send(1)

    @pl.loop(0, 9)
    def _(group):
        for n in range(14):
            start_send(group * 14 + n + 2)
        make_tables(group)

    @pl.loop(9, half_waves // 32)
    def _(group):
        make_tables(group)

    landed = send_ref.at[pl.ds(0, everyone - 1), pl.ds(0, 6), :]
    arrival = send(landed, landed, sems, (my_wave, my_level))
    arrival.wait_recv()

    for dev in range(devices):
        at = slice(dev * share, (dev + 1) * share)
        for j, units in enumerate(COEF_ROWS):
            for lv in range(2):
                sorted_x[dev % 4, j, pl.ds(lv, 8, stride=2), :] = in_ref[holder(dev), pl.ds(3 * lv + j, 8, stride=8), :]
            for n, (f, part, odd) in enumerate(units):
                to = slice(32 * part + 16 * f, 32 * part + 16 * f + 16)
                x_ref = odd_x if odd else even_x
                x_ref[to, at] = sorted_x[dev % 4, j, :, n * share : (n + 1) * share]

    highest = jnp.minimum(wave_top, lax.shift_right_logical(length - 1, 1))
    @pl.loop(0, blocks)
    def _(block):
        at = pl.ds(pl.multiple_of(block * LANES, LANES), LANES)
        evens = row_ref[:, at]
        for odd, x_ref, l_ref in ((False, even_x, even_l), (True, odd_x, odd_l)):
            wave = wave_top - evens if odd else evens
            kept = (wave <= highest).astype(F32)
            weight = jnp.where(wave == 0, 1.0, 2.0) * kept
            slope_weight = weight * wave.astype(F32) / (wave_top + 1.0)
            real, imag = x_ref[0:32, at], x_ref[32:64, at]
            a = jnp.concatenate([real * weight, -imag * slope_weight], axis=0)
            b = jnp.concatenate([imag * weight, real * slope_weight], axis=0)
            flip = (1 - (wave & 2)).astype(F32)
            if odd:
                on_cos = jnp.concatenate([a, flip * b], axis=0)
                on_sin = jnp.concatenate([-b, flip * a], axis=0)
            else:
                on_cos = jnp.concatenate([a, flip * a], axis=0)
                on_sin = jnp.concatenate([-b, -flip * b], axis=0)
            for offset, value in ((0, on_cos), (LANES, on_sin)):
                to = pl.ds(pl.multiple_of(block * 256 + offset, LANES), LANES)
                high, low = split(value)
                l_ref[0:128, to] = high
                l_ref[128:256, to] = low

    def grid_values(start, width):
        at = pl.ds(pl.multiple_of(start, LANES), width)
        halves = []
        for l_ref, table_hi, table_lo in ((even_l, even_hi, even_lo), (odd_l, odd_hi, odd_lo)):
            whole = dot(l_ref[...], table_hi[:, at], NN)
            halves.append(whole[:128] + whole[128:] + dot(l_ref[0:128, :], table_lo[:, at], NN))
        inside = (start + lax.broadcasted_iota(jnp.int32, (1, width), 1)) < quarter
        even, odd = (jnp.where(inside, half, 0.0) for half in halves)
        quarters = [even[:64] + odd[:64], even[64:] - odd[64:], even[:64] - odd[:64], even[64:] + odd[64:]]
        fluxes = []
        for i, values in enumerate(quarters):
            segs[i, :, at] = values[:32]
            u, v, su, sv = (values[16 * n : 16 * n + 16] for n in range(4))
            fluxes.append(jnp.concatenate([u * u, u * v, v * v, u * su, u * sv], axis=0))
        for f_ref, sign in ((even_f, 1.0), (odd_f, -1.0)):
            for n in range(2):
                value = fluxes[n] + fluxes[n + 2] if sign > 0 else fluxes[n] - fluxes[n + 2]
                high, low = split(value)
                f_ref[80 * n : 80 * n + 80, at] = high
                f_ref[160 + 80 * n : 240 + 80 * n, at] = low

    @pl.loop(0, tiles // 2)
    def _(pair):
        grid_values(pair * 256, 256)

    if tiles % 2:
        grid_values((tiles - 1) * LANES, LANES)

    scale = gauss_ref[row] * inverse

    def fourier_sums(block):
        at = pl.ds(pl.multiple_of(block * LANES, LANES), LANES)
        rows = pl.ds(pl.multiple_of(block * 256, 256), 256)
        evens = row_ref[:, at]
        for odd, f_ref, table_hi, table_lo in ((0, even_f, even_hi, even_lo), (1, odd_f, odd_hi, odd_lo)):
            whole = dot(f_ref[...], table_hi[rows, :], NT)
            total = whole[:160] + whole[160:] + dot(f_ref[0:160, :], table_lo[rows, :], NT)
            waves = wave_top - evens if odd else evens
            kept = jnp.where(waves <= highest, scale, 0.0)
            flip = (1 - (waves & 2)).astype(F32)
            first_cos, first_sin = total[:80, :LANES], total[:80, LANES:]
            second_cos, second_sin = total[80:, :LANES] * flip, total[80:, LANES:] * flip
            if odd:
                back[2, :, at] = (first_cos - second_sin) * kept
                back[3, :, at] = -(first_sin + second_cos) * kept
            else:
                back[0, :, at] = (first_cos + second_cos) * kept
                back[1, :, at] = -(first_sin + second_sin) * kept

    def send_back(dev):
        begin = dev * share
        base = lax.shift_right_logical(begin, 7)
        offset = begin & (LANES - 1)
        tiles_at = [pl.ds(pl.multiple_of((base + n) * LANES, LANES), LANES) for n in range(2)]

        def unit(x, odd, part, place):
            low, high = (back[2 * odd + part, 16 * x : 16 * x + 16, at] for at in tiles_at)
            shift = (place * share - offset + LANES) & (LANES - 1)
            return pltpu.roll(jnp.where(lane < offset, high, low), shift, 1)

        def joined(units):
            value = units[0]
            for n, other in enumerate(units[1:]):
                value = jnp.where(lane < (n + 1) * share, value, other)
            return value

        for part in range(2):
            for j, units in enumerate(FLUX_ROWS):
                packed[3 * part + j] = joined([unit(x, odd, part, n) for n, (x, odd) in enumerate(units)])
        packed[6] = joined([unit(4, 1, part, part) for part in range(2)])
        for lv in range(2):
            for part in range(2):
                for j in range(3):
                    back_ref[dev, pl.ds(6 * lv + 3 * part + j, 8, stride=16), :] = packed[
                        3 * part + j, pl.ds(lv, 8, stride=2), :
                    ]
            back_ref[dev, pl.ds(12 + lv, 8, stride=16), :] = packed[6, pl.ds(lv, 8, stride=2), :]

        to_wave = holder(dev)

        def start_block(to_level):
            block = back_ref.at[dev, pl.ds(pl.multiple_of(to_level * 16, 16), 14), :]
            send(block, out_ref.at[here, pl.ds(0, 14), :], back_sems, (to_wave, to_level)).start()

        for n in range(1, 8):
            start_block(my_level ^ n)

        @pl.when(to_wave != my_wave)
        def _():
            start_block(my_level)

    first = my_wave * blocks // devices

    @pl.loop(0, blocks)
    def _(turn):
        block = (turn + first) % blocks
        fourier_sums(block)
        low = jnp.where((turn == 0) & (block > 0), 3 * block + 1, 3 * block)
        high = jnp.where(block == blocks - 1, devices, 3 * block + 3)

        extra = jnp.where((turn == blocks - 1) & (first > 0), 1, 0)

        @pl.loop(low, high + extra)
        def _(n):
            send_back(jnp.where(n == high, 3 * first, n))

    my_place = ((my_wave - (my_wave >> 2)) & 3) * 4 + (my_wave >> 2)
    own_rows = pl.ds(pl.multiple_of(my_level * 16, 16), 16)
    own = pltpu.make_async_copy(back_ref.at[my_place, own_rows, :], out_ref.at[here], local_sems.at[1])
    own.start()

    @pl.loop(0, 4)
    def _(i):
        shift = (i * quarter) & (LANES - 1)
        before = jnp.zeros((32, LANES), F32)
        for tile in range(tiles + 1):
            at = slice(tile * LANES, (tile + 1) * LANES)
            rolled = pltpu.roll(segs[i, :, at], shift, 1) if tile < tiles else jnp.zeros((32, LANES), F32)
            turned[i, :, at] = jnp.where(lane < shift, before, rolled)
            before = rolled

    grid_copy = pltpu.make_async_copy(turned, segs_ref, local_sems.at[0])
    grid_copy.start()

    arrival.wait_send()
    landed = out_ref.at[pl.ds(0, everyone - 1), pl.ds(0, 14), :]
    arrival = send(landed, landed, back_sems, (my_wave, my_level))
    arrival.wait_recv()
    arrival.wait_send()
    own.wait()
    grid_copy.wait()


def lay_quarters(quarter, segs, acc, grid_ref):
    pad_len = grid_ref.shape[3]
    acc[...] = jnp.zeros_like(acc)
    for i in range(4):
        base = lax.shift_right_logical(i * quarter, 7)
        for tile in range(segs.shape[2] // LANES):
            at = pl.ds(pl.multiple_of((base + tile) * LANES, LANES), LANES)
            acc[:, at] += segs[i, :, tile * LANES : (tile + 1) * LANES]
    for f in range(2):
        grid_ref[0, f] = acc[16 * f : 16 * f + 16, :pad_len]


def direct_kernel(
    group, wave_hbm, band_hbm, len_hbm, in_hbm, segs_hbm, leg_hbm, spec_hbm, grid_hbm,
    wave_ref, band_ref, len_ref, in_ref, segs_ref, leg_ref, spec_ref, grid_ref, natural, turned, acc, small_sems, load_sems, store_sems, grid_sem,
):
    pack = leg_ref.shape[2]
    slots = DIRECT_STEPS * group
    wave_pos = lax.axis_index("wave")
    loads = group_copies(group, (leg_hbm,), (leg_ref,), load_sems)
    stores = group_copies(group, (spec_ref,), (spec_hbm,), store_sems)
    small = small_copies(
        (wave_hbm, band_hbm, len_hbm, in_hbm, segs_hbm), (wave_ref, band_ref, len_ref, in_ref, segs_ref), small_sems
    )
    for copy in small[:4] + loads(0):
        copy.start()
    for copy in small[:4]:
        copy.wait()
    for copy in small[4:] + loads(1):
        copy.start()

    @pl.loop(0, in_ref.shape[0], unroll=8)
    def _(i):
        natural[pl.ds(pl.multiple_of(band_ref[i] * 16, 16), 16), :] = in_ref[i]

    for lv in range(2):
        lines = [(3 * p + j, p, FLUX_ROWS[j]) for p in range(2) for j in range(3)]
        for line, part, units in [(6 * lv + n, p, u) for n, p, u in lines] + [(12 + lv, None, ())]:
            block = natural[pl.ds(line, LANES, stride=16), :].T
            placed = [(x, odd, part) for x, odd in units] or [(4, 1, 0), (4, 1, 1)]
            for n, (x, odd, p) in enumerate(placed):
                to = 4 * x + 2 * lv + p + 24 * odd
                turned[pl.ds(to, slots, stride=48), :] = block[n * slots : (n + 1) * slots]

    small[4].wait()
    row = band_ref[wave_pos * lax.axis_size("level") + lax.axis_index("level")] & 63
    lay_quarters(lax.shift_right_logical(len_ref[row], 2), segs_ref, acc, grid_ref)
    grid_copy = pltpu.make_async_copy(grid_ref, grid_hbm, grid_sem)
    grid_copy.start()

    south = lax.broadcasted_iota(jnp.int32, (1, LANES), 1) >= 64

    def both_parities(x):
        other = pltpu.roll(x, 64, 1)
        difference = x - other
        y = jnp.concatenate([x + other, jnp.where(south, -difference, difference)], axis=0)
        return jnp.concatenate(split(y), axis=0)

    def store_chunk(both, slot, boundary, begin, end):
        position = begin + lax.broadcasted_iota(jnp.int32, (1, end - begin), 1)
        rows = both.shape[0] // 2
        both = both[:rows] + both[rows:]
        if end <= pack // 2:
            chosen = jnp.where((position & 1) == 0, both[:24], both[24:])
            main, last = chosen[:16], chosen[16:20]
        else:
            in_first = position < boundary
            parity = jnp.where(in_first, position, position + boundary) & 1
            chosen = jnp.where(parity == 0, both[:40], both[40:])
            main = jnp.where(in_first, chosen[:16], chosen[16:32])
            last = jnp.where(in_first, chosen[32:36], chosen[36:40])
        for n in range(10):
            value = main[2 * n : 2 * n + 2] if n < 8 else last[2 * n - 16 : 2 * n - 14]
            spec_ref[slot, n // 2, n % 2, :, begin:end] = value

    @pl.loop(0, DIRECT_STEPS)
    def _(step):
        loads(step)[0].wait()

        @pl.when(step < DIRECT_STEPS - AHEAD)
        def _():
            loads(step + AHEAD)[0].start()

        stored = None
        for g in range(group):
            slot = step * group + g
            first_wave = wave_ref[wave_pos * slots + slot]
            boundary = (pack - 1) - first_wave
            first_at = slot * 48 + (first_wave & 1) * 24
            x = turned[pl.ds(pl.multiple_of(first_at, 8), 24), :]
            second_x = turned[pl.ds(pl.multiple_of(slot * 96 + 24 - first_at, 8), 24), :]
            last = jnp.concatenate([x[16:20], second_x[16:20]], axis=0)
            first_left = both_parities(x)
            left = both_parities(jnp.concatenate([x[:16], second_x[:16], last], axis=0))
            for begin, end in chunks_of(pack):
                at = slice(begin, end)
                right = jnp.concatenate(split(leg_ref[slot, :, at]), axis=0)
                both = dot(first_left if end <= pack // 2 else left, right, NN)
                if stored is not None:
                    store_chunk(*stored)
                stored = (both, slot, boundary, begin, end)
        store_chunk(*stored)
        stores(step)[0].start()

    for n in range(DIRECT_STEPS):
        stores(n)[0].wait()
    grid_copy.wait()


def shards(spec_in, legendre, gauss, wave_map, band_map, row_len):
    wave_devices = lax.axis_size("wave")
    devices = wave_devices * lax.axis_size("level")
    slots, _, _, _, pack = spec_in.shape
    waves = pack - 1
    lat_pairs = legendre.shape[1]
    pad_len = (20 + 4 * (waves - 1) + 127) // 128 * 128
    table_len = (pad_len // 4 + 127) // 128 * 128
    group = slots // INVERSE_STEPS

    anywhere = pl.BlockSpec(memory_space=pl.ANY)
    half = waves // 2
    table = pltpu.VMEM((waves, table_len), BF16)
    segs, returned = pl.pallas_call(
        functools.partial(main_kernel, group),
        out_shape=(
            jax.ShapeDtypeStruct((4, 32, table_len + LANES), F32),
            jax.ShapeDtypeStruct((devices, 16, LANES), F32),
        ),
        in_specs=[anywhere] * 6,
        out_specs=(anywhere, anywhere),
        scratch_shapes=[
            pltpu.SMEM((waves // 2,), jnp.int32),
            pltpu.SMEM((devices,), jnp.int32),
            pltpu.SMEM((lat_pairs,), jnp.int32),
            pltpu.SMEM((lat_pairs,), F32),
            pltpu.VMEM((slots, 2, 2, 2, pack), F32),
            pltpu.VMEM((slots, lat_pairs, pack), F32),
            pltpu.VMEM((group, 8, pack), F32),
            pltpu.VMEM((slots * 32, LANES), F32),
            pltpu.VMEM((LANES * 8, LANES), F32),
            pltpu.VMEM((LANES, 8, LANES), F32),
            pltpu.VMEM((half // LANES, LANES), jnp.int32),
            pltpu.VMEM((1, half), jnp.int32),
            pltpu.VMEM((1, half), jnp.int32),
            pltpu.VMEM((half, LANES), F32),
            pltpu.VMEM((devices, 8, LANES), F32),
            pltpu.VMEM((wave_devices, 64, LANES), F32),
            pltpu.VMEM((4, 3, 16, LANES), F32),
            pltpu.VMEM((64, half), F32),
            pltpu.VMEM((64, half), F32),
            pltpu.VMEM((256, waves), BF16),
            pltpu.VMEM((256, waves), BF16),
            table,
            table,
            table,
            table,
            pltpu.VMEM((4, 32, table_len), F32),
            pltpu.VMEM((4, 32, table_len + LANES), F32),
            pltpu.VMEM((320, table_len), BF16),
            pltpu.VMEM((320, table_len), BF16),
            pltpu.VMEM((4, 80, half + LANES), F32),
            pltpu.VMEM((7, 16, LANES), F32),
            pltpu.VMEM((wave_devices, 128, LANES), F32),
            pltpu.SemaphoreType.DMA((4,)),
            pltpu.SemaphoreType.DMA((half // LANES,)),
            pltpu.SemaphoreType.DMA((2, INVERSE_STEPS)),
            pltpu.SemaphoreType.DMA((2,)),
            pltpu.SemaphoreType.DMA((2,)),
            pltpu.SemaphoreType.DMA((2,)),
        ],
        compiler_params=pltpu.CompilerParams(
            collective_id=0, has_side_effects=True, vmem_limit_bytes=56 * MIB
        ),
        name="rows",
    )(wave_map, band_map, row_len, gauss, spec_in, legendre)

    spec_out, grid_out = pl.pallas_call(
        functools.partial(direct_kernel, slots // DIRECT_STEPS),
        out_shape=(
            jax.ShapeDtypeStruct((slots, 5, 2, 2, pack), F32),
            jax.ShapeDtypeStruct((1, 2, 16, pad_len), F32),
        ),
        in_specs=[anywhere] * 6,
        out_specs=(anywhere, anywhere),
        scratch_shapes=[
            pltpu.SMEM((waves // 2,), jnp.int32),
            pltpu.SMEM((devices,), jnp.int32),
            pltpu.SMEM((lat_pairs,), jnp.int32),
            pltpu.VMEM((devices, 16, LANES), F32),
            pltpu.VMEM((4, 32, table_len + LANES), F32),
            pltpu.VMEM((slots, lat_pairs, pack), F32),
            pltpu.VMEM((slots, 5, 2, 2, pack), F32),
            pltpu.VMEM((1, 2, 16, pad_len), F32),
            pltpu.VMEM((LANES * 16, LANES), F32),
            pltpu.VMEM((slots * 48, LANES), F32),
            pltpu.VMEM((32, 4 * table_len), F32),
            pltpu.SemaphoreType.DMA((5,)),
            pltpu.SemaphoreType.DMA((1, DIRECT_STEPS)),
            pltpu.SemaphoreType.DMA((1, DIRECT_STEPS)),
            pltpu.SemaphoreType.DMA,
        ],
        compiler_params=pltpu.CompilerParams(vmem_limit_bytes=56 * MIB),
        name="direct",
    )(wave_map, band_map, row_len, returned, segs, legendre)
    return (grid_out, spec_out)


def solution(mesh):
    in_specs = (P("wave", None, "level", None, None), P("wave", None, None), P(), P(), P(), P())
    out_specs = (P(("wave", "level"), None, None, None), P("wave", None, "level", None, None))
    return jax.shard_map(shards, mesh=mesh, in_specs=in_specs, out_specs=out_specs, check_vma=False)
```

```python
import functools
import math

import jax
import jax.numpy as jnp
from jax import lax
from jax.experimental import pallas as pl
from jax.experimental.pallas import tpu as pltpu
from jax.sharding import PartitionSpec as P

F32 = jnp.float32
BF16 = jnp.bfloat16
LANES = 128
MIB = 1 << 20
INVERSE_STEPS = 4
DIRECT_STEPS = 5
AHEAD = 2
TOGETHER = 2
SIN_TERMS = [(-1.0) ** i / math.factorial(2 * i + 1) for i in range(6)]
COS_TERMS = [(-1.0) ** i / math.factorial(2 * i) for i in range(7)]
MESH = pl.DeviceIdType.MESH
NT = (((1,), (1,)), ((), ()))
NN = (((1,), (0,)), ((), ()))
COEF_UNITS = [(f, part, odd) for f in range(2) for part in range(2) for odd in range(2)]
COEF_ROWS = [COEF_UNITS[i : i + 3] for i in range(0, 8, 3)]
FLUX_UNITS = [(x, odd) for x in range(5) for odd in range(2)]
FLUX_ROWS = [FLUX_UNITS[i : i + 3] for i in range(0, 9, 3)]


def dot(a, b, dims):
    return lax.dot_general(a, b, dims, preferred_element_type=F32)


def split(x):
    high = x.astype(BF16)
    return high, (x - high.astype(F32)).astype(BF16)


def horner(terms, x):
    total = jnp.full_like(x, terms[-1])
    for term in reversed(terms[:-1]):
        total = total * x + term
    return total


def turn_trig(steps, length, inverse):
    left = steps - jnp.floor(steps * inverse + 0.5) * length
    half = left * (inverse * math.pi)
    square = half * half
    sine = half * horner(SIN_TERMS, square)
    cosine = horner(COS_TERMS, square)
    return 1.0 - 2.0 * sine * sine, 2.0 * sine * cosine


def peer(k):
    mask = (k * 37) & 127
    return lax.axis_index("wave") ^ (mask >> 3), lax.axis_index("level") ^ (mask & 7)


def holder(place):
    return (place & 3) * 4 + ((place + (place >> 2)) & 3)


def send(source, target, sems, device):
    return pltpu.make_async_remote_copy(
        src_ref=source, dst_ref=target, send_sem=sems.at[0], recv_sem=sems.at[1], device_id=device, device_id_type=MESH
    )


def chunks_of(pack):
    ends = list(range(256, pack - 255, 256)) + [pack]
    return list(zip([0] + ends[:-1], ends))


def group_copies(group, sources, targets, sems):
    def copies(n):
        at = pl.ds(n * group, group)
        return [
            pltpu.make_async_copy(source.at[at], target.at[at], sems.at[i, n])
            for i, (source, target) in enumerate(zip(sources, targets))
        ]

    return copies


def small_copies(sources, targets, sems):
    return [
        pltpu.make_async_copy(source, target, sems.at[i])
        for i, (source, target) in enumerate(zip(sources, targets))
    ]


def inverse_step(step, group, wave_ref, spec_ref, leg_ref, flat, sums):
    slots = sums.shape[0] // 32
    pack = leg_ref.shape[2]
    wave_pos = lax.axis_index("wave")
    for g in range(group):
        for pair in range(4):
            flat[g, 2 * pair : 2 * pair + 2, :] = spec_ref[step * group + g, pair // 2, pair % 2]
    results = []
    for g in range(0, group, TOGETHER):
        both = None
        for begin, end in chunks_of(pack):
            at = slice(begin, end)
            position = begin + lax.broadcasted_iota(jnp.int32, (8, end - begin), 1)
            parts, tables = [], []
            for n in range(g, g + TOGETHER):
                first_wave = wave_ref[wave_pos * slots + step * group + n]
                boundary = (pack - 1) - first_wave
                in_first = position < boundary
                parity = jnp.where(in_first, position, position + boundary) & 1
                in_even = in_first == ((first_wave & 1) == 0)
                x = flat[n, :, at]
                high = x.astype(BF16).astype(F32)
                for part in (high, x - high):
                    signed = jnp.where(parity == 0, part, -part)
                    for kept in (in_even, jnp.logical_not(in_even)):
                        parts += [jnp.where(kept, part, 0.0), jnp.where(kept, signed, 0.0)]
                tables += split(leg_ref[step * group + n, :, at])
            left = jnp.concatenate(parts, axis=0).astype(BF16)
            product = dot(left, jnp.concatenate(tables, axis=0), NT)
            both = product if both is None else both + product
        for n in range(TOGETHER):
            own = both[64 * n : 64 * n + 64, LANES * n : LANES * n + LANES]
            own = own[:32] + own[32:]
            results.append(own + pltpu.roll(own, 64, 1))
    sums[pl.ds(pl.multiple_of(step * (32 * group), 32), 32 * group), :] = jnp.concatenate(results, axis=0)


def sort_rows(band_ref, sums, flat_rows, rows, out_ref):
    slots = sums.shape[0] // 32
    north = lax.broadcasted_iota(jnp.int32, (slots, LANES), 1) < 64

    def piece(f, lv, part, odd):
        at = 16 * odd + 4 * f + 2 * lv + part
        south_at = at + 8
        return jnp.where(
            north, sums[pl.ds(at, slots, stride=32), :], sums[pl.ds(south_at, slots, stride=32), :]
        )

    for lv in range(2):
        for j, units in enumerate(COEF_ROWS):
            pieces = [piece(f, lv, part, odd) for f, part, odd in units]
            pieces.append(jnp.zeros((LANES - len(units) * slots, LANES), F32))
            flat_rows[pl.ds(3 * lv + j, LANES, stride=8), :] = jnp.concatenate(pieces, axis=0).T

    @pl.loop(0, LANES, unroll=8)
    def _(i):
        rows[i] = flat_rows[pl.ds(pl.multiple_of(i * 8, 8), 8), :]

    @pl.loop(0, out_ref.shape[0], unroll=8)
    def _(i):
        out_ref[i] = rows[band_ref[i]]


def main_kernel(
    group, wave_hbm, band_hbm, len_hbm, gauss_hbm, spec_hbm, leg_hbm, segs_ref, out_ref,
    wave_ref, band_ref, len_ref, gauss_ref, spec_ref, leg_ref,
    flat, sums, flat_rows, rows, map_ref, mapped, row_ref, col_ref, send_ref, in_ref, sorted_x, even_x, odd_x, even_l, odd_l,
    even_hi, even_lo, odd_hi, odd_lo, segs, turned, even_f, odd_f, back, packed, back_ref,
    small_sems, map_sems, load_sems, sems, back_sems, local_sems,
):
    devices = send_ref.shape[0]
    barrier = pltpu.get_barrier_semaphore()
    copies = group_copies(group, (spec_hbm, leg_hbm), (spec_ref, leg_ref), load_sems)
    for n in range(INVERSE_STEPS):
        for copy in copies(n):
            copy.start()
    map_copies = [
        pltpu.make_async_copy(wave_hbm.at[pl.ds(n * LANES, LANES)], map_ref.at[n], map_sems.at[n])
        for n in range(map_ref.shape[0])
    ]
    small = small_copies(
        (wave_hbm, band_hbm, len_hbm, gauss_hbm), (wave_ref, band_ref, len_ref, gauss_ref), small_sems
    )
    for copy in map_copies + small:
        copy.start()

    def greet(k):
        pl.semaphore_signal(barrier, inc=1, device_id=peer(k), device_id_type=MESH)

    greet(1)

    @pl.loop(2, devices, unroll=14)
    def _(k):
        greet(k)

    for copy in small:
        copy.wait()

    @pl.loop(0, INVERSE_STEPS)
    def _(step):
        for copy in copies(step):
            copy.wait()
        inverse_step(step, group, wave_ref, spec_ref, leg_ref, flat, sums)

    sort_rows(band_ref, sums, flat_rows, rows, send_ref)
    for copy in map_copies:
        copy.wait()
    pl.semaphore_wait(barrier, devices - 1)
    row_part(
        band_ref, len_ref, gauss_ref, map_ref, mapped, row_ref, col_ref, segs_ref, out_ref, send_ref, in_ref, sorted_x,
        even_x, odd_x, even_l, odd_l, even_hi, even_lo, odd_hi, odd_lo, segs, turned, even_f, odd_f, back, packed,
        back_ref, sems, back_sems, local_sems,
    )


def row_part(
    band_ref, len_ref, gauss_ref, map_ref, mapped, row_ref, col_ref, segs_ref, out_ref, send_ref, in_ref, sorted_x,
    even_x, odd_x, even_l, odd_l, even_hi, even_lo, odd_hi, odd_lo, segs, turned, even_f, odd_f, back, packed,
    back_ref, sems, back_sems, local_sems,
):
    my_wave, my_level = lax.axis_index("wave"), lax.axis_index("level")
    levels = lax.axis_size("level")
    here = my_wave * levels + my_level
    row = band_ref[here] & 63
    length = len_ref[row]
    quarter = lax.shift_right_logical(length, 2)
    wave_top = 2 * row_ref.shape[1] - 1
    length_f = jnp.full((1, LANES), length.astype(F32))
    inverse = 1.0 / length_f
    half_waves = row_ref.shape[1]
    blocks = half_waves // LANES
    devices = in_ref.shape[0]
    everyone = devices * levels
    share = half_waves // devices
    tiles = even_hi.shape[1] // LANES
    lane = lax.broadcasted_iota(jnp.int32, (1, LANES), 1)

    for block in range(blocks):
        mapped[:, block * LANES : (block + 1) * LANES] = map_ref[block : block + 1, :]
    for place in range(devices):
        begin = holder(place) * share
        first = mapped[:, begin : begin + share]
        row_ref[:, place * share : (place + 1) * share] = jnp.where((first & 1) == 0, first, wave_top - first)
    for block in range(blocks):
        at = slice(block * LANES, (block + 1) * LANES)
        col_ref[at, :] = jnp.broadcast_to(row_ref[:, at].astype(F32), (LANES, LANES)).T

    def start_send(k):
        to_wave, to_level = peer(k)
        mine = in_ref.at[my_wave, pl.ds(pl.multiple_of(my_level * 8, 8), 6), :]
        send(send_ref.at[to_wave * levels + to_level, pl.ds(0, 6), :], mine, sems, (to_wave, to_level)).start()

    def make_tables(group):
        block, inner = group // 4, group % 4
        at_cos = pl.multiple_of(block * 256 + inner * 32, 32)
        at_sin = pl.multiple_of(block * 256 + LANES + inner * 32, 32)
        evens = col_ref[pl.ds(pl.multiple_of(group * 32, 32), 32), :]
        for waves, table_hi, table_lo in ((evens, even_hi, even_lo), (wave_top - evens, odd_hi, odd_lo)):
            cosine, sine = turn_trig(waves * lane.astype(F32), length_f, inverse)
            turn_cos, turn_sin = turn_trig(waves * float(LANES), length_f, inverse)
            for tile in range(tiles):
                at = slice(tile * LANES, (tile + 1) * LANES)
                high, low = split(cosine)
                table_hi[pl.ds(at_cos, 32), at] = high
                table_lo[pl.ds(at_cos, 32), at] = low
                high, low = split(sine)
                table_hi[pl.ds(at_sin, 32), at] = high
                table_lo[pl.ds(at_sin, 32), at] = low
                if tile < tiles - 1:
                    cosine, sine = (
                        cosine * turn_cos - sine * turn_sin,
                        sine * turn_cos + cosine * turn_sin,
                    )

    in_ref[my_wave, pl.ds(pl.multiple_of(my_level * 8, 8), 8), :] = send_ref[here]
    start_send(1)

    @pl.loop(0, 9)
    def _(group):
        for n in range(14):
            start_send(group * 14 + n + 2)
        make_tables(group)

    @pl.loop(9, half_waves // 32)
    def _(group):
        make_tables(group)

    landed = send_ref.at[pl.ds(0, everyone - 1), pl.ds(0, 6), :]
    arrival = send(landed, landed, sems, (my_wave, my_level))
    arrival.wait_recv()

    for dev in range(devices):
        at = slice(dev * share, (dev + 1) * share)
        for j, units in enumerate(COEF_ROWS):
            for lv in range(2):
                sorted_x[dev % 4, j, pl.ds(lv, 8, stride=2), :] = in_ref[holder(dev), pl.ds(3 * lv + j, 8, stride=8), :]
            for n, (f, part, odd) in enumerate(units):
                to = slice(32 * part + 16 * f, 32 * part + 16 * f + 16)
                x_ref = odd_x if odd else even_x
                x_ref[to, at] = sorted_x[dev % 4, j, :, n * share : (n + 1) * share]

    highest = jnp.minimum(wave_top, lax.shift_right_logical(length - 1, 1))
    @pl.loop(0, blocks)
    def _(block):
        at = pl.ds(pl.multiple_of(block * LANES, LANES), LANES)
        evens = row_ref[:, at]
        for odd, x_ref, l_ref in ((False, even_x, even_l), (True, odd_x, odd_l)):
            wave = wave_top - evens if odd else evens
            kept = (wave <= highest).astype(F32)
            weight = jnp.where(wave == 0, 1.0, 2.0) * kept
            slope_weight = weight * wave.astype(F32) / (wave_top + 1.0)
            real, imag = x_ref[0:32, at], x_ref[32:64, at]
            a = jnp.concatenate([real * weight, -imag * slope_weight], axis=0)
            b = jnp.concatenate([imag * weight, real * slope_weight], axis=0)
            flip = (1 - (wave & 2)).astype(F32)
            if odd:
                on_cos = jnp.concatenate([a, flip * b], axis=0)
                on_sin = jnp.concatenate([-b, flip * a], axis=0)
            else:
                on_cos = jnp.concatenate([a, flip * a], axis=0)
                on_sin = jnp.concatenate([-b, -flip * b], axis=0)
            for offset, value in ((0, on_cos), (LANES, on_sin)):
                to = pl.ds(pl.multiple_of(block * 256 + offset, LANES), LANES)
                high, low = split(value)
                l_ref[0:128, to] = high
                l_ref[128:256, to] = low

    def grid_values(start, width):
        at = pl.ds(pl.multiple_of(start, LANES), width)
        halves = []
        for l_ref, table_hi, table_lo in ((even_l, even_hi, even_lo), (odd_l, odd_hi, odd_lo)):
            whole = dot(l_ref[...], table_hi[:, at], NN)
            halves.append(whole[:128] + whole[128:] + dot(l_ref[0:128, :], table_lo[:, at], NN))
        inside = (start + lax.broadcasted_iota(jnp.int32, (1, width), 1)) < quarter
        even, odd = (jnp.where(inside, half, 0.0) for half in halves)
        quarters = [even[:64] + odd[:64], even[64:] - odd[64:], even[:64] - odd[:64], even[64:] + odd[64:]]
        fluxes = []
        for i, values in enumerate(quarters):
            segs[i, :, at] = values[:32]
            u, v, su, sv = (values[16 * n : 16 * n + 16] for n in range(4))
            fluxes.append(jnp.concatenate([u * u, u * v, v * v, u * su, u * sv], axis=0))
        for f_ref, sign in ((even_f, 1.0), (odd_f, -1.0)):
            for n in range(2):
                value = fluxes[n] + fluxes[n + 2] if sign > 0 else fluxes[n] - fluxes[n + 2]
                high, low = split(value)
                f_ref[80 * n : 80 * n + 80, at] = high
                f_ref[160 + 80 * n : 240 + 80 * n, at] = low

    @pl.loop(0, tiles // 2)
    def _(pair):
        grid_values(pair * 256, 256)

    if tiles % 2:
        grid_values((tiles - 1) * LANES, LANES)

    scale = gauss_ref[row] * inverse

    def fourier_sums(block):
        at = pl.ds(pl.multiple_of(block * LANES, LANES), LANES)
        rows = pl.ds(pl.multiple_of(block * 256, 256), 256)
        evens = row_ref[:, at]
        for odd, f_ref, table_hi, table_lo in ((0, even_f, even_hi, even_lo), (1, odd_f, odd_hi, odd_lo)):
            whole = dot(f_ref[...], table_hi[rows, :], NT)
            total = whole[:160] + whole[160:] + dot(f_ref[0:160, :], table_lo[rows, :], NT)
            waves = wave_top - evens if odd else evens
            kept = jnp.where(waves <= highest, scale, 0.0)
            flip = (1 - (waves & 2)).astype(F32)
            first_cos, first_sin = total[:80, :LANES], total[:80, LANES:]
            second_cos, second_sin = total[80:, :LANES] * flip, total[80:, LANES:] * flip
            if odd:
                back[2, :, at] = (first_cos - second_sin) * kept
                back[3, :, at] = -(first_sin + second_cos) * kept
            else:
                back[0, :, at] = (first_cos + second_cos) * kept
                back[1, :, at] = -(first_sin + second_sin) * kept

    def send_back(dev):
        begin = dev * share
        base = lax.shift_right_logical(begin, 7)
        offset = begin & (LANES - 1)
        tiles_at = [pl.ds(pl.multiple_of((base + n) * LANES, LANES), LANES) for n in range(2)]

        def unit(x, odd, part, place):
            low, high = (back[2 * odd + part, 16 * x : 16 * x + 16, at] for at in tiles_at)
            shift = (place * share - offset + LANES) & (LANES - 1)
            return pltpu.roll(jnp.where(lane < offset, high, low), shift, 1)

        def joined(units):
            value = units[0]
            for n, other in enumerate(units[1:]):
                value = jnp.where(lane < (n + 1) * share, value, other)
            return value

        for part in range(2):
            for j, units in enumerate(FLUX_ROWS):
                packed[3 * part + j] = joined([unit(x, odd, part, n) for n, (x, odd) in enumerate(units)])
        packed[6] = joined([unit(4, 1, part, part) for part in range(2)])
        for lv in range(2):
            for part in range(2):
                for j in range(3):
                    back_ref[dev, pl.ds(6 * lv + 3 * part + j, 8, stride=16), :] = packed[
                        3 * part + j, pl.ds(lv, 8, stride=2), :
                    ]
            back_ref[dev, pl.ds(12 + lv, 8, stride=16), :] = packed[6, pl.ds(lv, 8, stride=2), :]

        to_wave = holder(dev)

        def start_block(to_level):
            block = back_ref.at[dev, pl.ds(pl.multiple_of(to_level * 16, 16), 14), :]
            send(block, out_ref.at[here, pl.ds(0, 14), :], back_sems, (to_wave, to_level)).start()

        for n in range(1, 8):
            start_block(my_level ^ n)

        @pl.when(to_wave != my_wave)
        def _():
            start_block(my_level)

    first = my_wave * blocks // devices

    @pl.loop(0, blocks)
    def _(turn):
        block = (turn + first) % blocks
        fourier_sums(block)
        low = jnp.where((turn == 0) & (block > 0), 3 * block + 1, 3 * block)
        high = jnp.where(block == blocks - 1, devices, 3 * block + 3)

        extra = jnp.where((turn == blocks - 1) & (first > 0), 1, 0)

        @pl.loop(low, high + extra)
        def _(n):
            send_back(jnp.where(n == high, 3 * first, n))

    my_place = ((my_wave - (my_wave >> 2)) & 3) * 4 + (my_wave >> 2)
    own_rows = pl.ds(pl.multiple_of(my_level * 16, 16), 16)
    own = pltpu.make_async_copy(back_ref.at[my_place, own_rows, :], out_ref.at[here], local_sems.at[1])
    own.start()

    @pl.loop(0, 4)
    def _(i):
        shift = (i * quarter) & (LANES - 1)
        before = jnp.zeros((32, LANES), F32)
        for tile in range(tiles + 1):
            at = slice(tile * LANES, (tile + 1) * LANES)
            rolled = pltpu.roll(segs[i, :, at], shift, 1) if tile < tiles else jnp.zeros((32, LANES), F32)
            turned[i, :, at] = jnp.where(lane < shift, before, rolled)
            before = rolled

    grid_copy = pltpu.make_async_copy(turned, segs_ref, local_sems.at[0])
    grid_copy.start()

    arrival.wait_send()
    landed = out_ref.at[pl.ds(0, everyone - 1), pl.ds(0, 14), :]
    arrival = send(landed, landed, back_sems, (my_wave, my_level))
    arrival.wait_recv()
    arrival.wait_send()
    own.wait()
    grid_copy.wait()


def lay_quarters(quarter, segs, acc, grid_ref):
    pad_len = grid_ref.shape[3]
    acc[...] = jnp.zeros_like(acc)
    for i in range(4):
        base = lax.shift_right_logical(i * quarter, 7)
        for tile in range(segs.shape[2] // LANES):
            at = pl.ds(pl.multiple_of((base + tile) * LANES, LANES), LANES)
            acc[:, at] += segs[i, :, tile * LANES : (tile + 1) * LANES]
    for f in range(2):
        grid_ref[0, f] = acc[16 * f : 16 * f + 16, :pad_len]


def direct_kernel(
    group, wave_hbm, band_hbm, len_hbm, in_hbm, segs_hbm, leg_hbm, spec_hbm, grid_hbm,
    wave_ref, band_ref, len_ref, in_ref, segs_ref, leg_ref, spec_ref, grid_ref, natural, turned, acc, small_sems, load_sems, store_sems, grid_sem,
):
    pack = leg_ref.shape[2]
    slots = DIRECT_STEPS * group
    wave_pos = lax.axis_index("wave")
    loads = group_copies(group, (leg_hbm,), (leg_ref,), load_sems)
    stores = group_copies(group, (spec_ref,), (spec_hbm,), store_sems)
    small = small_copies(
        (wave_hbm, band_hbm, len_hbm, in_hbm, segs_hbm), (wave_ref, band_ref, len_ref, in_ref, segs_ref), small_sems
    )
    for copy in small[:4] + loads(0):
        copy.start()
    for copy in small[:4]:
        copy.wait()
    for copy in small[4:] + loads(1):
        copy.start()

    @pl.loop(0, in_ref.shape[0], unroll=8)
    def _(i):
        natural[pl.ds(pl.multiple_of(band_ref[i] * 16, 16), 16), :] = in_ref[i]

    for lv in range(2):
        lines = [(3 * p + j, p, FLUX_ROWS[j]) for p in range(2) for j in range(3)]
        for line, part, units in [(6 * lv + n, p, u) for n, p, u in lines] + [(12 + lv, None, ())]:
            block = natural[pl.ds(line, LANES, stride=16), :].T
            placed = [(x, odd, part) for x, odd in units] or [(4, 1, 0), (4, 1, 1)]
            for n, (x, odd, p) in enumerate(placed):
                to = 4 * x + 2 * lv + p + 24 * odd
                turned[pl.ds(to, slots, stride=48), :] = block[n * slots : (n + 1) * slots]

    small[4].wait()
    row = band_ref[wave_pos * lax.axis_size("level") + lax.axis_index("level")] & 63
    lay_quarters(lax.shift_right_logical(len_ref[row], 2), segs_ref, acc, grid_ref)
    grid_copy = pltpu.make_async_copy(grid_ref, grid_hbm, grid_sem)
    grid_copy.start()

    south = lax.broadcasted_iota(jnp.int32, (1, LANES), 1) >= 64

    def both_parities(x):
        other = pltpu.roll(x, 64, 1)
        difference = x - other
        y = jnp.concatenate([x + other, jnp.where(south, -difference, difference)], axis=0)
        return jnp.concatenate(split(y), axis=0)

    def store_chunk(both, slot, boundary, begin, end):
        position = begin + lax.broadcasted_iota(jnp.int32, (1, end - begin), 1)
        rows = both.shape[0] // 2
        both = both[:rows] + both[rows:]
        if end <= pack // 2:
            chosen = jnp.where((position & 1) == 0, both[:24], both[24:])
            main, last = chosen[:16], chosen[16:20]
        else:
            in_first = position < boundary
            parity = jnp.where(in_first, position, position + boundary) & 1
            chosen = jnp.where(parity == 0, both[:40], both[40:])
            main = jnp.where(in_first, chosen[:16], chosen[16:32])
            last = jnp.where(in_first, chosen[32:36], chosen[36:40])
        for n in range(10):
            value = main[2 * n : 2 * n + 2] if n < 8 else last[2 * n - 16 : 2 * n - 14]
            spec_ref[slot, n // 2, n % 2, :, begin:end] = value

    @pl.loop(0, DIRECT_STEPS)
    def _(step):
        loads(step)[0].wait()

        @pl.when(step < DIRECT_STEPS - AHEAD)
        def _():
            loads(step + AHEAD)[0].start()

        stored = None
        for g in range(group):
            slot = step * group + g
            first_wave = wave_ref[wave_pos * slots + slot]
            boundary = (pack - 1) - first_wave
            first_at = slot * 48 + (first_wave & 1) * 24
            x = turned[pl.ds(pl.multiple_of(first_at, 8), 24), :]
            second_x = turned[pl.ds(pl.multiple_of(slot * 96 + 24 - first_at, 8), 24), :]
            last = jnp.concatenate([x[16:20], second_x[16:20]], axis=0)
            first_left = both_parities(x)
            left = both_parities(jnp.concatenate([x[:16], second_x[:16], last], axis=0))
            for begin, end in chunks_of(pack):
                at = slice(begin, end)
                right = jnp.concatenate(split(leg_ref[slot, :, at]), axis=0)
                both = dot(first_left if end <= pack // 2 else left, right, NN)
                if stored is not None:
                    store_chunk(*stored)
                stored = (both, slot, boundary, begin, end)
        store_chunk(*stored)
        stores(step)[0].start()

    for n in range(DIRECT_STEPS):
        stores(n)[0].wait()
    grid_copy.wait()


def shards(spec_in, legendre, gauss, wave_map, band_map, row_len):
    wave_devices = lax.axis_size("wave")
    devices = wave_devices * lax.axis_size("level")
    slots, _, _, _, pack = spec_in.shape
    waves = pack - 1
    lat_pairs = legendre.shape[1]
    pad_len = (20 + 4 * (waves - 1) + 127) // 128 * 128
    table_len = (pad_len // 4 + 127) // 128 * 128
    group = slots // INVERSE_STEPS

    anywhere = pl.BlockSpec(memory_space=pl.ANY)
    half = waves // 2
    table = pltpu.VMEM((waves, table_len), BF16)
    segs, returned = pl.pallas_call(
        functools.partial(main_kernel, group),
        out_shape=(
            jax.ShapeDtypeStruct((4, 32, table_len + LANES), F32),
            jax.ShapeDtypeStruct((devices, 16, LANES), F32),
        ),
        in_specs=[anywhere] * 6,
        out_specs=(anywhere, anywhere),
        scratch_shapes=[
            pltpu.SMEM((waves // 2,), jnp.int32),
            pltpu.SMEM((devices,), jnp.int32),
            pltpu.SMEM((lat_pairs,), jnp.int32),
            pltpu.SMEM((lat_pairs,), F32),
            pltpu.VMEM((slots, 2, 2, 2, pack), F32),
            pltpu.VMEM((slots, lat_pairs, pack), F32),
            pltpu.VMEM((group, 8, pack), F32),
            pltpu.VMEM((slots * 32, LANES), F32),
            pltpu.VMEM((LANES * 8, LANES), F32),
            pltpu.VMEM((LANES, 8, LANES), F32),
            pltpu.VMEM((half // LANES, LANES), jnp.int32),
            pltpu.VMEM((1, half), jnp.int32),
            pltpu.VMEM((1, half), jnp.int32),
            pltpu.VMEM((half, LANES), F32),
            pltpu.VMEM((devices, 8, LANES), F32),
            pltpu.VMEM((wave_devices, 64, LANES), F32),
            pltpu.VMEM((4, 3, 16, LANES), F32),
            pltpu.VMEM((64, half), F32),
            pltpu.VMEM((64, half), F32),
            pltpu.VMEM((256, waves), BF16),
            pltpu.VMEM((256, waves), BF16),
            table,
            table,
            table,
            table,
            pltpu.VMEM((4, 32, table_len), F32),
            pltpu.VMEM((4, 32, table_len + LANES), F32),
            pltpu.VMEM((320, table_len), BF16),
            pltpu.VMEM((320, table_len), BF16),
            pltpu.VMEM((4, 80, half + LANES), F32),
            pltpu.VMEM((7, 16, LANES), F32),
            pltpu.VMEM((wave_devices, 128, LANES), F32),
            pltpu.SemaphoreType.DMA((4,)),
            pltpu.SemaphoreType.DMA((half // LANES,)),
            pltpu.SemaphoreType.DMA((2, INVERSE_STEPS)),
            pltpu.SemaphoreType.DMA((2,)),
            pltpu.SemaphoreType.DMA((2,)),
            pltpu.SemaphoreType.DMA((2,)),
        ],
        compiler_params=pltpu.CompilerParams(
            collective_id=0, has_side_effects=True, vmem_limit_bytes=56 * MIB
        ),
        name="rows",
    )(wave_map, band_map, row_len, gauss, spec_in, legendre)

    spec_out, grid_out = pl.pallas_call(
        functools.partial(direct_kernel, slots // DIRECT_STEPS),
        out_shape=(
            jax.ShapeDtypeStruct((slots, 5, 2, 2, pack), F32),
            jax.ShapeDtypeStruct((1, 2, 16, pad_len), F32),
        ),
        in_specs=[anywhere] * 6,
        out_specs=(anywhere, anywhere),
        scratch_shapes=[
            pltpu.SMEM((waves // 2,), jnp.int32),
            pltpu.SMEM((devices,), jnp.int32),
            pltpu.SMEM((lat_pairs,), jnp.int32),
            pltpu.VMEM((devices, 16, LANES), F32),
            pltpu.VMEM((4, 32, table_len + LANES), F32),
            pltpu.VMEM((slots, lat_pairs, pack), F32),
            pltpu.VMEM((slots, 5, 2, 2, pack), F32),
            pltpu.VMEM((1, 2, 16, pad_len), F32),
            pltpu.VMEM((LANES * 16, LANES), F32),
            pltpu.VMEM((slots * 48, LANES), F32),
            pltpu.VMEM((32, 4 * table_len), F32),
            pltpu.SemaphoreType.DMA((5,)),
            pltpu.SemaphoreType.DMA((1, DIRECT_STEPS)),
            pltpu.SemaphoreType.DMA((1, DIRECT_STEPS)),
            pltpu.SemaphoreType.DMA,
        ],
        compiler_params=pltpu.CompilerParams(vmem_limit_bytes=50 * MIB),
        name="direct",
    )(wave_map, band_map, row_len, returned, segs, legendre)
    return (grid_out, spec_out)


def solution(mesh):
    in_specs = (P("wave", None, "level", None, None), P("wave", None, None), P(), P(), P(), P())
    out_specs = (P(("wave", "level"), None, None, None), P("wave", None, "level", None, None))
    return jax.shard_map(shards, mesh=mesh, in_specs=in_specs, out_specs=out_specs, check_vma=False)
```
